32 devices in a mesh: groups: 2 (over y), dp: 4 (over z), expert: 2 (over x), pair: 2 (over core).
Axes of the slice: x: 2, y: 2, z: 4, core: 2. Of those that a mesh axis runs over, the one named last changes fastest.
Arguments:
- states: bfloat16 [2, 256, 6144], P(None, ('groups', 'dp'), ('expert', 'pair')), parts along dimension 1, may hold values from -6 to 6
- base_gate_up_projection: bfloat16 [2, 256, 2, 2, 16384], P(None, ('groups', 'dp'), None, None, ('expert', 'pair')), parts along dimension 1, may hold values from -6 to 6
- route_panel_index: int32 [2, 256, 2], P(None, ('groups', 'dp')), parts along dimension 1, may hold values from 0 to 63, as said below
- adapter_down_maps: bfloat16 [64, 2, 16, 6144], P('dp', None, None, ('expert', 'pair')), may hold values from -0.078125 to 0.078125
- adapter_up_maps: bfloat16 [64, 2, 16, 16384], P('dp', None, None, ('expert', 'pair')), may hold values from -0.75 to 0.75
- magnitude_over_norm: bfloat16 [64, 2, 16384], P('dp', None, ('expert', 'pair')), may hold values from 0.5 to 2
Outputs:
- hidden_units: bfloat16 [2, 256, 2, 16384], P(None, ('groups', 'dp'), None, ('expert', 'pair')), parts along dimension 1
The draws below stay inside these ranges and needn't reach their ends.
There are 2 independent parts, one for each index of `groups`. The reference program is written for one: setup_inputs(seed, part) draws one part's arguments, and reference() takes and returns one part's arrays. A program takes and returns all parts, laid end to end along the dimension named above; an argument that names none is the same for every part. Nothing has to cross between parts.
Inputs may be any that keep to these rules, and one draw needn't show every extreme that they name: `route_panel_index`: A panel u is held by owner u // 16. In each step the 64 routes of the rows of one index of dp name panels of any one owner at most 40 times, and some owner exactly 40 times.
All inputs are finite; a program needn't handle non-finite values.
Results may differ from the reference program's by a relative error of at most 0.0048.
Values may be sent and summed in bfloat16 or wider, within the bound.
No kernel may reach another device: no remote copies, remote signals or barrier semaphores. Data moves between devices by JAX's collectives and lax.ppermute only.
A program may use at most 128 MiB of HBM per device.

```python
import math
import jax
import jax.numpy as jnp
from jax import lax

MODEL_WIDTH = 6144
EXPERT_HIDDEN = 16384
ADAPTER_RANK = 16
STEPS = 2
ROW_DEV = 32
UNIT_DEV = 16
ROWS = 128
PANEL_COUNT = 64
CAP = 40


def draw_route_panel_index(key, part):
    key = jax.random.fold_in(key, 11)
    owners = PANEL_COUNT // UNIT_DEV
    routes = 2 * ROW_DEV
    pool_size = owners * CAP
    pool = jnp.arange(pool_size, dtype=jnp.int32) // CAP

    def one_block(block_key):
        first, second, third = jax.random.split(block_key, 3)
        shuffled = pool[jax.random.permutation(first, pool_size)]
        hottest = shuffled[0]
        order_key = jnp.where(shuffled == hottest, 0, 1) * pool_size + jnp.arange(pool_size, dtype=jnp.int32)
        chosen = shuffled[jnp.argsort(order_key)][:routes]
        chosen = chosen[jax.random.permutation(second, routes)]
        within = jax.random.randint(third, (routes,), 0, UNIT_DEV)
        return chosen * UNIT_DEV + within
    block_keys = jax.random.split(key, STEPS * owners)
    units = jax.vmap(one_block)(block_keys)
    return units.reshape(STEPS, owners * ROW_DEV, 2).astype(jnp.int32)


def level_of(own_key, extent, cuts, least, largest):
    def one(dim, parts):
        steps = jax.random.uniform(jax.random.fold_in(jax.random.fold_in(own_key, 6), dim), (parts,), jnp.float32, least / len(cuts), largest / len(cuts))
        return jnp.repeat(jnp.exp(steps), extent[dim] // parts).reshape((-1,) + (1,) * (len(extent) - dim - 1))

    level = one(*cuts[0])
    for cut in cuts[1:]:
        level = level * one(*cut)
    return level


def noise(stream_key, extent, scale, reach, cuts=(), held_as=jnp.bfloat16):
    drawn = jax.random.normal(stream_key, extent, jnp.float32) * scale
    if len(cuts) > 0:
        drawn = level_of(stream_key, extent, cuts, -0.22, 0.18) * drawn
    return jnp.clip(drawn, min=-reach, max=reach).astype(held_as)


def setup_inputs(seed: int = 0, part: int = 0) -> dict:
    arg_keys = jax.random.split(jax.random.key(seed), 7)
    own_keys = jax.random.split(jax.random.fold_in(arg_keys[6], part), 7)
    states = noise(own_keys[0], (STEPS, ROWS, MODEL_WIDTH), 1.0, 6.0, ((1, 4), (2, 4)))
    base_gate_up_projection = noise(own_keys[1], (STEPS, ROWS, 2, 2, EXPERT_HIDDEN), 1.0, 6.0, ((1, 4), (4, 4)))
    route_panel_index = draw_route_panel_index(jax.random.fold_in(jax.random.fold_in(arg_keys[6], part), 71), part)
    adapter_down_maps = noise(arg_keys[3], (PANEL_COUNT, 2, ADAPTER_RANK, MODEL_WIDTH), MODEL_WIDTH ** -0.5, 0.078125, ((0, 4), (3, 4)))
    adapter_up_maps = noise(arg_keys[4], (PANEL_COUNT, 2, ADAPTER_RANK, EXPERT_HIDDEN), (4 * ADAPTER_RANK) ** -0.5, 0.75, ((0, 4), (3, 4)))
    magnitude_over_norm = jnp.clip(jnp.exp(math.log(2.0) - 1.3862944 * jax.random.uniform(arg_keys[5], (PANEL_COUNT, 2, EXPERT_HIDDEN), jnp.float32) ** level_of(arg_keys[5], (PANEL_COUNT, 2, EXPERT_HIDDEN), ((0, 4), (2, 4)), -0.2, 0.2)), 0.5, 2.0).astype(jnp.bfloat16)
    return dict(states=states, base_gate_up_projection=base_gate_up_projection, route_panel_index=route_panel_index, adapter_down_maps=adapter_down_maps, adapter_up_maps=adapter_up_maps, magnitude_over_norm=magnitude_over_norm)


def reference(states, base_gate_up_projection, route_panel_index, adapter_down_maps, adapter_up_maps, magnitude_over_norm):
    total = STEPS * ROWS * 2
    width = 2 * ROW_DEV
    blocks = total // width
    units = route_panel_index.reshape(blocks, width).astype(jnp.int32)
    repeated = jnp.repeat(states.reshape(STEPS * ROWS, MODEL_WIDTH), 2, axis=0).reshape(blocks, width, MODEL_WIDTH)
    base_rows = base_gate_up_projection.reshape(blocks, width, 2, EXPERT_HIDDEN)

    def one_block(packed):
        store_panel_index, features, base_block = packed
        gathered_down_maps = adapter_down_maps[store_panel_index].astype(jnp.float32)
        low = jnp.einsum('bd,bprd->bpr', features.astype(jnp.float32), gathered_down_maps).astype(jnp.bfloat16)
        gathered_up_maps = adapter_up_maps[store_panel_index].astype(jnp.float32)
        delta = jnp.einsum('bpr,bprf->bpf', low.astype(jnp.float32), gathered_up_maps).astype(jnp.bfloat16)
        scales = magnitude_over_norm[store_panel_index].astype(jnp.float32)
        adapted = scales * (base_block.astype(jnp.float32) + delta.astype(jnp.float32))
        return (jax.nn.silu(adapted[:, 0]) * adapted[:, 1]).astype(jnp.bfloat16)

    result = lax.map(one_block, (units, repeated, base_rows))
    return result.reshape(STEPS, ROWS, 2, EXPERT_HIDDEN)
```

```python
import functools

import jax
import jax.numpy as jnp
from jax import lax
from jax.experimental import pallas as pl
from jax.experimental.pallas import tpu as pltpu
from jax.sharding import PartitionSpec as P

LANES = 128
ROW_TILE = 16
VMEM_LIMIT = 48 * 1024 * 1024


def nt_dot(a, b):
    return lax.dot_general(a, b, (((1,), (1,)), ((), ())), preferred_element_type=jnp.float32)


def earlier_in_step(steps, rows):
    routes = 2 * steps * rows
    first = lax.broadcasted_iota(jnp.int32, (routes, routes), 0)
    second = lax.broadcasted_iota(jnp.int32, (routes, routes), 1)
    same = (first // rows) % steps == (second // rows) % steps
    return jnp.where(same & (first < second), 1.0, 0.0).astype(jnp.bfloat16)


def low_kernel(count, steps, rows, cap, slots, me_ref, down_ref, *refs):
    state_refs, (part_ref, info_ref) = refs[:count], refs[count:]
    panels, _, rank, width = down_ref.shape
    routes = 2 * steps * rows
    me = me_ref[0].astype(jnp.float32)
    down = down_ref[...].reshape(panels * 2 * rank, width)
    pick = jnp.where(
        lax.broadcasted_iota(jnp.int32, (8, LANES), 0) == lax.broadcasted_iota(jnp.int32, (8, LANES), 1), 1.0, 0.0
    ).astype(jnp.bfloat16)
    before = earlier_in_step(steps, rows)
    lane = lax.broadcasted_iota(jnp.int32, (1, routes), 1)
    step_of = ((lane // rows) % steps).astype(jnp.float32)
    panel_of = (lax.broadcasted_iota(jnp.int32, (panels * 2 * rank, routes), 0) // (2 * rank)).astype(jnp.float32)
    for s in range(count):
        one = state_refs[s][...]
        both = jnp.concatenate([one, one], axis=0)
        numbers = nt_dot(pick, both[:, width:])
        owner = jnp.where(lane < routes // 2, numbers[0:1], numbers[1:2])
        within = jnp.where(lane < routes // 2, numbers[2:3], numbers[3:4])
        mine = owner == me
        rank_of = jnp.dot(
            jnp.broadcast_to(jnp.where(mine, 1.0, 0.0), (8, routes)).astype(jnp.bfloat16),
            before,
            preferred_element_type=jnp.float32,
        )[0:1]
        slot = jnp.where(mine, step_of * cap + rank_of, -1.0)
        held = jnp.where(mine, within, -1.0)
        cols = pl.ds(s * routes, routes)
        info_ref[:, cols] = jnp.concatenate([slot, held, jnp.zeros((6, routes), jnp.float32)], axis=0)
        low = nt_dot(down, both[:, :width])
        low = jnp.where(panel_of == held, low, 0.0)
        part_ref[:, cols] = jnp.sum(low.reshape(panels, 2 * rank, routes), axis=0)


def delta_kernel(count, slots, info_ref, own_ref, core_ref, far_ref, diag_ref, up_ref, *refs):
    out_refs, (lhs_ref,) = refs[:count], refs[count:]
    panels, rank, tile = up_ref.shape
    routes = info_ref.shape[1] // count

    @pl.when((pl.program_id(0) == 0) & (pl.program_id(1) == 0))
    def _():
        low = (own_ref[...] + core_ref[...]) + (far_ref[...] + diag_ref[...])
        low = low.astype(jnp.bfloat16).astype(jnp.float32)
        panel_of = (lax.broadcasted_iota(jnp.int32, (panels * rank, routes), 0) // rank).astype(jnp.float32)
        slot_of = lax.broadcasted_iota(jnp.int32, (slots, routes), 0).astype(jnp.float32)
        for s in range(count):
            cols = slice(s * routes, (s + 1) * routes)
            slot, held = info_ref[0:1, cols], info_ref[1:2, cols]
            place = jnp.where(slot_of == slot, 1.0, 0.0).astype(jnp.bfloat16)
            for p in range(2):
                wide = jnp.concatenate([low[p * rank : (p + 1) * rank, cols]] * panels, axis=0)
                wide = jnp.where(panel_of == held, wide, 0.0).astype(jnp.bfloat16)
                lhs_ref[p, s * slots : (s + 1) * slots, :] = nt_dot(place, wide).astype(jnp.bfloat16)

    p = pl.program_id(0)
    up = up_ref[...].reshape(panels * rank, tile)
    delta = jnp.dot(lhs_ref[p], up, preferred_element_type=jnp.float32).astype(jnp.bfloat16)
    for s in range(count):
        out_refs[s][...] = delta[s * slots : (s + 1) * slots]


def gate_kernel(count, group_ref, pick_ref, panel_ref, base_ref, mine_ref, other_ref, *refs):
    blocks, out_ref = refs[: 2 * count], refs[2 * count]
    slots = blocks[0].shape[0]
    group = group_ref[0]
    adapted = []
    for p in range(2):
        delta = None
        for s in range(count):
            part = jnp.dot(
                pick_ref[:, s * slots : (s + 1) * slots],
                blocks[p * count + s][...],
                preferred_element_type=jnp.float32,
            )
            delta = part if delta is None else delta + part
        scales = jnp.where(group == p, mine_ref[...], other_ref[...])
        scale = jnp.dot(panel_ref[...], scales, preferred_element_type=jnp.float32)
        adapted.append(scale * (base_ref[p].astype(jnp.float32) + delta))
    gate, value = adapted
    out_ref[...] = (gate / (1.0 + jnp.exp(-gate)) * value).astype(out_ref.dtype)


def on_device(states, base, route_panels, down, up, magnitude):
    count = lax.axis_size("dp")
    me = lax.axis_index("dp")
    group = lax.axis_index("groups")
    steps, rows, width = states.shape
    hidden = base.shape[-1]
    panels, _, rank, _ = down.shape
    routes = 2 * steps * rows
    cap = max(2, (5 * rows + count - 1) // count)
    slots = -(-steps * cap // ROW_TILE) * ROW_TILE
    bf16, f32, i32 = jnp.bfloat16, jnp.float32, jnp.int32

    def turn(x, shift):
        return lax.ppermute(x, "dp", [(i, (i + shift) % count) for i in range(count)])

    pairs = route_panels.reshape(steps * rows, 2)
    numbers = jnp.concatenate([pairs // panels, pairs % panels], axis=1).astype(bf16)
    sent = jnp.concatenate(
        [states.reshape(steps * rows, width), jnp.pad(numbers, ((0, 0), (0, LANES - 4)))], axis=1
    )
    seen = [sent] + [turn(sent, s) for s in range(1, count)]

    half = lax.dynamic_index_in_dim(magnitude, group, axis=1, keepdims=False)
    mine = jnp.concatenate([half] + [turn(half, s) for s in range(1, count)], axis=0)
    other = lax.ppermute(mine, "groups", [(0, 1), (1, 0)])

    vmem = pl.BlockSpec(memory_space=pltpu.VMEM)
    smem = pl.BlockSpec(memory_space=pltpu.SMEM)
    params = pltpu.CompilerParams(vmem_limit_bytes=VMEM_LIMIT)
    part, info = pl.pallas_call(
        functools.partial(low_kernel, count, steps, rows, cap, slots),
        out_shape=(
            jax.ShapeDtypeStruct((2 * rank, count * routes), f32),
            jax.ShapeDtypeStruct((8, count * routes), f32),
        ),
        in_specs=[smem] + [vmem] * (1 + count),
        out_specs=(vmem, vmem),
        compiler_params=params,
    )(me.reshape(1).astype(i32), down, *seen)

    expert, pair = lax.axis_size("expert"), lax.axis_size("pair")
    lows = [part]
    if (expert, pair) == (2, 2):
        for mask in (1, 2, 3):
            lows.append(lax.ppermute(part, ("expert", "pair"), [(i, i ^ mask) for i in range(4)]))
    else:
        total = lax.psum(part, ("expert", "pair"))
        lows = [total] + [jnp.zeros_like(total)] * 3

    tile = min(1024, hidden)
    col_tiles = hidden // tile
    whole = lambda shape: pl.BlockSpec(shape, lambda p, n: (0,) * len(shape))
    deltas = pl.pallas_call(
        functools.partial(delta_kernel, count, slots),
        out_shape=[jax.ShapeDtypeStruct((slots, 2 * hidden), bf16)] * count,
        grid=(2, col_tiles),
        in_specs=[whole(info.shape)]
        + [whole(part.shape)] * 4
        + [pl.BlockSpec((panels, None, rank, tile), lambda p, n: (0, p, 0, n))],
        out_specs=[pl.BlockSpec((slots, tile), lambda p, n: (0, p * col_tiles + n))] * count,
        scratch_shapes=[pltpu.VMEM((2, count * slots, panels * rank), bf16)],
        compiler_params=params,
    )(info, *lows, up)
    got = [deltas[0]] + [turn(deltas[s], count - s) for s in range(1, count)]

    ordered = route_panels.transpose(2, 0, 1).reshape(2, steps, rows)
    owner, within = ordered // panels, ordered % panels
    by_step = owner.transpose(1, 0, 2).reshape(steps, 2 * rows)
    earlier = jnp.tril(jnp.ones((2 * rows, 2 * rows), jnp.bool_), -1)
    rank_of = jnp.sum((by_step[:, :, None] == by_step[:, None, :]) & earlier[None], axis=2, dtype=i32)
    slot = rank_of + jnp.arange(steps, dtype=i32)[:, None] * cap
    slot = slot.reshape(steps, 2, rows).transpose(1, 0, 2).reshape(routes)
    owner, within = owner.reshape(routes), within.reshape(routes)
    ahead = (owner - me) % count
    behind = (me - owner) % count
    pick = (jnp.arange(count * slots, dtype=i32)[None, :] == (ahead * slots + slot)[:, None]).astype(bf16)
    panel = (jnp.arange(count * panels, dtype=i32)[None, :] == (behind * panels + within)[:, None]).astype(bf16)
    base_rows = base.transpose(3, 2, 0, 1, 4).reshape(2, routes, hidden)

    tile = min(512, hidden)
    col_tiles = hidden // tile
    whole = lambda shape: pl.BlockSpec(shape, lambda n: (0,) * len(shape))
    col = lambda depth, p: pl.BlockSpec((depth, tile), lambda n, p=p: (0, p * col_tiles + n))
    out = pl.pallas_call(
        functools.partial(gate_kernel, count),
        out_shape=jax.ShapeDtypeStruct((routes, hidden), bf16),
        grid=(col_tiles,),
        in_specs=[smem, whole(pick.shape), whole(panel.shape)]
        + [pl.BlockSpec((2, routes, tile), lambda n: (0, 0, n))]
        + [col(count * panels, 0)] * 2
        + [col(slots, 0)] * count
        + [col(slots, 1)] * count,
        out_specs=col(routes, 0),
        compiler_params=params,
    )(group.reshape(1).astype(i32), pick, panel, base_rows, mine, other, *got, *got)
    return out.reshape(2, steps, rows, hidden).transpose(1, 2, 0, 3)


def solution(mesh):
    return jax.shard_map(
        on_device,
        mesh=mesh,
        in_specs=(
            P(None, ("groups", "dp"), ("expert", "pair")),
            P(None, ("groups", "dp"), None, None, ("expert", "pair")),
            P(None, ("groups", "dp"), None),
            P("dp", None, None, ("expert", "pair")),
            P("dp", None, None, ("expert", "pair")),
            P("dp", None, ("expert", "pair")),
        ),
        out_specs=P(None, ("groups", "dp"), None, ("expert", "pair")),
        check_vma=False,
    )
```

```python
import functools

import jax
import jax.numpy as jnp
from jax import lax
from jax.experimental import pallas as pl
from jax.experimental.pallas import tpu as pltpu
from jax.sharding import PartitionSpec as P

LANES = 128
ROW_TILE = 16
VMEM_LIMIT = 48 * 1024 * 1024


def nt_dot(a, b):
    return lax.dot_general(a, b, (((1,), (1,)), ((), ())), preferred_element_type=jnp.float32)


def earlier_in_step(steps, rows):
    routes = 2 * steps * rows
    first = lax.broadcasted_iota(jnp.int32, (routes, routes), 0)
    second = lax.broadcasted_iota(jnp.int32, (routes, routes), 1)
    same = (first // rows) % steps == (second // rows) % steps
    return jnp.where(same & (first < second), 1.0, 0.0).astype(jnp.bfloat16)


def low_kernel(count, steps, rows, cap, slots, me_ref, down_ref, *refs):
    state_refs, (part_ref, info_ref) = refs[:count], refs[count:]
    panels, _, rank, width = down_ref.shape
    routes = 2 * steps * rows
    me = me_ref[0].astype(jnp.float32)
    down = down_ref[...].reshape(panels * 2 * rank, width)
    pick = jnp.where(
        lax.broadcasted_iota(jnp.int32, (8, LANES), 0) == lax.broadcasted_iota(jnp.int32, (8, LANES), 1), 1.0, 0.0
    ).astype(jnp.bfloat16)
    before = earlier_in_step(steps, rows)
    lane = lax.broadcasted_iota(jnp.int32, (1, routes), 1)
    step_of = ((lane // rows) % steps).astype(jnp.float32)
    panel_of = (lax.broadcasted_iota(jnp.int32, (panels * 2 * rank, routes), 0) // (2 * rank)).astype(jnp.float32)
    for s in range(count):
        one = state_refs[s][...]
        both = jnp.concatenate([one, one], axis=0)
        numbers = nt_dot(pick, both[:, width:])
        owner = jnp.where(lane < routes // 2, numbers[0:1], numbers[1:2])
        within = jnp.where(lane < routes // 2, numbers[2:3], numbers[3:4])
        mine = owner == me
        rank_of = jnp.dot(
            jnp.broadcast_to(jnp.where(mine, 1.0, 0.0), (8, routes)).astype(jnp.bfloat16),
            before,
            preferred_element_type=jnp.float32,
        )[0:1]
        slot = jnp.where(mine, step_of * cap + rank_of, -1.0)
        held = jnp.where(mine, within, -1.0)
        cols = pl.ds(s * routes, routes)
        info_ref[:, cols] = jnp.concatenate([slot, held, jnp.zeros((6, routes), jnp.float32)], axis=0)
        low = nt_dot(down, both[:, :width])
        low = jnp.where(panel_of == held, low, 0.0)
        part_ref[:, cols] = jnp.sum(low.reshape(panels, 2 * rank, routes), axis=0)


def delta_kernel(count, slots, info_ref, own_ref, core_ref, far_ref, diag_ref, up_ref, *refs):
    out_refs, (lhs_ref,) = refs[:count], refs[count:]
    panels, rank, tile = up_ref.shape
    routes = info_ref.shape[1] // count

    @pl.when((pl.program_id(0) == 0) & (pl.program_id(1) == 0))
    def _():
        low = (own_ref[...] + core_ref[...]) + (far_ref[...] + diag_ref[...])
        low = low.astype(jnp.bfloat16).astype(jnp.float32)
        panel_of = (lax.broadcasted_iota(jnp.int32, (panels * rank, routes), 0) // rank).astype(jnp.float32)
        slot_of = lax.broadcasted_iota(jnp.int32, (slots, routes), 0).astype(jnp.float32)
        for s in range(count):
            cols = slice(s * routes, (s + 1) * routes)
            slot, held = info_ref[0:1, cols], info_ref[1:2, cols]
            place = jnp.where(slot_of == slot, 1.0, 0.0).astype(jnp.bfloat16)
            for p in range(2):
                wide = jnp.concatenate([low[p * rank : (p + 1) * rank, cols]] * panels, axis=0)
                wide = jnp.where(panel_of == held, wide, 0.0).astype(jnp.bfloat16)
                lhs_ref[p, s * slots : (s + 1) * slots, :] = nt_dot(place, wide).astype(jnp.bfloat16)

    p = pl.program_id(0)
    up = up_ref[...].reshape(panels * rank, tile)
    delta = jnp.dot(lhs_ref[p], up, preferred_element_type=jnp.float32).astype(jnp.bfloat16)
    for s in range(count):
        out_refs[s][...] = delta[s * slots : (s + 1) * slots]


def gate_kernel(count, group_ref, pick_ref, panel_ref, base_ref, mine_ref, other_ref, *refs):
    blocks, out_ref = refs[: 2 * count], refs[2 * count]
    slots = blocks[0].shape[0]
    group = group_ref[0]
    adapted = []
    for p in range(2):
        delta = None
        for s in range(count):
            part = jnp.dot(
                pick_ref[:, s * slots : (s + 1) * slots],
                blocks[p * count + s][...],
                preferred_element_type=jnp.float32,
            )
            delta = part if delta is None else delta + part
        scales = jnp.where(group == p, mine_ref[...], other_ref[...])
        scale = jnp.dot(panel_ref[...], scales, preferred_element_type=jnp.float32)
        adapted.append(scale * (base_ref[p].astype(jnp.float32) + delta))
    gate, value = adapted
    out_ref[...] = (gate / (1.0 + jnp.exp(-gate)) * value).astype(out_ref.dtype)


CHUNK = 32
LAG = 2
LEAST_CHUNKS = 5


def right_layout(n):
    gap = float(LAG * CHUNK)
    zero = jnp.zeros_like(n[0][0])
    place = {}

    def put(link, j, d, first, split=None, second=None):
        place[link, j, d] = (first, split, second)

    put(0, 0, 3, zero)
    put(0, 0, 2, n[0][3])
    put(0, 0, 1, n[0][3] + n[0][2])
    end = n[0][3] + n[0][2] + n[0][1]
    early = jnp.maximum(jnp.minimum(n[1][2], gap - n[1][3]), 0.0)
    far = jnp.maximum(n[1][3], gap)
    late = far + n[0][3] + n[1][2] - early
    put(1, 1, 3, zero)
    put(1, 0, 3, far)
    put(1, 1, 2, n[1][3], early, far + n[0][3] - early)
    put(1, 0, 2, late)
    end = jnp.maximum(end, late + n[0][2])
    one = jnp.maximum(n[2][3], gap)
    two = jnp.maximum(one + n[1][3], far + gap)
    put(2, 2, 3, zero)
    put(2, 1, 3, one)
    put(2, 0, 3, two)
    return place, jnp.maximum(end, two + n[0][3])


def relay_low_kernel(steps, rows, me_ref, down_ref, *refs):
    count = 4
    state_refs, (part_ref, info_ref) = refs[:count], refs[count:]
    panels, _, rank, width = down_ref.shape
    routes = 2 * steps * rows
    me = me_ref[0]
    down = down_ref[...].reshape(panels * 2 * rank, width)
    pick = jnp.where(
        lax.broadcasted_iota(jnp.int32, (8, LANES), 0) == lax.broadcasted_iota(jnp.int32, (8, LANES), 1), 1.0, 0.0
    ).astype(jnp.bfloat16)
    before = jnp.where(
        lax.broadcasted_iota(jnp.int32, (routes, routes), 0) < lax.broadcasted_iota(jnp.int32, (routes, routes), 1),
        1.0,
        0.0,
    ).astype(jnp.bfloat16)
    lane = lax.broadcasted_iota(jnp.int32, (1, routes), 1)
    owners = lax.broadcasted_iota(jnp.int32, (8, routes), 0).astype(jnp.float32)
    panel_of = (lax.broadcasted_iota(jnp.int32, (panels * 2 * rank, routes), 0) // (2 * rank)).astype(jnp.float32)
    owner, within, order, tally = [], [], [], []
    info_ref[...] = jnp.full(info_ref.shape, -1.0, jnp.float32)
    for s in range(count):
        one = state_refs[s][...]
        both = jnp.concatenate([one, one], axis=0)
        numbers = nt_dot(pick, both[:, width:])
        owner.append(jnp.where(lane < routes // 2, numbers[0:1], numbers[1:2]))
        within.append(jnp.where(lane < routes // 2, numbers[2:3], numbers[3:4]))
        hits = jnp.where(owners == owner[s], 1.0, 0.0)
        ahead = jnp.dot(hits.astype(jnp.bfloat16), before, preferred_element_type=jnp.float32)
        order.append(jnp.sum(ahead * hits, axis=0, keepdims=True))
        tally.append(jnp.sum(hits, axis=1, keepdims=True))
        cols = slice(s * routes, (s + 1) * routes)
        held = jnp.where(owner[s] == me.astype(jnp.float32), within[s], -1.0)
        info_ref[0:1, cols] = held
        low = nt_dot(down, both[:, :width])
        low = jnp.where(panel_of == held, low, 0.0)
        part_ref[:, cols] = jnp.sum(low.reshape(panels, 2 * rank, routes), axis=0)
    info_ref[9:10, 0:routes] = owner[0]
    info_ref[10:11, 0:routes] = within[0]

    def position(place, link, d, s, turned, owners_from, owners_to):
        found = jnp.full((1, routes), -1.0, jnp.float32)
        for j in range(owners_from, owners_to):
            first, split, second = place[link, j, d]
            at = first + order[s]
            if split is not None:
                at = jnp.where(order[s] < split, at, second + order[s])
            found = jnp.where(owner[s] == float(3 - j if turned else j), at, found)
        return found

    for case in range(count):

        @pl.when(me == case)
        def _():
            longest = None
            for turned in (False, True):
                node = 3 - case if turned else case
                n = [[None] * count for _ in range(count)]
                for j in range(count):
                    for d in range(count):
                        s = (case - d) % count
                        if turned:
                            n[3 - j][3 - d] = tally[s][j : j + 1]
                        else:
                            n[j][d] = tally[s][j : j + 1]
                place, end = right_layout(n)
                longest = end if longest is None else jnp.maximum(longest, end)
                row = 4 if turned else 1
                for d in range(node + 1, count):
                    s = (case - (3 - d if turned else d)) % count
                    cols = slice(s * routes, (s + 1) * routes)
                    info_ref[row : row + 1, cols] = position(place, node, d, s, turned, node, node + 1)
                    if node > 0:
                        info_ref[row + 1 : row + 2, cols] = position(place, node, d, s, turned, 0, node)
                        info_ref[row + 2 : row + 3, cols] = position(place, node - 1, d, s, turned, 0, node)
                if node > 0:
                    arrive = 8 if turned else 7
                    info_ref[arrive : arrive + 1, 0:routes] = position(place, node - 1, node, 0, turned, 0, node)
            info_ref[11:12, 0:routes] = jnp.broadcast_to(longest, (1, routes))


def relay_rows_kernel(limit, info_ref, own_ref, core_ref, far_ref, diag_ref, up_ref, *refs):
    chunk_refs, (lhs_ref, forward_ref, local_ref) = refs[:4], refs[4:]
    panels, rank, tile = up_ref.shape
    routes = info_ref.shape[1] // 4

    @pl.when((pl.program_id(0) == 0) & (pl.program_id(1) == 0))
    def _():
        low = (own_ref[...] + core_ref[...]) + (far_ref[...] + diag_ref[...])
        low = low.astype(jnp.bfloat16).astype(jnp.float32)
        everything = info_ref.shape[1]
        panel_of = (lax.broadcasted_iota(jnp.int32, (panels * rank, everything), 0) // rank).astype(jnp.float32)
        slot_of = lax.broadcasted_iota(jnp.int32, (limit, everything), 0).astype(jnp.float32)
        held = info_ref[0:1, :]

        def place(row):
            return jnp.where(slot_of == info_ref[row : row + 1, :], 1.0, 0.0).astype(jnp.bfloat16)

        own = [place(1), place(4)]
        same = lax.broadcasted_iota(jnp.int32, (routes, routes), 0) == lax.broadcasted_iota(
            jnp.int32, (routes, routes), 1
        )
        same = jnp.where(same, 1.0, 0.0).astype(jnp.bfloat16)
        for p in range(2):
            wide = jnp.concatenate([low[p * rank : (p + 1) * rank]] * panels, axis=0)
            wide = jnp.where(panel_of == held, wide, 0.0).astype(jnp.bfloat16)
            for way in range(2):
                lhs_ref[p, way] = nt_dot(own[way], wide).astype(jnp.bfloat16)
            local_ref[p] = nt_dot(same, wide[:, :routes]).astype(jnp.bfloat16)
        for way in range(2):
            forward_ref[way] = nt_dot(place(3 * way + 2), place(3 * way + 3)).astype(jnp.bfloat16)

    p = pl.program_id(0)
    up = up_ref[...].reshape(panels * rank, tile)
    lhs = jnp.concatenate([lhs_ref[p, 0, : 2 * CHUNK, :], lhs_ref[p, 1, : 2 * CHUNK, :]], axis=0)
    delta = jnp.dot(lhs, up, preferred_element_type=jnp.float32).astype(jnp.bfloat16)
    for i in range(4):
        chunk_refs[i][...] = delta[i * CHUNK : (i + 1) * CHUNK]


def relay_chunk_kernel(known, lhs_ref, forward_ref, up_ref, *refs):
    came, (right_ref, left_ref) = refs[: 2 * known], refs[2 * known :]
    panels, rank, tile = up_ref.shape
    p = pl.program_id(0)
    up = up_ref[...].reshape(panels * rank, tile)
    lhs = jnp.concatenate([lhs_ref[p, 0], lhs_ref[p, 1]], axis=0)
    delta = jnp.dot(lhs, up, preferred_element_type=jnp.float32)
    for way, out_ref in ((0, right_ref), (1, left_ref)):
        rows = jnp.concatenate([came[way * known + i][...] for i in range(known)], axis=0)
        passed = jnp.dot(forward_ref[way][:, : known * CHUNK], rows, preferred_element_type=jnp.float32)
        out_ref[...] = (delta[way * CHUNK : (way + 1) * CHUNK] + passed).astype(out_ref.dtype)


def relay_gate_kernel(chunks, group_ref, pick_ref, panel_ref, local_ref, base_ref, mine_ref, other_ref, *refs):
    up_refs, came, out_ref = refs[:2], refs[2:-1], refs[-1]
    panels, rank, tile = up_refs[0].shape
    group = group_ref[0]
    adapted = []
    for p in range(2):
        up = up_refs[p][...].reshape(panels * rank, tile)
        delta = jnp.dot(local_ref[p], up, preferred_element_type=jnp.float32).astype(jnp.bfloat16).astype(jnp.float32)
        rows = jnp.concatenate([came[p * 2 * chunks + i][...] for i in range(2 * chunks)], axis=0)
        delta = delta + jnp.dot(pick_ref[...], rows, preferred_element_type=jnp.float32)
        scales = jnp.where(group == p, mine_ref[...], other_ref[...])
        scale = jnp.dot(panel_ref[...], scales, preferred_element_type=jnp.float32)
        adapted.append(scale * (base_ref[p].astype(jnp.float32) + delta))
    gate, value = adapted
    out_ref[...] = (gate / (1.0 + jnp.exp(-gate)) * value).astype(out_ref.dtype)


def relayed(seen, mine, other, base, down, up):
    count = 4
    me, group = lax.axis_index("dp"), lax.axis_index("groups")
    steps, rows, hidden = base.shape[0], base.shape[1], base.shape[-1]
    panels, _, rank, _ = down.shape
    routes = 2 * steps * rows
    cap = max(2, (5 * rows + count - 1) // count)
    gap = LAG * CHUNK
    limit = max(
        3 * steps * cap,
        2 * routes,
        gap + 2 * steps * cap,
        gap + routes,
        2 * gap + steps * cap,
    )
    limit = -(-limit // CHUNK) * CHUNK
    most = limit // CHUNK
    bf16, f32, i32 = jnp.bfloat16, jnp.float32, jnp.int32
    vmem = pl.BlockSpec(memory_space=pltpu.VMEM)
    smem = pl.BlockSpec(memory_space=pltpu.SMEM)
    params = pltpu.CompilerParams(vmem_limit_bytes=VMEM_LIMIT)

    part, info = pl.pallas_call(
        functools.partial(relay_low_kernel, steps, rows),
        out_shape=(
            jax.ShapeDtypeStruct((2 * rank, count * routes), f32),
            jax.ShapeDtypeStruct((16, count * routes), f32),
        ),
        in_specs=[smem] + [vmem] * (1 + count),
        out_specs=(vmem, vmem),
        compiler_params=params,
    )(me.reshape(1).astype(i32), down, *seen)
    lows = [part]
    for mask in (1, 2, 3):
        lows.append(lax.ppermute(part, ("expert", "pair"), [(i, i ^ mask) for i in range(4)]))
    longest = info[8:16, 0:LANES]
    longest = jnp.maximum(longest, lax.ppermute(longest, "groups", [(0, 1), (1, 0)]))[3, 0]

    tile = min(1024, hidden)
    col_tiles = hidden // tile
    whole = lambda shape: pl.BlockSpec(shape, lambda p, n: (0,) * len(shape))
    up_block = pl.BlockSpec((panels, None, rank, tile), lambda p, n: (0, p, 0, n))
    row_block = pl.BlockSpec((CHUNK, tile), lambda p, n: (0, p * col_tiles + n))
    chunk_shape = jax.ShapeDtypeStruct((CHUNK, 2 * hidden), bf16)
    shapes = ((2, 2, limit, panels * rank), (2, limit, limit), (2, routes, panels * rank))
    first = pl.pallas_call(
        functools.partial(relay_rows_kernel, limit),
        out_shape=[chunk_shape] * 4 + [jax.ShapeDtypeStruct(shape, bf16) for shape in shapes],
        grid=(2, col_tiles),
        in_specs=[whole(info.shape)] + [whole(part.shape)] * 4 + [up_block],
        out_specs=[row_block] * 4 + [whole(shape) for shape in shapes],
        compiler_params=params,
    )(info, *lows, up)
    right_first, left_first, (lhs, forward, local) = first[0:2], first[2:4], first[4:]

    owner, within = info[9, :routes].astype(i32), info[10, :routes].astype(i32)
    behind = (me - owner) % count
    panel = (jnp.arange(count * panels, dtype=i32)[None, :] == (behind * panels + within)[:, None]).astype(bf16)
    base_rows = base.transpose(3, 2, 0, 1, 4).reshape(2, routes, hidden)
    slot = jnp.arange(limit, dtype=f32)[None, :]
    from_left = (slot == info[7, :routes, None]).astype(bf16)
    from_right = (slot == info[8, :routes, None]).astype(bf16)
    here = group.reshape(1).astype(i32)

    def flow(chunks, operands):
        right_first, left_first, lhs, forward, local, up, panel, base_rows, from_left, from_right, mine, other = operands
        got_right, got_left = [], []
        for k in range(chunks):
            if k < LAG:
                right, left = right_first[k], left_first[k]
            else:
                known = k + 1 - LAG
                right, left = pl.pallas_call(
                    functools.partial(relay_chunk_kernel, known),
                    out_shape=[chunk_shape] * 2,
                    grid=(2, col_tiles),
                    in_specs=[
                        pl.BlockSpec((2, 2, CHUNK, panels * rank), lambda p, n, k=k: (0, 0, k, 0)),
                        pl.BlockSpec((2, CHUNK, limit), lambda p, n, k=k: (0, k, 0)),
                        up_block,
                    ]
                    + [row_block] * (2 * known),
                    out_specs=[row_block] * 2,
                    compiler_params=params,
                )(lhs, forward, up, *got_right[:known], *got_left[:known])
            got_right.append(lax.ppermute(right, "dp", [(i, i + 1) for i in range(count - 1)]))
            got_left.append(lax.ppermute(left, "dp", [(i + 1, i) for i in range(count - 1)]))
        pick = jnp.concatenate([from_left[:, : chunks * CHUNK], from_right[:, : chunks * CHUNK]], axis=1)
        tile = min(512, hidden)
        tiles = hidden // tile
        whole = lambda shape: pl.BlockSpec(shape, lambda n: (0,) * len(shape))
        col = lambda depth, p: pl.BlockSpec((depth, tile), lambda n, p=p: (0, p * tiles + n))
        up_of = lambda p: pl.BlockSpec((panels, None, rank, tile), lambda n, p=p: (0, p, 0, n))
        came = got_right + got_left
        return pl.pallas_call(
            functools.partial(relay_gate_kernel, chunks),
            out_shape=jax.ShapeDtypeStruct((routes, hidden), bf16),
            grid=(tiles,),
            in_specs=[smem, whole(pick.shape), whole(panel.shape), whole(local.shape)]
            + [pl.BlockSpec((2, routes, tile), lambda n: (0, 0, n))]
            + [col(count * panels, 0)] * 2
            + [up_of(0), up_of(1)]
            + [col(CHUNK, 0)] * (2 * chunks)
            + [col(CHUNK, 1)] * (2 * chunks),
            out_specs=col(routes, 0),
            compiler_params=params,
        )(here, pick, panel, local, base_rows, mine, other, up, up, *came, *came)

    operands = (right_first, left_first, lhs, forward, local, up, panel, base_rows, from_left, from_right, mine, other)
    branch = jnp.clip((longest.astype(i32) + CHUNK - 1) // CHUNK - LEAST_CHUNKS, 0, most - LEAST_CHUNKS)
    out = lax.switch(branch, [functools.partial(flow, c) for c in range(LEAST_CHUNKS, most + 1)], operands)
    return out.reshape(2, steps, rows, hidden).transpose(1, 2, 0, 3)


def on_device(states, base, route_panels, down, up, magnitude):
    count = lax.axis_size("dp")
    me = lax.axis_index("dp")
    group = lax.axis_index("groups")
    steps, rows, width = states.shape
    hidden = base.shape[-1]
    panels, _, rank, _ = down.shape
    routes = 2 * steps * rows
    cap = max(2, (5 * rows + count - 1) // count)
    slots = -(-steps * cap // ROW_TILE) * ROW_TILE
    bf16, f32, i32 = jnp.bfloat16, jnp.float32, jnp.int32

    def turn(x, shift):
        return lax.ppermute(x, "dp", [(i, (i + shift) % count) for i in range(count)])

    pairs = route_panels.reshape(steps * rows, 2)
    numbers = jnp.concatenate([pairs // panels, pairs % panels], axis=1).astype(bf16)
    sent = jnp.concatenate(
        [states.reshape(steps * rows, width), jnp.pad(numbers, ((0, 0), (0, LANES - 4)))], axis=1
    )
    seen = [sent] + [turn(sent, s) for s in range(1, count)]

    half = lax.dynamic_index_in_dim(magnitude, group, axis=1, keepdims=False)
    mine = jnp.concatenate([half] + [turn(half, s) for s in range(1, count)], axis=0)
    other = lax.ppermute(mine, "groups", [(0, 1), (1, 0)])

    if (count, lax.axis_size("expert"), lax.axis_size("pair")) == (4, 2, 2):
        return relayed(seen, mine, other, base, down, up)

    vmem = pl.BlockSpec(memory_space=pltpu.VMEM)
    smem = pl.BlockSpec(memory_space=pltpu.SMEM)
    params = pltpu.CompilerParams(vmem_limit_bytes=VMEM_LIMIT)
    part, info = pl.pallas_call(
        functools.partial(low_kernel, count, steps, rows, cap, slots),
        out_shape=(
            jax.ShapeDtypeStruct((2 * rank, count * routes), f32),
            jax.ShapeDtypeStruct((8, count * routes), f32),
        ),
        in_specs=[smem] + [vmem] * (1 + count),
        out_specs=(vmem, vmem),
        compiler_params=params,
    )(me.reshape(1).astype(i32), down, *seen)

    expert, pair = lax.axis_size("expert"), lax.axis_size("pair")
    lows = [part]
    if (expert, pair) == (2, 2):
        for mask in (1, 2, 3):
            lows.append(lax.ppermute(part, ("expert", "pair"), [(i, i ^ mask) for i in range(4)]))
    else:
        total = lax.psum(part, ("expert", "pair"))
        lows = [total] + [jnp.zeros_like(total)] * 3

    tile = min(1024, hidden)
    col_tiles = hidden // tile
    whole = lambda shape: pl.BlockSpec(shape, lambda p, n: (0,) * len(shape))
    deltas = pl.pallas_call(
        functools.partial(delta_kernel, count, slots),
        out_shape=[jax.ShapeDtypeStruct((slots, 2 * hidden), bf16)] * count,
        grid=(2, col_tiles),
        in_specs=[whole(info.shape)]
        + [whole(part.shape)] * 4
        + [pl.BlockSpec((panels, None, rank, tile), lambda p, n: (0, p, 0, n))],
        out_specs=[pl.BlockSpec((slots, tile), lambda p, n: (0, p * col_tiles + n))] * count,
        scratch_shapes=[pltpu.VMEM((2, count * slots, panels * rank), bf16)],
        compiler_params=params,
    )(info, *lows, up)
    got = [deltas[0]] + [turn(deltas[s], count - s) for s in range(1, count)]

    ordered = route_panels.transpose(2, 0, 1).reshape(2, steps, rows)
    owner, within = ordered // panels, ordered % panels
    by_step = owner.transpose(1, 0, 2).reshape(steps, 2 * rows)
    earlier = jnp.tril(jnp.ones((2 * rows, 2 * rows), jnp.bool_), -1)
    rank_of = jnp.sum((by_step[:, :, None] == by_step[:, None, :]) & earlier[None], axis=2, dtype=i32)
    slot = rank_of + jnp.arange(steps, dtype=i32)[:, None] * cap
    slot = slot.reshape(steps, 2, rows).transpose(1, 0, 2).reshape(routes)
    owner, within = owner.reshape(routes), within.reshape(routes)
    ahead = (owner - me) % count
    behind = (me - owner) % count
    pick = (jnp.arange(count * slots, dtype=i32)[None, :] == (ahead * slots + slot)[:, None]).astype(bf16)
    panel = (jnp.arange(count * panels, dtype=i32)[None, :] == (behind * panels + within)[:, None]).astype(bf16)
    base_rows = base.transpose(3, 2, 0, 1, 4).reshape(2, routes, hidden)

    tile = min(512, hidden)
    col_tiles = hidden // tile
    whole = lambda shape: pl.BlockSpec(shape, lambda n: (0,) * len(shape))
    col = lambda depth, p: pl.BlockSpec((depth, tile), lambda n, p=p: (0, p * col_tiles + n))
    out = pl.pallas_call(
        functools.partial(gate_kernel, count),
        out_shape=jax.ShapeDtypeStruct((routes, hidden), bf16),
        grid=(col_tiles,),
        in_specs=[smem, whole(pick.shape), whole(panel.shape)]
        + [pl.BlockSpec((2, routes, tile), lambda n: (0, 0, n))]
        + [col(count * panels, 0)] * 2
        + [col(slots, 0)] * count
        + [col(slots, 1)] * count,
        out_specs=col(routes, 0),
        compiler_params=params,
    )(group.reshape(1).astype(i32), pick, panel, base_rows, mine, other, *got, *got)
    return out.reshape(2, steps, rows, hidden).transpose(1, 2, 0, 3)


def solution(mesh):
    return jax.shard_map(
        on_device,
        mesh=mesh,
        in_specs=(
            P(None, ("groups", "dp"), ("expert", "pair")),
            P(None, ("groups", "dp"), None, None, ("expert", "pair")),
            P(None, ("groups", "dp"), None),
            P("dp", None, None, ("expert", "pair")),
            P("dp", None, None, ("expert", "pair")),
            P("dp", None, ("expert", "pair")),
        ),
        out_specs=P(None, ("groups", "dp"), None, ("expert", "pair")),
        check_vma=False,
    )
```

```python
import functools

import jax
import jax.numpy as jnp
from jax import lax
from jax.experimental import pallas as pl
from jax.experimental.pallas import tpu as pltpu
from jax.sharding import PartitionSpec as P

LANES = 128
ROW_TILE = 16
VMEM_LIMIT = 20 * 1024 * 1024


def nt_dot(a, b):
    return lax.dot_general(a, b, (((1,), (1,)), ((), ())), preferred_element_type=jnp.float32)


def earlier_in_step(steps, rows):
    routes = 2 * steps * rows
    first = lax.broadcasted_iota(jnp.int32, (routes, routes), 0)
    second = lax.broadcasted_iota(jnp.int32, (routes, routes), 1)
    same = (first // rows) % steps == (second // rows) % steps
    return jnp.where(same & (first < second), 1.0, 0.0).astype(jnp.bfloat16)


def low_kernel(count, steps, rows, cap, slots, me_ref, down_ref, *refs):
    state_refs, (part_ref, info_ref) = refs[:count], refs[count:]
    panels, _, rank, width = down_ref.shape
    routes = 2 * steps * rows
    me = me_ref[0].astype(jnp.float32)
    down = down_ref[...].reshape(panels * 2 * rank, width)
    pick = jnp.where(
        lax.broadcasted_iota(jnp.int32, (8, LANES), 0) == lax.broadcasted_iota(jnp.int32, (8, LANES), 1), 1.0, 0.0
    ).astype(jnp.bfloat16)
    before = earlier_in_step(steps, rows)
    lane = lax.broadcasted_iota(jnp.int32, (1, routes), 1)
    step_of = ((lane // rows) % steps).astype(jnp.float32)
    panel_of = (lax.broadcasted_iota(jnp.int32, (panels * 2 * rank, routes), 0) // (2 * rank)).astype(jnp.float32)
    for s in range(count):
        one = state_refs[s][...]
        both = jnp.concatenate([one, one], axis=0)
        numbers = nt_dot(pick, both[:, width:])
        owner = jnp.where(lane < routes // 2, numbers[0:1], numbers[1:2])
        within = jnp.where(lane < routes // 2, numbers[2:3], numbers[3:4])
        mine = owner == me
        rank_of = jnp.dot(
            jnp.broadcast_to(jnp.where(mine, 1.0, 0.0), (8, routes)).astype(jnp.bfloat16),
            before,
            preferred_element_type=jnp.float32,
        )[0:1]
        slot = jnp.where(mine, step_of * cap + rank_of, -1.0)
        held = jnp.where(mine, within, -1.0)
        cols = pl.ds(s * routes, routes)
        info_ref[:, cols] = jnp.concatenate([slot, held, jnp.zeros((6, routes), jnp.float32)], axis=0)
        low = nt_dot(down, both[:, :width])
        low = jnp.where(panel_of == held, low, 0.0)
        part_ref[:, cols] = jnp.sum(low.reshape(panels, 2 * rank, routes), axis=0)


def delta_kernel(count, slots, info_ref, own_ref, core_ref, far_ref, diag_ref, up_ref, *refs):
    out_refs, (lhs_ref,) = refs[:count], refs[count:]
    panels, rank, tile = up_ref.shape
    routes = info_ref.shape[1] // count

    @pl.when((pl.program_id(0) == 0) & (pl.program_id(1) == 0))
    def _():
        low = (own_ref[...] + core_ref[...]) + (far_ref[...] + diag_ref[...])
        low = low.astype(jnp.bfloat16).astype(jnp.float32)
        panel_of = (lax.broadcasted_iota(jnp.int32, (panels * rank, routes), 0) // rank).astype(jnp.float32)
        slot_of = lax.broadcasted_iota(jnp.int32, (slots, routes), 0).astype(jnp.float32)
        for s in range(count):
            cols = slice(s * routes, (s + 1) * routes)
            slot, held = info_ref[0:1, cols], info_ref[1:2, cols]
            place = jnp.where(slot_of == slot, 1.0, 0.0).astype(jnp.bfloat16)
            for p in range(2):
                wide = jnp.concatenate([low[p * rank : (p + 1) * rank, cols]] * panels, axis=0)
                wide = jnp.where(panel_of == held, wide, 0.0).astype(jnp.bfloat16)
                lhs_ref[p, s * slots : (s + 1) * slots, :] = nt_dot(place, wide).astype(jnp.bfloat16)

    p = pl.program_id(0)
    up = up_ref[...].reshape(panels * rank, tile)
    delta = jnp.dot(lhs_ref[p], up, preferred_element_type=jnp.float32).astype(jnp.bfloat16)
    for s in range(count):
        out_refs[s][...] = delta[s * slots : (s + 1) * slots]


def gate_kernel(count, group_ref, pick_ref, panel_ref, base_ref, mine_ref, other_ref, *refs):
    blocks, out_ref = refs[: 2 * count], refs[2 * count]
    slots = blocks[0].shape[0]
    group = group_ref[0]
    adapted = []
    for p in range(2):
        delta = None
        for s in range(count):
            part = jnp.dot(
                pick_ref[:, s * slots : (s + 1) * slots],
                blocks[p * count + s][...],
                preferred_element_type=jnp.float32,
            )
            delta = part if delta is None else delta + part
        scales = jnp.where(group == p, mine_ref[...], other_ref[...])
        scale = jnp.dot(panel_ref[...], scales, preferred_element_type=jnp.float32)
        adapted.append(scale * (base_ref[p].astype(jnp.float32) + delta))
    gate, value = adapted
    out_ref[...] = (gate / (1.0 + jnp.exp(-gate)) * value).astype(out_ref.dtype)


CHUNK = 32
LAG = 2
LEAST_CHUNKS = 5


def right_layout(n):
    gap = float(LAG * CHUNK)
    zero = jnp.zeros_like(n[0][0])
    place = {}

    def put(link, j, d, first, split=None, second=None):
        place[link, j, d] = (first, split, second)

    put(0, 0, 3, zero)
    put(0, 0, 2, n[0][3])
    put(0, 0, 1, n[0][3] + n[0][2])
    end = n[0][3] + n[0][2] + n[0][1]
    early = jnp.maximum(jnp.minimum(n[1][2], gap - n[1][3]), 0.0)
    far = jnp.maximum(n[1][3], gap)
    late = far + n[0][3] + n[1][2] - early
    put(1, 1, 3, zero)
    put(1, 0, 3, far)
    put(1, 1, 2, n[1][3], early, far + n[0][3] - early)
    put(1, 0, 2, late)
    end = jnp.maximum(end, late + n[0][2])
    one = jnp.maximum(n[2][3], gap)
    two = jnp.maximum(one + n[1][3], far + gap)
    put(2, 2, 3, zero)
    put(2, 1, 3, one)
    put(2, 0, 3, two)
    return place, jnp.maximum(end, two + n[0][3])


def relay_low_kernel(steps, rows, me_ref, down_ref, *refs):
    count = 4
    state_refs, (part_ref, info_ref) = refs[:count], refs[count:]
    panels, _, rank, width = down_ref.shape
    routes = 2 * steps * rows
    me = me_ref[0]
    down = down_ref[...].reshape(panels * 2 * rank, width)
    pick = jnp.where(
        lax.broadcasted_iota(jnp.int32, (8, LANES), 0) == lax.broadcasted_iota(jnp.int32, (8, LANES), 1), 1.0, 0.0
    ).astype(jnp.bfloat16)
    before = jnp.where(
        lax.broadcasted_iota(jnp.int32, (routes, routes), 0) < lax.broadcasted_iota(jnp.int32, (routes, routes), 1),
        1.0,
        0.0,
    ).astype(jnp.bfloat16)
    lane = lax.broadcasted_iota(jnp.int32, (1, routes), 1)
    owners = lax.broadcasted_iota(jnp.int32, (8, routes), 0).astype(jnp.float32)
    panel_of = (lax.broadcasted_iota(jnp.int32, (panels * 2 * rank, routes), 0) // (2 * rank)).astype(jnp.float32)
    owner, within, order, tally = [], [], [], []
    info_ref[...] = jnp.full(info_ref.shape, -1.0, jnp.float32)
    for s in range(count):
        one = state_refs[s][...]
        both = jnp.concatenate([one, one], axis=0)
        numbers = nt_dot(pick, both[:, width:])
        owner.append(jnp.where(lane < routes // 2, numbers[0:1], numbers[1:2]))
        within.append(jnp.where(lane < routes // 2, numbers[2:3], numbers[3:4]))
        hits = jnp.where(owners == owner[s], 1.0, 0.0)
        ahead = jnp.dot(hits.astype(jnp.bfloat16), before, preferred_element_type=jnp.float32)
        order.append(jnp.sum(ahead * hits, axis=0, keepdims=True))
        tally.append(jnp.sum(hits, axis=1, keepdims=True))
        cols = slice(s * routes, (s + 1) * routes)
        held = jnp.where(owner[s] == me.astype(jnp.float32), within[s], -1.0)
        info_ref[0:1, cols] = held
        low = nt_dot(down, both[:, :width])
        low = jnp.where(panel_of == held, low, 0.0)
        part_ref[:, cols] = jnp.sum(low.reshape(panels, 2 * rank, routes), axis=0)
    info_ref[9:10, 0:routes] = owner[0]
    info_ref[10:11, 0:routes] = within[0]

    def position(place, link, d, s, turned, owners_from, owners_to):
        found = jnp.full((1, routes), -1.0, jnp.float32)
        for j in range(owners_from, owners_to):
            first, split, second = place[link, j, d]
            at = first + order[s]
            if split is not None:
                at = jnp.where(order[s] < split, at, second + order[s])
            found = jnp.where(owner[s] == float(3 - j if turned else j), at, found)
        return found

    for case in range(count):

        @pl.when(me == case)
        def _():
            longest = None
            for turned in (False, True):
                node = 3 - case if turned else case
                n = [[None] * count for _ in range(count)]
                for j in range(count):
                    for d in range(count):
                        s = (case - d) % count
                        if turned:
                            n[3 - j][3 - d] = tally[s][j : j + 1]
                        else:
                            n[j][d] = tally[s][j : j + 1]
                place, end = right_layout(n)
                longest = end if longest is None else jnp.maximum(longest, end)
                row = 4 if turned else 1
                for d in range(node + 1, count):
                    s = (case - (3 - d if turned else d)) % count
                    cols = slice(s * routes, (s + 1) * routes)
                    info_ref[row : row + 1, cols] = position(place, node, d, s, turned, node, node + 1)
                    if node > 0:
                        info_ref[row + 1 : row + 2, cols] = position(place, node, d, s, turned, 0, node)
                        info_ref[row + 2 : row + 3, cols] = position(place, node - 1, d, s, turned, 0, node)
                if node > 0:
                    arrive = 8 if turned else 7
                    info_ref[arrive : arrive + 1, 0:routes] = position(place, node - 1, node, 0, turned, 0, node)
            info_ref[11:12, 0:routes] = jnp.broadcast_to(longest, (1, routes))


def summed_low(own_ref, core_ref, far_ref, diag_ref):
    low = (own_ref[...] + core_ref[...]) + (far_ref[...] + diag_ref[...])
    return low.astype(jnp.bfloat16).astype(jnp.float32)


def spread_low(low, info_ref, panels, p):
    rank = low.shape[0] // 2
    held = info_ref[0:1, :]
    panel_of = lax.broadcasted_iota(jnp.int32, (panels * rank, held.shape[1]), 0) // rank
    wide = jnp.concatenate([low[p * rank : (p + 1) * rank]] * panels, axis=0)
    return jnp.where(panel_of.astype(jnp.float32) == held, wide, 0.0).astype(jnp.bfloat16)


def placed(info_ref, row, slots):
    at = info_ref[row : row + 1, :]
    slot_of = lax.broadcasted_iota(jnp.int32, (slots, at.shape[1]), 0).astype(jnp.float32)
    return jnp.where(slot_of == at, 1.0, 0.0).astype(jnp.bfloat16)


def relay_first_kernel(info_ref, own_ref, core_ref, far_ref, diag_ref, up_ref, *refs):
    chunk_refs, lhs_ref = refs[:4], refs[4]
    panels, rank, tile = up_ref.shape

    @pl.when((pl.program_id(0) == 0) & (pl.program_id(1) == 0))
    def _():
        low = summed_low(own_ref, core_ref, far_ref, diag_ref)
        own = jnp.concatenate([placed(info_ref, 1, 2 * CHUNK), placed(info_ref, 4, 2 * CHUNK)], axis=0)
        for p in range(2):
            lhs_ref[p] = nt_dot(own, spread_low(low, info_ref, panels, p)).astype(jnp.bfloat16)

    up = up_ref[...].reshape(panels * rank, tile)
    delta = jnp.dot(lhs_ref[pl.program_id(0)], up, preferred_element_type=jnp.float32).astype(jnp.bfloat16)
    for i in range(4):
        chunk_refs[i][...] = delta[i * CHUNK : (i + 1) * CHUNK]


def relay_rows_kernel(panels, info_ref, own_ref, core_ref, far_ref, diag_ref, lhs_ref, forward_ref, local_ref):
    limit = lhs_ref.shape[2]
    routes = local_ref.shape[1]
    low = summed_low(own_ref, core_ref, far_ref, diag_ref)
    own = [placed(info_ref, 1, limit), placed(info_ref, 4, limit)]
    same = lax.broadcasted_iota(jnp.int32, (routes, routes), 0) == lax.broadcasted_iota(jnp.int32, (routes, routes), 1)
    same = jnp.where(same, 1.0, 0.0).astype(jnp.bfloat16)
    for p in range(2):
        wide = spread_low(low, info_ref, panels, p)
        for way in range(2):
            lhs_ref[p, way] = nt_dot(own[way], wide).astype(jnp.bfloat16)
        local_ref[p] = nt_dot(same, wide[:, :routes]).astype(jnp.bfloat16)
    for way in range(2):
        forward_ref[way] = nt_dot(
            placed(info_ref, 3 * way + 2, limit), placed(info_ref, 3 * way + 3, limit)
        ).astype(jnp.bfloat16)


def relay_chunk_kernel(known, lhs_ref, forward_ref, up_ref, *refs):
    came, (right_ref, left_ref) = refs[: 2 * known], refs[2 * known :]
    panels, rank, tile = up_ref.shape
    p = pl.program_id(0)
    up = up_ref[...].reshape(panels * rank, tile)
    lhs = jnp.concatenate([lhs_ref[p, 0], lhs_ref[p, 1]], axis=0)
    delta = jnp.dot(lhs, up, preferred_element_type=jnp.float32)
    for way, out_ref in ((0, right_ref), (1, left_ref)):
        rows = jnp.concatenate([came[way * known + i][...] for i in range(known)], axis=0)
        passed = jnp.dot(forward_ref[way][:, : known * CHUNK], rows, preferred_element_type=jnp.float32)
        out_ref[...] = (delta[way * CHUNK : (way + 1) * CHUNK] + passed).astype(out_ref.dtype)


def relay_pick_kernel(blocks, pick_ref, local_ref, up_ref, *refs):
    came, out_ref = refs[:blocks], refs[blocks]
    panels, rank, tile = up_ref.shape
    up = up_ref[...].reshape(panels * rank, tile)
    delta = jnp.dot(local_ref[pl.program_id(0)], up, preferred_element_type=jnp.float32).astype(jnp.bfloat16)
    rows = jnp.concatenate([block[...] for block in came], axis=0)
    picked = jnp.dot(pick_ref[...], rows, preferred_element_type=jnp.float32)
    out_ref[...] = (delta.astype(jnp.float32) + picked).astype(out_ref.dtype)


def relay_gate_kernel(group_ref, pick_ref, panel_ref, base_ref, mine_ref, other_ref, *refs):
    out_ref = refs[-1]
    group = group_ref[0]
    adapted = []
    for p in range(2):
        early, right, left = refs[3 * p : 3 * p + 3]
        rows = jnp.concatenate([right[...], left[...]], axis=0)
        delta = early[...].astype(jnp.float32) + jnp.dot(pick_ref[...], rows, preferred_element_type=jnp.float32)
        scales = jnp.where(group == p, mine_ref[...], other_ref[...])
        scale = jnp.dot(panel_ref[...], scales, preferred_element_type=jnp.float32)
        adapted.append(scale * (base_ref[p].astype(jnp.float32) + delta))
    gate, value = adapted
    out_ref[...] = (gate / (1.0 + jnp.exp(-gate)) * value).astype(out_ref.dtype)


def relayed(seen, mine, other, base, down, up):
    count = 4
    me, group = lax.axis_index("dp"), lax.axis_index("groups")
    steps, rows, hidden = base.shape[0], base.shape[1], base.shape[-1]
    panels, _, rank, _ = down.shape
    routes = 2 * steps * rows
    cap = max(2, (5 * rows + count - 1) // count)
    gap = LAG * CHUNK
    limit = max(
        3 * steps * cap,
        2 * routes,
        gap + 2 * steps * cap,
        gap + routes,
        2 * gap + steps * cap,
    )
    limit = -(-limit // CHUNK) * CHUNK
    most = limit // CHUNK
    bf16, f32, i32 = jnp.bfloat16, jnp.float32, jnp.int32
    vmem = pl.BlockSpec(memory_space=pltpu.VMEM)
    smem = pl.BlockSpec(memory_space=pltpu.SMEM)
    params = pltpu.CompilerParams(vmem_limit_bytes=VMEM_LIMIT)

    part, info = pl.pallas_call(
        functools.partial(relay_low_kernel, steps, rows),
        out_shape=(
            jax.ShapeDtypeStruct((2 * rank, count * routes), f32),
            jax.ShapeDtypeStruct((16, count * routes), f32),
        ),
        in_specs=[smem] + [vmem] * (1 + count),
        out_specs=(vmem, vmem),
        compiler_params=params,
    )(me.reshape(1).astype(i32), down, *seen)
    lows = [part]
    for mask in (1, 2, 3):
        lows.append(lax.ppermute(part, ("expert", "pair"), [(i, i ^ mask) for i in range(4)]))
    longest = info[8:16, 0:LANES]
    longest = jnp.maximum(longest, lax.ppermute(longest, "groups", [(0, 1), (1, 0)]))[3, 0]

    tile = min(1024, hidden)
    col_tiles = hidden // tile
    whole = lambda shape: pl.BlockSpec(shape, lambda p, n: (0,) * len(shape))
    up_block = pl.BlockSpec((panels, None, rank, tile), lambda p, n: (0, p, 0, n))
    row_block = pl.BlockSpec((CHUNK, tile), lambda p, n: (0, p * col_tiles + n))
    chunk_shape = jax.ShapeDtypeStruct((CHUNK, 2 * hidden), bf16)
    first = pl.pallas_call(
        relay_first_kernel,
        out_shape=[chunk_shape] * 4,
        grid=(2, col_tiles),
        in_specs=[whole(info.shape)] + [whole(part.shape)] * 4 + [up_block],
        out_specs=[row_block] * 4,
        scratch_shapes=[pltpu.VMEM((2, 4 * CHUNK, panels * rank), bf16)],
        compiler_params=params,
    )(info, *lows, up)
    right_first, left_first = first[0:2], first[2:4]
    shapes = ((2, 2, limit, panels * rank), (2, limit, limit), (2, routes, panels * rank))
    lhs, forward, local = pl.pallas_call(
        functools.partial(relay_rows_kernel, panels),
        out_shape=[jax.ShapeDtypeStruct(shape, bf16) for shape in shapes],
        in_specs=[vmem] * 5,
        out_specs=[vmem] * 3,
        compiler_params=params,
    )(info, *lows)

    owner, within = info[9, :routes].astype(i32), info[10, :routes].astype(i32)
    behind = (me - owner) % count
    panel = (jnp.arange(count * panels, dtype=i32)[None, :] == (behind * panels + within)[:, None]).astype(bf16)
    base_rows = base.transpose(3, 2, 0, 1, 4).reshape(2, routes, hidden)
    slot = jnp.arange(limit, dtype=f32)[None, :]
    from_left = (slot == info[7, :routes, None]).astype(bf16)
    from_right = (slot == info[8, :routes, None]).astype(bf16)
    here = group.reshape(1).astype(i32)

    def flow(chunks, operands):
        right_first, left_first, lhs, forward, local, up, panel, base_rows, from_left, from_right, mine, other = operands
        got_right, got_left = [], []
        for k in range(chunks):
            if k < LAG:
                right, left = right_first[k], left_first[k]
            else:
                known = k + 1 - LAG
                right, left = pl.pallas_call(
                    functools.partial(relay_chunk_kernel, known),
                    out_shape=[chunk_shape] * 2,
                    grid=(2, col_tiles),
                    in_specs=[
                        pl.BlockSpec((2, 2, CHUNK, panels * rank), lambda p, n, k=k: (0, 0, k, 0)),
                        pl.BlockSpec((2, CHUNK, limit), lambda p, n, k=k: (0, k, 0)),
                        up_block,
                    ]
                    + [row_block] * (2 * known),
                    out_specs=[row_block] * 2,
                    compiler_params=params,
                    cost_estimate=pl.CostEstimate(
                        flops=2 * 2 * CHUNK * 512 * 2 * hidden, bytes_accessed=8 << 20, transcendentals=0
                    ),
                )(lhs, forward, up, *got_right[:known], *got_left[:known])
            got_right.append(lax.ppermute(right, "dp", [(i, i + 1) for i in range(count - 1)]))
            got_left.append(lax.ppermute(left, "dp", [(i + 1, i) for i in range(count - 1)]))
        last = (chunks - 1) * CHUNK
        early = jnp.concatenate([from_left[:, :last], from_right[:, :last]], axis=1)
        late = jnp.concatenate([from_left[:, last : last + CHUNK], from_right[:, last : last + CHUNK]], axis=1)
        came = got_right[:-1] + got_left[:-1]
        routes_block = pl.BlockSpec((routes, tile), lambda p, n: (0, p * col_tiles + n))
        picked = pl.pallas_call(
            functools.partial(relay_pick_kernel, len(came)),
            out_shape=jax.ShapeDtypeStruct((routes, 2 * hidden), bf16),
            grid=(2, col_tiles),
            in_specs=[whole(early.shape), whole(local.shape), up_block] + [row_block] * len(came),
            out_specs=routes_block,
            compiler_params=params,
            cost_estimate=pl.CostEstimate(flops=2 * routes * 512 * 2 * hidden, bytes_accessed=12 << 20, transcendentals=0),
        )(early, local, up, *came)
        flat = lambda shape: pl.BlockSpec(shape, lambda n: (0,) * len(shape))
        col = lambda depth, p: pl.BlockSpec((depth, tile), lambda n, p=p: (0, p * col_tiles + n))
        pieces = [col(routes, 0), col(CHUNK, 0), col(CHUNK, 0), col(routes, 1), col(CHUNK, 1), col(CHUNK, 1)]
        return pl.pallas_call(
            relay_gate_kernel,
            out_shape=jax.ShapeDtypeStruct((routes, hidden), bf16),
            grid=(col_tiles,),
            in_specs=[smem, flat(late.shape), flat(panel.shape)]
            + [pl.BlockSpec((2, routes, tile), lambda n: (0, 0, n))]
            + [col(count * panels, 0)] * 2
            + pieces,
            out_specs=col(routes, 0),
            compiler_params=params,
        )(here, late, panel, base_rows, mine, other, *([picked, got_right[-1], got_left[-1]] * 2))

    operands = (right_first, left_first, lhs, forward, local, up, panel, base_rows, from_left, from_right, mine, other)
    branch = jnp.clip((longest.astype(i32) + CHUNK - 1) // CHUNK - LEAST_CHUNKS, 0, most - LEAST_CHUNKS)
    out = lax.switch(branch, [functools.partial(flow, c) for c in range(LEAST_CHUNKS, most + 1)], operands)
    return out.reshape(2, steps, rows, hidden).transpose(1, 2, 0, 3)


def on_device(states, base, route_panels, down, up, magnitude):
    count = lax.axis_size("dp")
    me = lax.axis_index("dp")
    group = lax.axis_index("groups")
    steps, rows, width = states.shape
    hidden = base.shape[-1]
    panels, _, rank, _ = down.shape
    routes = 2 * steps * rows
    cap = max(2, (5 * rows + count - 1) // count)
    slots = -(-steps * cap // ROW_TILE) * ROW_TILE
    bf16, f32, i32 = jnp.bfloat16, jnp.float32, jnp.int32

    def turn(x, shift):
        return lax.ppermute(x, "dp", [(i, (i + shift) % count) for i in range(count)])

    pairs = route_panels.reshape(steps * rows, 2)
    numbers = jnp.concatenate([pairs // panels, pairs % panels], axis=1).astype(bf16)
    sent = jnp.concatenate(
        [states.reshape(steps * rows, width), jnp.pad(numbers, ((0, 0), (0, LANES - 4)))], axis=1
    )
    seen = [sent] + [turn(sent, s) for s in range(1, count)]

    half = lax.dynamic_index_in_dim(magnitude, group, axis=1, keepdims=False)
    half, *seen = lax.optimization_barrier((half, *seen))
    mine = jnp.concatenate([half] + [turn(half, s) for s in range(1, count)], axis=0)
    other = lax.ppermute(mine, "groups", [(0, 1), (1, 0)])

    if (count, lax.axis_size("expert"), lax.axis_size("pair")) == (4, 2, 2):
        return relayed(seen, mine, other, base, down, up)

    vmem = pl.BlockSpec(memory_space=pltpu.VMEM)
    smem = pl.BlockSpec(memory_space=pltpu.SMEM)
    params = pltpu.CompilerParams(vmem_limit_bytes=VMEM_LIMIT)
    part, info = pl.pallas_call(
        functools.partial(low_kernel, count, steps, rows, cap, slots),
        out_shape=(
            jax.ShapeDtypeStruct((2 * rank, count * routes), f32),
            jax.ShapeDtypeStruct((8, count * routes), f32),
        ),
        in_specs=[smem] + [vmem] * (1 + count),
        out_specs=(vmem, vmem),
        compiler_params=params,
    )(me.reshape(1).astype(i32), down, *seen)

    expert, pair = lax.axis_size("expert"), lax.axis_size("pair")
    lows = [part]
    if (expert, pair) == (2, 2):
        for mask in (1, 2, 3):
            lows.append(lax.ppermute(part, ("expert", "pair"), [(i, i ^ mask) for i in range(4)]))
    else:
        total = lax.psum(part, ("expert", "pair"))
        lows = [total] + [jnp.zeros_like(total)] * 3

    tile = min(1024, hidden)
    col_tiles = hidden // tile
    whole = lambda shape: pl.BlockSpec(shape, lambda p, n: (0,) * len(shape))
    deltas = pl.pallas_call(
        functools.partial(delta_kernel, count, slots),
        out_shape=[jax.ShapeDtypeStruct((slots, 2 * hidden), bf16)] * count,
        grid=(2, col_tiles),
        in_specs=[whole(info.shape)]
        + [whole(part.shape)] * 4
        + [pl.BlockSpec((panels, None, rank, tile), lambda p, n: (0, p, 0, n))],
        out_specs=[pl.BlockSpec((slots, tile), lambda p, n: (0, p * col_tiles + n))] * count,
        scratch_shapes=[pltpu.VMEM((2, count * slots, panels * rank), bf16)],
        compiler_params=params,
    )(info, *lows, up)
    got = [deltas[0]] + [turn(deltas[s], count - s) for s in range(1, count)]

    ordered = route_panels.transpose(2, 0, 1).reshape(2, steps, rows)
    owner, within = ordered // panels, ordered % panels
    by_step = owner.transpose(1, 0, 2).reshape(steps, 2 * rows)
    earlier = jnp.tril(jnp.ones((2 * rows, 2 * rows), jnp.bool_), -1)
    rank_of = jnp.sum((by_step[:, :, None] == by_step[:, None, :]) & earlier[None], axis=2, dtype=i32)
    slot = rank_of + jnp.arange(steps, dtype=i32)[:, None] * cap
    slot = slot.reshape(steps, 2, rows).transpose(1, 0, 2).reshape(routes)
    owner, within = owner.reshape(routes), within.reshape(routes)
    ahead = (owner - me) % count
    behind = (me - owner) % count
    pick = (jnp.arange(count * slots, dtype=i32)[None, :] == (ahead * slots + slot)[:, None]).astype(bf16)
    panel = (jnp.arange(count * panels, dtype=i32)[None, :] == (behind * panels + within)[:, None]).astype(bf16)
    base_rows = base.transpose(3, 2, 0, 1, 4).reshape(2, routes, hidden)

    tile = min(512, hidden)
    col_tiles = hidden // tile
    whole = lambda shape: pl.BlockSpec(shape, lambda n: (0,) * len(shape))
    col = lambda depth, p: pl.BlockSpec((depth, tile), lambda n, p=p: (0, p * col_tiles + n))
    out = pl.pallas_call(
        functools.partial(gate_kernel, count),
        out_shape=jax.ShapeDtypeStruct((routes, hidden), bf16),
        grid=(col_tiles,),
        in_specs=[smem, whole(pick.shape), whole(panel.shape)]
        + [pl.BlockSpec((2, routes, tile), lambda n: (0, 0, n))]
        + [col(count * panels, 0)] * 2
        + [col(slots, 0)] * count
        + [col(slots, 1)] * count,
        out_specs=col(routes, 0),
        compiler_params=params,
    )(group.reshape(1).astype(i32), pick, panel, base_rows, mine, other, *got, *got)
    return out.reshape(2, steps, rows, hidden).transpose(1, 2, 0, 3)


def solution(mesh):
    return jax.shard_map(
        on_device,
        mesh=mesh,
        in_specs=(
            P(None, ("groups", "dp"), ("expert", "pair")),
            P(None, ("groups", "dp"), None, None, ("expert", "pair")),
            P(None, ("groups", "dp"), None),
            P("dp", None, None, ("expert", "pair")),
            P("dp", None, None, ("expert", "pair")),
            P("dp", None, ("expert", "pair")),
        ),
        out_specs=P(None, ("groups", "dp"), None, ("expert", "pair")),
        check_vma=False,
    )
```

```python
import functools

import jax
import jax.numpy as jnp
from jax import lax
from jax.experimental import pallas as pl
from jax.experimental.pallas import tpu as pltpu
from jax.sharding import PartitionSpec as P

LANES = 128
ROW_TILE = 16
VMEM_LIMIT = 20 * 1024 * 1024


def nt_dot(a, b):
    return lax.dot_general(a, b, (((1,), (1,)), ((), ())), preferred_element_type=jnp.float32)


def earlier_in_step(steps, rows):
    routes = 2 * steps * rows
    first = lax.broadcasted_iota(jnp.int32, (routes, routes), 0)
    second = lax.broadcasted_iota(jnp.int32, (routes, routes), 1)
    same = (first // rows) % steps == (second // rows) % steps
    return jnp.where(same & (first < second), 1.0, 0.0).astype(jnp.bfloat16)


def low_kernel(count, steps, rows, cap, slots, me_ref, down_ref, *refs):
    state_refs, (part_ref, info_ref) = refs[:count], refs[count:]
    panels, _, rank, width = down_ref.shape
    routes = 2 * steps * rows
    me = me_ref[0].astype(jnp.float32)
    down = down_ref[...].reshape(panels * 2 * rank, width)
    pick = jnp.where(
        lax.broadcasted_iota(jnp.int32, (8, LANES), 0) == lax.broadcasted_iota(jnp.int32, (8, LANES), 1), 1.0, 0.0
    ).astype(jnp.bfloat16)
    before = earlier_in_step(steps, rows)
    lane = lax.broadcasted_iota(jnp.int32, (1, routes), 1)
    step_of = ((lane // rows) % steps).astype(jnp.float32)
    panel_of = (lax.broadcasted_iota(jnp.int32, (panels * 2 * rank, routes), 0) // (2 * rank)).astype(jnp.float32)
    for s in range(count):
        one = state_refs[s][...]
        both = jnp.concatenate([one, one], axis=0)
        numbers = nt_dot(pick, both[:, width:])
        owner = jnp.where(lane < routes // 2, numbers[0:1], numbers[1:2])
        within = jnp.where(lane < routes // 2, numbers[2:3], numbers[3:4])
        mine = owner == me
        rank_of = jnp.dot(
            jnp.broadcast_to(jnp.where(mine, 1.0, 0.0), (8, routes)).astype(jnp.bfloat16),
            before,
            preferred_element_type=jnp.float32,
        )[0:1]
        slot = jnp.where(mine, step_of * cap + rank_of, -1.0)
        held = jnp.where(mine, within, -1.0)
        cols = pl.ds(s * routes, routes)
        info_ref[:, cols] = jnp.concatenate([slot, held, jnp.zeros((6, routes), jnp.float32)], axis=0)
        low = nt_dot(down, both[:, :width])
        low = jnp.where(panel_of == held, low, 0.0)
        part_ref[:, cols] = jnp.sum(low.reshape(panels, 2 * rank, routes), axis=0)


def delta_kernel(count, slots, info_ref, own_ref, core_ref, far_ref, diag_ref, up_ref, *refs):
    out_refs, (lhs_ref,) = refs[:count], refs[count:]
    panels, rank, tile = up_ref.shape
    routes = info_ref.shape[1] // count

    @pl.when((pl.program_id(0) == 0) & (pl.program_id(1) == 0))
    def _():
        low = (own_ref[...] + core_ref[...]) + (far_ref[...] + diag_ref[...])
        low = low.astype(jnp.bfloat16).astype(jnp.float32)
        panel_of = (lax.broadcasted_iota(jnp.int32, (panels * rank, routes), 0) // rank).astype(jnp.float32)
        slot_of = lax.broadcasted_iota(jnp.int32, (slots, routes), 0).astype(jnp.float32)
        for s in range(count):
            cols = slice(s * routes, (s + 1) * routes)
            slot, held = info_ref[0:1, cols], info_ref[1:2, cols]
            place = jnp.where(slot_of == slot, 1.0, 0.0).astype(jnp.bfloat16)
            for p in range(2):
                wide = jnp.concatenate([low[p * rank : (p + 1) * rank, cols]] * panels, axis=0)
                wide = jnp.where(panel_of == held, wide, 0.0).astype(jnp.bfloat16)
                lhs_ref[p, s * slots : (s + 1) * slots, :] = nt_dot(place, wide).astype(jnp.bfloat16)

    p = pl.program_id(0)
    up = up_ref[...].reshape(panels * rank, tile)
    delta = jnp.dot(lhs_ref[p], up, preferred_element_type=jnp.float32).astype(jnp.bfloat16)
    for s in range(count):
        out_refs[s][...] = delta[s * slots : (s + 1) * slots]


def gate_kernel(count, group_ref, pick_ref, panel_ref, base_ref, mine_ref, other_ref, *refs):
    blocks, out_ref = refs[: 2 * count], refs[2 * count]
    slots = blocks[0].shape[0]
    group = group_ref[0]
    adapted = []
    for p in range(2):
        delta = None
        for s in range(count):
            part = jnp.dot(
                pick_ref[:, s * slots : (s + 1) * slots],
                blocks[p * count + s][...],
                preferred_element_type=jnp.float32,
            )
            delta = part if delta is None else delta + part
        scales = jnp.where(group == p, mine_ref[...], other_ref[...])
        scale = jnp.dot(panel_ref[...], scales, preferred_element_type=jnp.float32)
        adapted.append(scale * (base_ref[p].astype(jnp.float32) + delta))
    gate, value = adapted
    out_ref[...] = (gate / (1.0 + jnp.exp(-gate)) * value).astype(out_ref.dtype)


CHUNK = 32
LAG = 2
LEAST_CHUNKS = 5


def right_layout(n):
    gap = float(LAG * CHUNK)
    zero = jnp.zeros_like(n[0][0])
    place = {}

    def put(link, j, d, first, split=None, second=None):
        place[link, j, d] = (first, split, second)

    put(0, 0, 3, zero)
    put(0, 0, 2, n[0][3])
    put(0, 0, 1, n[0][3] + n[0][2])
    end = n[0][3] + n[0][2] + n[0][1]
    early = jnp.maximum(jnp.minimum(n[1][2], gap - n[1][3]), 0.0)
    far = jnp.maximum(n[1][3], gap)
    late = far + n[0][3] + n[1][2] - early
    put(1, 1, 3, zero)
    put(1, 0, 3, far)
    put(1, 1, 2, n[1][3], early, far + n[0][3] - early)
    put(1, 0, 2, late)
    end = jnp.maximum(end, late + n[0][2])
    one = jnp.maximum(n[2][3], gap)
    two = jnp.maximum(one + n[1][3], far + gap)
    put(2, 2, 3, zero)
    put(2, 1, 3, one)
    put(2, 0, 3, two)
    return place, jnp.maximum(end, two + n[0][3])


def relay_low_kernel(steps, rows, me_ref, down_ref, *refs):
    count = 4
    state_refs, (part_ref, info_ref) = refs[:count], refs[count:]
    panels, _, rank, width = down_ref.shape
    routes = 2 * steps * rows
    me = me_ref[0]
    down = down_ref[...].reshape(panels * 2 * rank, width)
    pick = jnp.where(
        lax.broadcasted_iota(jnp.int32, (8, LANES), 0) == lax.broadcasted_iota(jnp.int32, (8, LANES), 1), 1.0, 0.0
    ).astype(jnp.bfloat16)
    before = jnp.where(
        lax.broadcasted_iota(jnp.int32, (routes, routes), 0) < lax.broadcasted_iota(jnp.int32, (routes, routes), 1),
        1.0,
        0.0,
    ).astype(jnp.bfloat16)
    lane = lax.broadcasted_iota(jnp.int32, (1, routes), 1)
    owners = lax.broadcasted_iota(jnp.int32, (8, routes), 0).astype(jnp.float32)
    panel_of = (lax.broadcasted_iota(jnp.int32, (panels * 2 * rank, routes), 0) // (2 * rank)).astype(jnp.float32)
    owner, within, order, tally = [], [], [], []
    info_ref[...] = jnp.full(info_ref.shape, -1.0, jnp.float32)
    for s in range(count):
        one = state_refs[s][...]
        both = jnp.concatenate([one, one], axis=0)
        numbers = nt_dot(pick, both[:, width:])
        owner.append(jnp.where(lane < routes // 2, numbers[0:1], numbers[1:2]))
        within.append(jnp.where(lane < routes // 2, numbers[2:3], numbers[3:4]))
        hits = jnp.where(owners == owner[s], 1.0, 0.0)
        ahead = jnp.dot(hits.astype(jnp.bfloat16), before, preferred_element_type=jnp.float32)
        order.append(jnp.sum(ahead * hits, axis=0, keepdims=True))
        tally.append(jnp.sum(hits, axis=1, keepdims=True))
        cols = slice(s * routes, (s + 1) * routes)
        held = jnp.where(owner[s] == me.astype(jnp.float32), within[s], -1.0)
        info_ref[0:1, cols] = held
        low = nt_dot(down, both[:, :width])
        low = jnp.where(panel_of == held, low, 0.0)
        part_ref[:, cols] = jnp.sum(low.reshape(panels, 2 * rank, routes), axis=0)
    info_ref[9:10, 0:routes] = owner[0]
    info_ref[10:11, 0:routes] = within[0]

    def position(place, link, d, s, turned, owners_from, owners_to):
        found = jnp.full((1, routes), -1.0, jnp.float32)
        for j in range(owners_from, owners_to):
            first, split, second = place[link, j, d]
            at = first + order[s]
            if split is not None:
                at = jnp.where(order[s] < split, at, second + order[s])
            found = jnp.where(owner[s] == float(3 - j if turned else j), at, found)
        return found

    for case in range(count):

        @pl.when(me == case)
        def _():
            longest = None
            for turned in (False, True):
                node = 3 - case if turned else case
                n = [[None] * count for _ in range(count)]
                for j in range(count):
                    for d in range(count):
                        s = (case - d) % count
                        if turned:
                            n[3 - j][3 - d] = tally[s][j : j + 1]
                        else:
                            n[j][d] = tally[s][j : j + 1]
                place, end = right_layout(n)
                longest = end if longest is None else jnp.maximum(longest, end)
                row = 4 if turned else 1
                for d in range(node + 1, count):
                    s = (case - (3 - d if turned else d)) % count
                    cols = slice(s * routes, (s + 1) * routes)
                    info_ref[row : row + 1, cols] = position(place, node, d, s, turned, node, node + 1)
                    if node > 0:
                        info_ref[row + 1 : row + 2, cols] = position(place, node, d, s, turned, 0, node)
                        info_ref[row + 2 : row + 3, cols] = position(place, node - 1, d, s, turned, 0, node)
                if node > 0:
                    arrive = 8 if turned else 7
                    info_ref[arrive : arrive + 1, 0:routes] = position(place, node - 1, node, 0, turned, 0, node)
            info_ref[11:12, 0:routes] = jnp.broadcast_to(longest, (1, routes))


def summed_low(own_ref, core_ref, far_ref, diag_ref):
    low = (own_ref[...] + core_ref[...]) + (far_ref[...] + diag_ref[...])
    return low.astype(jnp.bfloat16).astype(jnp.float32)


def spread_low(low, info_ref, panels, p):
    rank = low.shape[0] // 2
    held = info_ref[0:1, :]
    panel_of = lax.broadcasted_iota(jnp.int32, (panels * rank, held.shape[1]), 0) // rank
    wide = jnp.concatenate([low[p * rank : (p + 1) * rank]] * panels, axis=0)
    return jnp.where(panel_of.astype(jnp.float32) == held, wide, 0.0).astype(jnp.bfloat16)


def placed(info_ref, row, slots):
    at = info_ref[row : row + 1, :]
    slot_of = lax.broadcasted_iota(jnp.int32, (slots, at.shape[1]), 0).astype(jnp.float32)
    return jnp.where(slot_of == at, 1.0, 0.0).astype(jnp.bfloat16)


def relay_first_kernel(panels, info_ref, own_ref, core_ref, far_ref, diag_ref, up_ref, *chunk_refs):
    _, _, hidden = up_ref.shape
    tile = min(1024, hidden)
    low = summed_low(own_ref, core_ref, far_ref, diag_ref)
    own = jnp.concatenate([placed(info_ref, 1, 2 * CHUNK), placed(info_ref, 4, 2 * CHUNK)], axis=0)
    for p in range(2):
        lhs = nt_dot(own, spread_low(low, info_ref, panels, p)).astype(jnp.bfloat16)
        for col in range(0, hidden, tile):
            delta = jnp.dot(lhs, up_ref[p, :, col : col + tile], preferred_element_type=jnp.float32)
            delta = delta.astype(jnp.bfloat16)
            for i in range(4):
                at = p * hidden + col
                chunk_refs[i][:, at : at + tile] = delta[i * CHUNK : (i + 1) * CHUNK]


def relay_rows_kernel(panels, info_ref, own_ref, core_ref, far_ref, diag_ref, lhs_ref, forward_ref, local_ref):
    limit = lhs_ref.shape[2]
    routes = local_ref.shape[1]
    low = summed_low(own_ref, core_ref, far_ref, diag_ref)
    own = [placed(info_ref, 1, limit), placed(info_ref, 4, limit)]
    same = lax.broadcasted_iota(jnp.int32, (routes, routes), 0) == lax.broadcasted_iota(jnp.int32, (routes, routes), 1)
    same = jnp.where(same, 1.0, 0.0).astype(jnp.bfloat16)
    for p in range(2):
        wide = spread_low(low, info_ref, panels, p)
        for way in range(2):
            lhs_ref[p, way] = nt_dot(own[way], wide).astype(jnp.bfloat16)
        local_ref[p] = nt_dot(same, wide[:, :routes]).astype(jnp.bfloat16)
    for way in range(2):
        forward_ref[way] = nt_dot(
            placed(info_ref, 3 * way + 2, limit), placed(info_ref, 3 * way + 3, limit)
        ).astype(jnp.bfloat16)


def relay_chunk_kernel(index, lhs_ref, forward_ref, up_ref, *refs):
    known = index + 1 - LAG
    came, (right_ref, left_ref) = refs[: 2 * known], refs[2 * known :]
    _, _, hidden = up_ref.shape
    tile = min(1024, hidden)
    here = slice(index * CHUNK, (index + 1) * CHUNK)
    for p in range(2):
        lhs = jnp.concatenate([lhs_ref[p, 0, here, :], lhs_ref[p, 1, here, :]], axis=0)
        for col in range(0, hidden, tile):
            delta = jnp.dot(lhs, up_ref[p, :, col : col + tile], preferred_element_type=jnp.float32)
            at = p * hidden + col
            for way, out_ref in ((0, right_ref), (1, left_ref)):
                rows = jnp.concatenate([came[way * known + i][:, at : at + tile] for i in range(known)], axis=0)
                passed = jnp.dot(
                    forward_ref[way, here, : known * CHUNK], rows, preferred_element_type=jnp.float32
                )
                out_ref[:, at : at + tile] = (delta[way * CHUNK : (way + 1) * CHUNK] + passed).astype(out_ref.dtype)


def relay_pick_kernel(pick_ref, local_ref, up_ref, *refs):
    came, out_ref = refs[:-1], refs[-1]
    _, _, hidden = up_ref.shape
    tile = min(1024, hidden)
    for p in range(2):
        for col in range(0, hidden, tile):
            delta = jnp.dot(local_ref[p], up_ref[p, :, col : col + tile], preferred_element_type=jnp.float32)
            at = p * hidden + col
            rows = jnp.concatenate([block[:, at : at + tile] for block in came], axis=0)
            picked = jnp.dot(pick_ref[...], rows, preferred_element_type=jnp.float32)
            delta = delta.astype(jnp.bfloat16).astype(jnp.float32)
            out_ref[:, at : at + tile] = (delta + picked).astype(out_ref.dtype)


def relay_gate_kernel(group_ref, pick_ref, panel_ref, base_ref, mine_ref, other_ref, early_ref, right_ref, left_ref, out_ref):
    hidden = out_ref.shape[1]
    tile = min(512, hidden)
    group = group_ref[0]
    for col in range(0, hidden, tile):
        scales = [mine_ref[:, col : col + tile], other_ref[:, col : col + tile]]
        scales = [jnp.dot(panel_ref[...], part, preferred_element_type=jnp.float32) for part in scales]
        adapted = []
        for p in range(2):
            at = p * hidden + col
            rows = jnp.concatenate([right_ref[:, at : at + tile], left_ref[:, at : at + tile]], axis=0)
            delta = early_ref[:, at : at + tile].astype(jnp.float32) + jnp.dot(
                pick_ref[...], rows, preferred_element_type=jnp.float32
            )
            scale = jnp.where(group == p, scales[0], scales[1])
            adapted.append(scale * (base_ref[p, :, col : col + tile].astype(jnp.float32) + delta))
        gate, value = adapted
        out_ref[:, col : col + tile] = (gate / (1.0 + jnp.exp(-gate)) * value).astype(out_ref.dtype)


def relayed(seen, turn, magnitude, base, down, up):
    count = 4
    me, group = lax.axis_index("dp"), lax.axis_index("groups")
    steps, rows, hidden = base.shape[0], base.shape[1], base.shape[-1]
    panels, _, rank, _ = down.shape
    routes = 2 * steps * rows
    cap = max(2, (5 * rows + count - 1) // count)
    gap = LAG * CHUNK
    limit = max(
        3 * steps * cap,
        2 * routes,
        gap + 2 * steps * cap,
        gap + routes,
        2 * gap + steps * cap,
    )
    limit = -(-limit // CHUNK) * CHUNK
    most = limit // CHUNK
    bf16, f32, i32 = jnp.bfloat16, jnp.float32, jnp.int32
    vmem = pl.BlockSpec(memory_space=pltpu.VMEM)
    smem = pl.BlockSpec(memory_space=pltpu.SMEM)

    def kernel(body, inputs, outputs, flops=0, scalars=0):
        return pl.pallas_call(
            body,
            out_shape=[jax.ShapeDtypeStruct(shape, dtype) for shape, dtype in outputs],
            in_specs=[smem] * scalars + [vmem] * (len(inputs) - scalars),
            out_specs=[vmem] * len(outputs),
            compiler_params=pltpu.CompilerParams(vmem_limit_bytes=VMEM_LIMIT),
            cost_estimate=pl.CostEstimate(flops=flops, bytes_accessed=8 << 20, transcendentals=0),
        )(*inputs)

    up_rows = up.transpose(1, 0, 2, 3).reshape(2, panels * rank, hidden)
    base_rows = base.transpose(3, 2, 0, 1, 4).reshape(2, routes, hidden)
    half = lax.dynamic_index_in_dim(magnitude, group, axis=1, keepdims=False)
    up_rows, base_rows, half, *seen = lax.optimization_barrier((up_rows, base_rows, half, *seen))

    part, info = kernel(
        functools.partial(relay_low_kernel, steps, rows),
        [me.reshape(1).astype(i32), down, *seen],
        [((2 * rank, count * routes), f32), ((16, count * routes), f32)],
        scalars=1,
    )
    lows = [part]
    for mask in (1, 2, 3):
        lows.append(lax.ppermute(part, ("expert", "pair"), [(i, i ^ mask) for i in range(4)]))
    longest = info[8:16, 0:LANES]
    longest = jnp.maximum(longest, lax.ppermute(longest, "groups", [(0, 1), (1, 0)]))[3, 0]

    scales = [half, turn(lax.optimization_barrier((half, part))[0], 1)]
    after = lax.optimization_barrier((half, *lows))[0]
    scales += [turn(after, 2), turn(after, 3)]

    chunk = ((CHUNK, 2 * hidden), bf16)
    first = kernel(functools.partial(relay_first_kernel, panels), [info, *lows, up_rows], [chunk] * 4)
    right_first, left_first = first[0:2], first[2:4]
    lhs, forward, local = kernel(
        functools.partial(relay_rows_kernel, panels),
        [info, *lows],
        [((2, 2, limit, panels * rank), bf16), ((2, limit, limit), bf16), ((2, routes, panels * rank), bf16)],
    )

    owner, within = info[9, :routes].astype(i32), info[10, :routes].astype(i32)
    behind = (me - owner) % count
    panel = (jnp.arange(count * panels, dtype=i32)[None, :] == (behind * panels + within)[:, None]).astype(bf16)
    slot = jnp.arange(limit, dtype=f32)[None, :]
    from_left = (slot == info[7, :routes, None]).astype(bf16)
    from_right = (slot == info[8, :routes, None]).astype(bf16)
    here = group.reshape(1).astype(i32)

    def flow(chunks, operands):
        right_first, left_first, lhs, forward, local, up_rows, panel, base_rows, from_left, from_right, scales = operands
        got_right, got_left = [], []
        for k in range(chunks):
            if k < LAG:
                right, left = right_first[k], left_first[k]
            else:
                known = k + 1 - LAG
                right, left = kernel(
                    functools.partial(relay_chunk_kernel, k),
                    [lhs, forward, up_rows, *got_right[:known], *got_left[:known]],
                    [chunk] * 2,
                    flops=2 * 2 * CHUNK * 512 * 2 * hidden,
                )
            got_right.append(lax.ppermute(right, "dp", [(i, i + 1) for i in range(count - 1)]))
            got_left.append(lax.ppermute(left, "dp", [(i + 1, i) for i in range(count - 1)]))
        *scales, _ = lax.optimization_barrier((*scales, got_right[LAG - 1]))
        mine = jnp.concatenate(scales, axis=0)
        other = lax.ppermute(mine, "groups", [(0, 1), (1, 0)])
        last = (chunks - 1) * CHUNK
        early = jnp.concatenate([from_left[:, :last], from_right[:, :last]], axis=1)
        late = jnp.concatenate([from_left[:, last : last + CHUNK], from_right[:, last : last + CHUNK]], axis=1)
        [picked] = kernel(
            relay_pick_kernel,
            [early, local, up_rows, *got_right[:-1], *got_left[:-1]],
            [((routes, 2 * hidden), bf16)],
            flops=2 * routes * 512 * 2 * hidden,
        )
        [out] = kernel(
            relay_gate_kernel,
            [here, late, panel, base_rows, mine, other, picked, got_right[-1], got_left[-1]],
            [((routes, hidden), bf16)],
            scalars=1,
        )
        return out

    operands = (right_first, left_first, lhs, forward, local, up_rows, panel, base_rows, from_left, from_right, scales)
    branch = jnp.clip((longest.astype(i32) + CHUNK - 1) // CHUNK - LEAST_CHUNKS, 0, most - LEAST_CHUNKS)
    out = lax.switch(branch, [functools.partial(flow, c) for c in range(LEAST_CHUNKS, most + 1)], operands)
    return out.reshape(2, steps, rows, hidden).transpose(1, 2, 0, 3)


def on_device(states, base, route_panels, down, up, magnitude):
    count = lax.axis_size("dp")
    me = lax.axis_index("dp")
    group = lax.axis_index("groups")
    steps, rows, width = states.shape
    hidden = base.shape[-1]
    panels, _, rank, _ = down.shape
    routes = 2 * steps * rows
    cap = max(2, (5 * rows + count - 1) // count)
    slots = -(-steps * cap // ROW_TILE) * ROW_TILE
    bf16, f32, i32 = jnp.bfloat16, jnp.float32, jnp.int32

    def turn(x, shift):
        return lax.ppermute(x, "dp", [(i, (i + shift) % count) for i in range(count)])

    pairs = route_panels.reshape(steps * rows, 2)
    numbers = jnp.concatenate([pairs // panels, pairs % panels], axis=1).astype(bf16)
    sent = jnp.concatenate(
        [states.reshape(steps * rows, width), jnp.pad(numbers, ((0, 0), (0, LANES - 4)))], axis=1
    )
    seen = [sent] + [turn(sent, s) for s in range(1, count)]

    if (count, lax.axis_size("expert"), lax.axis_size("pair")) == (4, 2, 2):
        return relayed(seen, turn, magnitude, base, down, up)

    half = lax.dynamic_index_in_dim(magnitude, group, axis=1, keepdims=False)
    mine = jnp.concatenate([half] + [turn(half, s) for s in range(1, count)], axis=0)
    other = lax.ppermute(mine, "groups", [(0, 1), (1, 0)])

    vmem = pl.BlockSpec(memory_space=pltpu.VMEM)
    smem = pl.BlockSpec(memory_space=pltpu.SMEM)
    params = pltpu.CompilerParams(vmem_limit_bytes=VMEM_LIMIT)
    part, info = pl.pallas_call(
        functools.partial(low_kernel, count, steps, rows, cap, slots),
        out_shape=(
            jax.ShapeDtypeStruct((2 * rank, count * routes), f32),
            jax.ShapeDtypeStruct((8, count * routes), f32),
        ),
        in_specs=[smem] + [vmem] * (1 + count),
        out_specs=(vmem, vmem),
        compiler_params=params,
    )(me.reshape(1).astype(i32), down, *seen)

    expert, pair = lax.axis_size("expert"), lax.axis_size("pair")
    lows = [part]
    if (expert, pair) == (2, 2):
        for mask in (1, 2, 3):
            lows.append(lax.ppermute(part, ("expert", "pair"), [(i, i ^ mask) for i in range(4)]))
    else:
        total = lax.psum(part, ("expert", "pair"))
        lows = [total] + [jnp.zeros_like(total)] * 3

    tile = min(1024, hidden)
    col_tiles = hidden // tile
    whole = lambda shape: pl.BlockSpec(shape, lambda p, n: (0,) * len(shape))
    deltas = pl.pallas_call(
        functools.partial(delta_kernel, count, slots),
        out_shape=[jax.ShapeDtypeStruct((slots, 2 * hidden), bf16)] * count,
        grid=(2, col_tiles),
        in_specs=[whole(info.shape)]
        + [whole(part.shape)] * 4
        + [pl.BlockSpec((panels, None, rank, tile), lambda p, n: (0, p, 0, n))],
        out_specs=[pl.BlockSpec((slots, tile), lambda p, n: (0, p * col_tiles + n))] * count,
        scratch_shapes=[pltpu.VMEM((2, count * slots, panels * rank), bf16)],
        compiler_params=params,
    )(info, *lows, up)
    got = [deltas[0]] + [turn(deltas[s], count - s) for s in range(1, count)]

    ordered = route_panels.transpose(2, 0, 1).reshape(2, steps, rows)
    owner, within = ordered // panels, ordered % panels
    by_step = owner.transpose(1, 0, 2).reshape(steps, 2 * rows)
    earlier = jnp.tril(jnp.ones((2 * rows, 2 * rows), jnp.bool_), -1)
    rank_of = jnp.sum((by_step[:, :, None] == by_step[:, None, :]) & earlier[None], axis=2, dtype=i32)
    slot = rank_of + jnp.arange(steps, dtype=i32)[:, None] * cap
    slot = slot.reshape(steps, 2, rows).transpose(1, 0, 2).reshape(routes)
    owner, within = owner.reshape(routes), within.reshape(routes)
    ahead = (owner - me) % count
    behind = (me - owner) % count
    pick = (jnp.arange(count * slots, dtype=i32)[None, :] == (ahead * slots + slot)[:, None]).astype(bf16)
    panel = (jnp.arange(count * panels, dtype=i32)[None, :] == (behind * panels + within)[:, None]).astype(bf16)
    base_rows = base.transpose(3, 2, 0, 1, 4).reshape(2, routes, hidden)

    tile = min(512, hidden)
    col_tiles = hidden // tile
    whole = lambda shape: pl.BlockSpec(shape, lambda n: (0,) * len(shape))
    col = lambda depth, p: pl.BlockSpec((depth, tile), lambda n, p=p: (0, p * col_tiles + n))
    out = pl.pallas_call(
        functools.partial(gate_kernel, count),
        out_shape=jax.ShapeDtypeStruct((routes, hidden), bf16),
        grid=(col_tiles,),
        in_specs=[smem, whole(pick.shape), whole(panel.shape)]
        + [pl.BlockSpec((2, routes, tile), lambda n: (0, 0, n))]
        + [col(count * panels, 0)] * 2
        + [col(slots, 0)] * count
        + [col(slots, 1)] * count,
        out_specs=col(routes, 0),
        compiler_params=params,
    )(group.reshape(1).astype(i32), pick, panel, base_rows, mine, other, *got, *got)
    return out.reshape(2, steps, rows, hidden).transpose(1, 2, 0, 3)


def solution(mesh):
    return jax.shard_map(
        on_device,
        mesh=mesh,
        in_specs=(
            P(None, ("groups", "dp"), ("expert", "pair")),
            P(None, ("groups", "dp"), None, None, ("expert", "pair")),
            P(None, ("groups", "dp"), None),
            P("dp", None, None, ("expert", "pair")),
            P("dp", None, None, ("expert", "pair")),
            P("dp", None, ("expert", "pair")),
        ),
        out_specs=P(None, ("groups", "dp"), None, ("expert", "pair")),
        check_vma=False,
    )
```

```python
import functools

import jax
import jax.numpy as jnp
from jax import lax
from jax.experimental import pallas as pl
from jax.experimental.pallas import tpu as pltpu
from jax.sharding import PartitionSpec as P

LANES = 128
ROW_TILE = 16
VMEM_LIMIT = 20 * 1024 * 1024


def nt_dot(a, b):
    return lax.dot_general(a, b, (((1,), (1,)), ((), ())), preferred_element_type=jnp.float32)


def earlier_in_step(steps, rows):
    routes = 2 * steps * rows
    first = lax.broadcasted_iota(jnp.int32, (routes, routes), 0)
    second = lax.broadcasted_iota(jnp.int32, (routes, routes), 1)
    same = (first // rows) % steps == (second // rows) % steps
    return jnp.where(same & (first < second), 1.0, 0.0).astype(jnp.bfloat16)


def low_kernel(count, steps, rows, cap, slots, me_ref, down_ref, *refs):
    state_refs, (part_ref, info_ref) = refs[:count], refs[count:]
    panels, _, rank, width = down_ref.shape
    routes = 2 * steps * rows
    me = me_ref[0].astype(jnp.float32)
    down = down_ref[...].reshape(panels * 2 * rank, width)
    pick = jnp.where(
        lax.broadcasted_iota(jnp.int32, (8, LANES), 0) == lax.broadcasted_iota(jnp.int32, (8, LANES), 1), 1.0, 0.0
    ).astype(jnp.bfloat16)
    before = earlier_in_step(steps, rows)
    lane = lax.broadcasted_iota(jnp.int32, (1, routes), 1)
    step_of = ((lane // rows) % steps).astype(jnp.float32)
    panel_of = (lax.broadcasted_iota(jnp.int32, (panels * 2 * rank, routes), 0) // (2 * rank)).astype(jnp.float32)
    for s in range(count):
        one = state_refs[s][...]
        both = jnp.concatenate([one, one], axis=0)
        numbers = nt_dot(pick, both[:, width:])
        owner = jnp.where(lane < routes // 2, numbers[0:1], numbers[1:2])
        within = jnp.where(lane < routes // 2, numbers[2:3], numbers[3:4])
        mine = owner == me
        rank_of = jnp.dot(
            jnp.broadcast_to(jnp.where(mine, 1.0, 0.0), (8, routes)).astype(jnp.bfloat16),
            before,
            preferred_element_type=jnp.float32,
        )[0:1]
        slot = jnp.where(mine, step_of * cap + rank_of, -1.0)
        held = jnp.where(mine, within, -1.0)
        cols = pl.ds(s * routes, routes)
        info_ref[:, cols] = jnp.concatenate([slot, held, jnp.zeros((6, routes), jnp.float32)], axis=0)
        low = nt_dot(down, both[:, :width])
        low = jnp.where(panel_of == held, low, 0.0)
        part_ref[:, cols] = jnp.sum(low.reshape(panels, 2 * rank, routes), axis=0)


def delta_kernel(count, slots, info_ref, own_ref, core_ref, far_ref, diag_ref, up_ref, *refs):
    out_refs, (lhs_ref,) = refs[:count], refs[count:]
    panels, rank, tile = up_ref.shape
    routes = info_ref.shape[1] // count

    @pl.when((pl.program_id(0) == 0) & (pl.program_id(1) == 0))
    def _():
        low = (own_ref[...] + core_ref[...]) + (far_ref[...] + diag_ref[...])
        low = low.astype(jnp.bfloat16).astype(jnp.float32)
        panel_of = (lax.broadcasted_iota(jnp.int32, (panels * rank, routes), 0) // rank).astype(jnp.float32)
        slot_of = lax.broadcasted_iota(jnp.int32, (slots, routes), 0).astype(jnp.float32)
        for s in range(count):
            cols = slice(s * routes, (s + 1) * routes)
            slot, held = info_ref[0:1, cols], info_ref[1:2, cols]
            place = jnp.where(slot_of == slot, 1.0, 0.0).astype(jnp.bfloat16)
            for p in range(2):
                wide = jnp.concatenate([low[p * rank : (p + 1) * rank, cols]] * panels, axis=0)
                wide = jnp.where(panel_of == held, wide, 0.0).astype(jnp.bfloat16)
                lhs_ref[p, s * slots : (s + 1) * slots, :] = nt_dot(place, wide).astype(jnp.bfloat16)

    p = pl.program_id(0)
    up = up_ref[...].reshape(panels * rank, tile)
    delta = jnp.dot(lhs_ref[p], up, preferred_element_type=jnp.float32).astype(jnp.bfloat16)
    for s in range(count):
        out_refs[s][...] = delta[s * slots : (s + 1) * slots]


def gate_kernel(count, group_ref, pick_ref, panel_ref, base_ref, mine_ref, other_ref, *refs):
    blocks, out_ref = refs[: 2 * count], refs[2 * count]
    slots = blocks[0].shape[0]
    group = group_ref[0]
    adapted = []
    for p in range(2):
        delta = None
        for s in range(count):
            part = jnp.dot(
                pick_ref[:, s * slots : (s + 1) * slots],
                blocks[p * count + s][...],
                preferred_element_type=jnp.float32,
            )
            delta = part if delta is None else delta + part
        scales = jnp.where(group == p, mine_ref[...], other_ref[...])
        scale = jnp.dot(panel_ref[...], scales, preferred_element_type=jnp.float32)
        adapted.append(scale * (base_ref[p].astype(jnp.float32) + delta))
    gate, value = adapted
    out_ref[...] = (gate / (1.0 + jnp.exp(-gate)) * value).astype(out_ref.dtype)


CHUNK = 32
LAG = 2
LEAST_CHUNKS = 5


def right_layout(n):
    gap = float(LAG * CHUNK)
    zero = jnp.zeros_like(n[0][0])
    place = {}

    def put(link, j, d, first, split=None, second=None):
        place[link, j, d] = (first, split, second)

    put(0, 0, 3, zero)
    put(0, 0, 2, n[0][3])
    put(0, 0, 1, n[0][3] + n[0][2])
    end = n[0][3] + n[0][2] + n[0][1]
    early = jnp.maximum(jnp.minimum(n[1][2], gap - n[1][3]), 0.0)
    far = jnp.maximum(n[1][3], gap)
    late = far + n[0][3] + n[1][2] - early
    put(1, 1, 3, zero)
    put(1, 0, 3, far)
    put(1, 1, 2, n[1][3], early, far + n[0][3] - early)
    put(1, 0, 2, late)
    end = jnp.maximum(end, late + n[0][2])
    one = jnp.maximum(n[2][3], gap)
    two = jnp.maximum(one + n[1][3], far + gap)
    put(2, 2, 3, zero)
    put(2, 1, 3, one)
    put(2, 0, 3, two)
    return place, jnp.maximum(end, two + n[0][3])


def relay_low_kernel(steps, rows, me_ref, down_ref, *refs):
    count = 4
    state_refs, (part_ref, info_ref) = refs[:count], refs[count:]
    panels, _, rank, width = down_ref.shape
    routes = 2 * steps * rows
    me = me_ref[0]
    down = down_ref[...].reshape(panels * 2 * rank, width)
    pick = jnp.where(
        lax.broadcasted_iota(jnp.int32, (8, LANES), 0) == lax.broadcasted_iota(jnp.int32, (8, LANES), 1), 1.0, 0.0
    ).astype(jnp.bfloat16)
    before = jnp.where(
        lax.broadcasted_iota(jnp.int32, (routes, routes), 0) < lax.broadcasted_iota(jnp.int32, (routes, routes), 1),
        1.0,
        0.0,
    ).astype(jnp.bfloat16)
    lane = lax.broadcasted_iota(jnp.int32, (1, routes), 1)
    owners = lax.broadcasted_iota(jnp.int32, (8, routes), 0).astype(jnp.float32)
    panel_of = (lax.broadcasted_iota(jnp.int32, (panels * 2 * rank, routes), 0) // (2 * rank)).astype(jnp.float32)
    owner, within, order, tally = [], [], [], []
    info_ref[...] = jnp.full(info_ref.shape, -1.0, jnp.float32)
    for s in range(count):
        one = state_refs[s][...]
        both = jnp.concatenate([one, one], axis=0)
        numbers = nt_dot(pick, both[:, width:])
        owner.append(jnp.where(lane < routes // 2, numbers[0:1], numbers[1:2]))
        within.append(jnp.where(lane < routes // 2, numbers[2:3], numbers[3:4]))
        hits = jnp.where(owners == owner[s], 1.0, 0.0)
        ahead = jnp.dot(hits.astype(jnp.bfloat16), before, preferred_element_type=jnp.float32)
        order.append(jnp.sum(ahead * hits, axis=0, keepdims=True))
        tally.append(jnp.sum(hits, axis=1, keepdims=True))
        cols = slice(s * routes, (s + 1) * routes)
        held = jnp.where(owner[s] == me.astype(jnp.float32), within[s], -1.0)
        info_ref[0:1, cols] = held
        low = nt_dot(down, both[:, :width])
        low = jnp.where(panel_of == held, low, 0.0)
        part_ref[:, cols] = jnp.sum(low.reshape(panels, 2 * rank, routes), axis=0)
    info_ref[9:10, 0:routes] = owner[0]
    info_ref[10:11, 0:routes] = within[0]

    def position(place, link, d, s, turned, owners_from, owners_to):
        found = jnp.full((1, routes), -1.0, jnp.float32)
        for j in range(owners_from, owners_to):
            first, split, second = place[link, j, d]
            at = first + order[s]
            if split is not None:
                at = jnp.where(order[s] < split, at, second + order[s])
            found = jnp.where(owner[s] == float(3 - j if turned else j), at, found)
        return found

    for case in range(count):

        @pl.when(me == case)
        def _():
            longest = None
            for turned in (False, True):
                node = 3 - case if turned else case
                n = [[None] * count for _ in range(count)]
                for j in range(count):
                    for d in range(count):
                        s = (case - d) % count
                        if turned:
                            n[3 - j][3 - d] = tally[s][j : j + 1]
                        else:
                            n[j][d] = tally[s][j : j + 1]
                place, end = right_layout(n)
                longest = end if longest is None else jnp.maximum(longest, end)
                row = 4 if turned else 1
                for d in range(node + 1, count):
                    s = (case - (3 - d if turned else d)) % count
                    cols = slice(s * routes, (s + 1) * routes)
                    info_ref[row : row + 1, cols] = position(place, node, d, s, turned, node, node + 1)
                    if node > 0:
                        info_ref[row + 1 : row + 2, cols] = position(place, node, d, s, turned, 0, node)
                        info_ref[row + 2 : row + 3, cols] = position(place, node - 1, d, s, turned, 0, node)
                if node > 0:
                    arrive = 8 if turned else 7
                    info_ref[arrive : arrive + 1, 0:routes] = position(place, node - 1, node, 0, turned, 0, node)
            info_ref[11:12, 0:routes] = jnp.broadcast_to(longest, (1, routes))


def summed_low(own_ref, core_ref, far_ref, diag_ref):
    low = (own_ref[...] + core_ref[...]) + (far_ref[...] + diag_ref[...])
    return low.astype(jnp.bfloat16).astype(jnp.float32)


def spread_low(low, info_ref, panels, p):
    rank = low.shape[0] // 2
    held = info_ref[0:1, :]
    panel_of = lax.broadcasted_iota(jnp.int32, (panels * rank, held.shape[1]), 0) // rank
    wide = jnp.concatenate([low[p * rank : (p + 1) * rank]] * panels, axis=0)
    return jnp.where(panel_of.astype(jnp.float32) == held, wide, 0.0).astype(jnp.bfloat16)


def placed(info_ref, row, slots):
    at = info_ref[row : row + 1, :]
    slot_of = lax.broadcasted_iota(jnp.int32, (slots, at.shape[1]), 0).astype(jnp.float32)
    return jnp.where(slot_of == at, 1.0, 0.0).astype(jnp.bfloat16)


def column_tiles(up_ref, body):
    hidden = up_ref.shape[2]
    tile = min(1024, hidden)
    each = hidden // tile

    @pl.loop(0, 2 * each)
    def _(i):
        p = i // each
        body(p, pl.multiple_of((i - p * each) * tile, tile), pl.multiple_of(i * tile, tile), tile)


def relay_first_kernel(panels, info_ref, own_ref, core_ref, far_ref, diag_ref, up_ref, *refs):
    chunk_refs, lhs_ref = refs[:4], refs[4]
    low = summed_low(own_ref, core_ref, far_ref, diag_ref)
    own = jnp.concatenate([placed(info_ref, 1, 2 * CHUNK), placed(info_ref, 4, 2 * CHUNK)], axis=0)
    for p in range(2):
        lhs_ref[p] = nt_dot(own, spread_low(low, info_ref, panels, p)).astype(jnp.bfloat16)

    def body(p, col, at, tile):
        delta = jnp.dot(lhs_ref[p], up_ref[p, :, pl.ds(col, tile)], preferred_element_type=jnp.float32)
        delta = delta.astype(jnp.bfloat16)
        for i in range(4):
            chunk_refs[i][:, pl.ds(at, tile)] = delta[i * CHUNK : (i + 1) * CHUNK]

    column_tiles(up_ref, body)


def relay_rows_kernel(panels, info_ref, own_ref, core_ref, far_ref, diag_ref, lhs_ref, forward_ref, local_ref):
    limit = lhs_ref.shape[2]
    routes = local_ref.shape[1]
    low = summed_low(own_ref, core_ref, far_ref, diag_ref)
    own = [placed(info_ref, 1, limit), placed(info_ref, 4, limit)]
    same = lax.broadcasted_iota(jnp.int32, (routes, routes), 0) == lax.broadcasted_iota(jnp.int32, (routes, routes), 1)
    same = jnp.where(same, 1.0, 0.0).astype(jnp.bfloat16)
    for p in range(2):
        wide = spread_low(low, info_ref, panels, p)
        for way in range(2):
            lhs_ref[p, way] = nt_dot(own[way], wide).astype(jnp.bfloat16)
        local_ref[p] = nt_dot(same, wide[:, :routes]).astype(jnp.bfloat16)
    for way in range(2):
        forward_ref[way] = nt_dot(
            placed(info_ref, 3 * way + 2, limit), placed(info_ref, 3 * way + 3, limit)
        ).astype(jnp.bfloat16)


def relay_chunk_kernel(index, lhs_ref, forward_ref, up_ref, *refs):
    known = index + 1 - LAG
    came, (right_ref, left_ref) = refs[: 2 * known], refs[2 * known :]
    here = slice(index * CHUNK, (index + 1) * CHUNK)

    def body(p, col, at, tile):
        lhs = jnp.concatenate([lhs_ref[p, 0, here, :], lhs_ref[p, 1, here, :]], axis=0)
        delta = jnp.dot(lhs, up_ref[p, :, pl.ds(col, tile)], preferred_element_type=jnp.float32)
        for way, out_ref in ((0, right_ref), (1, left_ref)):
            rows = jnp.concatenate([came[way * known + i][:, pl.ds(at, tile)] for i in range(known)], axis=0)
            passed = jnp.dot(forward_ref[way, here, : known * CHUNK], rows, preferred_element_type=jnp.float32)
            out_ref[:, pl.ds(at, tile)] = (delta[way * CHUNK : (way + 1) * CHUNK] + passed).astype(out_ref.dtype)

    column_tiles(up_ref, body)


def relay_pick_kernel(pick_ref, local_ref, up_ref, *refs):
    came, out_ref = refs[:-1], refs[-1]

    def body(p, col, at, tile):
        delta = jnp.dot(local_ref[p], up_ref[p, :, pl.ds(col, tile)], preferred_element_type=jnp.float32)
        rows = jnp.concatenate([block[:, pl.ds(at, tile)] for block in came], axis=0)
        picked = jnp.dot(pick_ref[...], rows, preferred_element_type=jnp.float32)
        delta = delta.astype(jnp.bfloat16).astype(jnp.float32)
        out_ref[:, pl.ds(at, tile)] = (delta + picked).astype(out_ref.dtype)

    column_tiles(up_ref, body)


def relay_gate_kernel(pick_ref, panel_ref, base_ref, scale_ref, early_ref, right_ref, left_ref, out_ref):
    hidden = out_ref.shape[1]
    tile = min(512, hidden)

    @pl.loop(0, hidden // tile)
    def _(i):
        adapted = []
        for p in range(2):
            col = pl.ds(pl.multiple_of(i * tile, tile), tile)
            at = pl.ds(pl.multiple_of(p * hidden + i * tile, tile), tile)
            rows = jnp.concatenate([right_ref[:, at], left_ref[:, at]], axis=0)
            delta = early_ref[:, at].astype(jnp.float32) + jnp.dot(
                pick_ref[...], rows, preferred_element_type=jnp.float32
            )
            scale = jnp.dot(panel_ref[...], scale_ref[p, :, col], preferred_element_type=jnp.float32)
            adapted.append(scale * (base_ref[p, :, col].astype(jnp.float32) + delta))
        gate, value = adapted
        out_ref[:, col] = (gate / (1.0 + jnp.exp(-gate)) * value).astype(out_ref.dtype)


def relayed(seen, magnitude, base, down, up):
    count = 4
    me, group = lax.axis_index("dp"), lax.axis_index("groups")
    steps, rows, hidden = base.shape[0], base.shape[1], base.shape[-1]
    panels, _, rank, _ = down.shape
    routes = 2 * steps * rows
    cap = max(2, (5 * rows + count - 1) // count)
    gap = LAG * CHUNK
    limit = max(
        3 * steps * cap,
        2 * routes,
        gap + 2 * steps * cap,
        gap + routes,
        2 * gap + steps * cap,
    )
    limit = -(-limit // CHUNK) * CHUNK
    most = limit // CHUNK
    bf16, f32, i32 = jnp.bfloat16, jnp.float32, jnp.int32
    vmem = pl.BlockSpec(memory_space=pltpu.VMEM)
    smem = pl.BlockSpec(memory_space=pltpu.SMEM)

    def kernel(body, inputs, outputs, flops=0, scalars=0, scratch=()):
        return pl.pallas_call(
            body,
            out_shape=[jax.ShapeDtypeStruct(shape, dtype) for shape, dtype in outputs],
            in_specs=[smem] * scalars + [vmem] * (len(inputs) - scalars),
            out_specs=[vmem] * len(outputs),
            scratch_shapes=list(scratch),
            compiler_params=pltpu.CompilerParams(vmem_limit_bytes=VMEM_LIMIT),
            cost_estimate=pl.CostEstimate(flops=flops, bytes_accessed=8 << 20, transcendentals=0),
        )(*inputs)

    up_rows = up.transpose(1, 0, 2, 3).reshape(2, panels * rank, hidden)
    base_rows = base.transpose(3, 2, 0, 1, 4).reshape(2, routes, hidden)
    half = lax.dynamic_index_in_dim(magnitude, group, axis=1, keepdims=False)
    up_rows, base_rows, half, *seen = lax.optimization_barrier((up_rows, base_rows, half, *seen))

    part, info = kernel(
        functools.partial(relay_low_kernel, steps, rows),
        [me.reshape(1).astype(i32), down, *seen],
        [((2 * rank, count * routes), f32), ((16, count * routes), f32)],
        scalars=1,
    )
    lows = [part]
    for mask in (1, 2, 3):
        lows.append(lax.ppermute(part, ("expert", "pair"), [(i, i ^ mask) for i in range(4)]))
    longest = info[8:16, 0:LANES]
    longest = jnp.maximum(longest, lax.ppermute(longest, "groups", [(0, 1), (1, 0)]))[3, 0]

    scales = lax.all_gather(half, ("groups", "dp")).reshape(2, count * panels, hidden)

    chunk = ((CHUNK, 2 * hidden), bf16)
    first = kernel(
        functools.partial(relay_first_kernel, panels),
        [info, *lows, up_rows],
        [chunk] * 4,
        scratch=[pltpu.VMEM((2, 4 * CHUNK, panels * rank), bf16)],
    )
    right_first, left_first = first[0:2], first[2:4]
    lhs, forward, local = kernel(
        functools.partial(relay_rows_kernel, panels),
        [info, *lows],
        [((2, 2, limit, panels * rank), bf16), ((2, limit, limit), bf16), ((2, routes, panels * rank), bf16)],
    )

    owner, within = info[9, :routes].astype(i32), info[10, :routes].astype(i32)
    panel = (jnp.arange(count * panels, dtype=i32)[None, :] == (owner * panels + within)[:, None]).astype(bf16)
    slot = jnp.arange(limit, dtype=f32)[None, :]
    from_left = (slot == info[7, :routes, None]).astype(bf16)
    from_right = (slot == info[8, :routes, None]).astype(bf16)

    def flow(chunks, operands):
        right_first, left_first, lhs, forward, local, up_rows, from_left, from_right = operands
        got_right, got_left = [], []
        for k in range(chunks):
            if k < LAG:
                right, left = right_first[k], left_first[k]
            else:
                known = k + 1 - LAG
                right, left = kernel(
                    functools.partial(relay_chunk_kernel, k),
                    [lhs, forward, up_rows, *got_right[:known], *got_left[:known]],
                    [chunk] * 2,
                    flops=2 * 2 * CHUNK * 512 * 2 * hidden,
                )
            got_right.append(lax.ppermute(right, "dp", [(i, i + 1) for i in range(count - 1)]))
            got_left.append(lax.ppermute(left, "dp", [(i + 1, i) for i in range(count - 1)]))
        last = (chunks - 1) * CHUNK
        early = jnp.concatenate([from_left[:, :last], from_right[:, :last]], axis=1)
        late = jnp.concatenate([from_left[:, last : last + CHUNK], from_right[:, last : last + CHUNK]], axis=1)
        [picked] = kernel(
            relay_pick_kernel,
            [early, local, up_rows, *got_right[:-1], *got_left[:-1]],
            [((routes, 2 * hidden), bf16)],
            flops=2 * routes * 512 * 2 * hidden,
        )
        return picked, got_right[-1], got_left[-1], late

    operands = (right_first, left_first, lhs, forward, local, up_rows, from_left, from_right)
    branch = jnp.clip((longest.astype(i32) + CHUNK - 1) // CHUNK - LEAST_CHUNKS, 0, most - LEAST_CHUNKS)
    picked, right, left, late = lax.switch(
        branch, [functools.partial(flow, c) for c in range(LEAST_CHUNKS, most + 1)], operands
    )
    [out] = kernel(
        relay_gate_kernel, [late, panel, base_rows, scales, picked, right, left], [((routes, hidden), bf16)]
    )
    return out.reshape(2, steps, rows, hidden).transpose(1, 2, 0, 3)


def on_device(states, base, route_panels, down, up, magnitude):
    count = lax.axis_size("dp")
    me = lax.axis_index("dp")
    group = lax.axis_index("groups")
    steps, rows, width = states.shape
    hidden = base.shape[-1]
    panels, _, rank, _ = down.shape
    routes = 2 * steps * rows
    cap = max(2, (5 * rows + count - 1) // count)
    slots = -(-steps * cap // ROW_TILE) * ROW_TILE
    bf16, f32, i32 = jnp.bfloat16, jnp.float32, jnp.int32

    def turn(x, shift):
        return lax.ppermute(x, "dp", [(i, (i + shift) % count) for i in range(count)])

    pairs = route_panels.reshape(steps * rows, 2)
    numbers = jnp.concatenate([pairs // panels, pairs % panels], axis=1).astype(bf16)
    sent = jnp.concatenate(
        [states.reshape(steps * rows, width), jnp.pad(numbers, ((0, 0), (0, LANES - 4)))], axis=1
    )
    seen = [sent] + [turn(sent, s) for s in range(1, count)]

    if (count, lax.axis_size("expert"), lax.axis_size("pair")) == (4, 2, 2):
        return relayed(seen, magnitude, base, down, up)

    half = lax.dynamic_index_in_dim(magnitude, group, axis=1, keepdims=False)
    mine = jnp.concatenate([half] + [turn(half, s) for s in range(1, count)], axis=0)
    other = lax.ppermute(mine, "groups", [(0, 1), (1, 0)])

    vmem = pl.BlockSpec(memory_space=pltpu.VMEM)
    smem = pl.BlockSpec(memory_space=pltpu.SMEM)
    params = pltpu.CompilerParams(vmem_limit_bytes=VMEM_LIMIT)
    part, info = pl.pallas_call(
        functools.partial(low_kernel, count, steps, rows, cap, slots),
        out_shape=(
            jax.ShapeDtypeStruct((2 * rank, count * routes), f32),
            jax.ShapeDtypeStruct((8, count * routes), f32),
        ),
        in_specs=[smem] + [vmem] * (1 + count),
        out_specs=(vmem, vmem),
        compiler_params=params,
    )(me.reshape(1).astype(i32), down, *seen)

    expert, pair = lax.axis_size("expert"), lax.axis_size("pair")
    lows = [part]
    if (expert, pair) == (2, 2):
        for mask in (1, 2, 3):
            lows.append(lax.ppermute(part, ("expert", "pair"), [(i, i ^ mask) for i in range(4)]))
    else:
        total = lax.psum(part, ("expert", "pair"))
        lows = [total] + [jnp.zeros_like(total)] * 3

    tile = min(1024, hidden)
    col_tiles = hidden // tile
    whole = lambda shape: pl.BlockSpec(shape, lambda p, n: (0,) * len(shape))
    deltas = pl.pallas_call(
        functools.partial(delta_kernel, count, slots),
        out_shape=[jax.ShapeDtypeStruct((slots, 2 * hidden), bf16)] * count,
        grid=(2, col_tiles),
        in_specs=[whole(info.shape)]
        + [whole(part.shape)] * 4
        + [pl.BlockSpec((panels, None, rank, tile), lambda p, n: (0, p, 0, n))],
        out_specs=[pl.BlockSpec((slots, tile), lambda p, n: (0, p * col_tiles + n))] * count,
        scratch_shapes=[pltpu.VMEM((2, count * slots, panels * rank), bf16)],
        compiler_params=params,
    )(info, *lows, up)
    got = [deltas[0]] + [turn(deltas[s], count - s) for s in range(1, count)]

    ordered = route_panels.transpose(2, 0, 1).reshape(2, steps, rows)
    owner, within = ordered // panels, ordered % panels
    by_step = owner.transpose(1, 0, 2).reshape(steps, 2 * rows)
    earlier = jnp.tril(jnp.ones((2 * rows, 2 * rows), jnp.bool_), -1)
    rank_of = jnp.sum((by_step[:, :, None] == by_step[:, None, :]) & earlier[None], axis=2, dtype=i32)
    slot = rank_of + jnp.arange(steps, dtype=i32)[:, None] * cap
    slot = slot.reshape(steps, 2, rows).transpose(1, 0, 2).reshape(routes)
    owner, within = owner.reshape(routes), within.reshape(routes)
    ahead = (owner - me) % count
    behind = (me - owner) % count
    pick = (jnp.arange(count * slots, dtype=i32)[None, :] == (ahead * slots + slot)[:, None]).astype(bf16)
    panel = (jnp.arange(count * panels, dtype=i32)[None, :] == (behind * panels + within)[:, None]).astype(bf16)
    base_rows = base.transpose(3, 2, 0, 1, 4).reshape(2, routes, hidden)

    tile = min(512, hidden)
    col_tiles = hidden // tile
    whole = lambda shape: pl.BlockSpec(shape, lambda n: (0,) * len(shape))
    col = lambda depth, p: pl.BlockSpec((depth, tile), lambda n, p=p: (0, p * col_tiles + n))
    out = pl.pallas_call(
        functools.partial(gate_kernel, count),
        out_shape=jax.ShapeDtypeStruct((routes, hidden), bf16),
        grid=(col_tiles,),
        in_specs=[smem, whole(pick.shape), whole(panel.shape)]
        + [pl.BlockSpec((2, routes, tile), lambda n: (0, 0, n))]
        + [col(count * panels, 0)] * 2
        + [col(slots, 0)] * count
        + [col(slots, 1)] * count,
        out_specs=col(routes, 0),
        compiler_params=params,
    )(group.reshape(1).astype(i32), pick, panel, base_rows, mine, other, *got, *got)
    return out.reshape(2, steps, rows, hidden).transpose(1, 2, 0, 3)


def solution(mesh):
    return jax.shard_map(
        on_device,
        mesh=mesh,
        in_specs=(
            P(None, ("groups", "dp"), ("expert", "pair")),
            P(None, ("groups", "dp"), None, None, ("expert", "pair")),
            P(None, ("groups", "dp"), None),
            P("dp", None, None, ("expert", "pair")),
            P("dp", None, None, ("expert", "pair")),
            P("dp", None, ("expert", "pair")),
        ),
        out_specs=P(None, ("groups", "dp"), None, ("expert", "pair")),
        check_vma=False,
    )
```

```python
import functools

import jax
import jax.numpy as jnp
from jax import lax
from jax.experimental import pallas as pl
from jax.experimental.pallas import tpu as pltpu
from jax.sharding import PartitionSpec as P

LANES = 128
ROW_TILE = 16
VMEM_LIMIT = 10 * 1024 * 1024


def nt_dot(a, b):
    return lax.dot_general(a, b, (((1,), (1,)), ((), ())), preferred_element_type=jnp.float32)


def earlier_in_step(steps, rows):
    routes = 2 * steps * rows
    first = lax.broadcasted_iota(jnp.int32, (routes, routes), 0)
    second = lax.broadcasted_iota(jnp.int32, (routes, routes), 1)
    same = (first // rows) % steps == (second // rows) % steps
    return jnp.where(same & (first < second), 1.0, 0.0).astype(jnp.bfloat16)


def low_kernel(count, steps, rows, cap, slots, me_ref, down_ref, *refs):
    state_refs, (part_ref, info_ref) = refs[:count], refs[count:]
    panels, _, rank, width = down_ref.shape
    routes = 2 * steps * rows
    me = me_ref[0].astype(jnp.float32)
    down = down_ref[...].reshape(panels * 2 * rank, width)
    pick = jnp.where(
        lax.broadcasted_iota(jnp.int32, (8, LANES), 0) == lax.broadcasted_iota(jnp.int32, (8, LANES), 1), 1.0, 0.0
    ).astype(jnp.bfloat16)
    before = earlier_in_step(steps, rows)
    lane = lax.broadcasted_iota(jnp.int32, (1, routes), 1)
    step_of = ((lane // rows) % steps).astype(jnp.float32)
    panel_of = (lax.broadcasted_iota(jnp.int32, (panels * 2 * rank, routes), 0) // (2 * rank)).astype(jnp.float32)
    for s in range(count):
        one = state_refs[s][...]
        both = jnp.concatenate([one, one], axis=0)
        numbers = nt_dot(pick, both[:, width:])
        owner = jnp.where(lane < routes // 2, numbers[0:1], numbers[1:2])
        within = jnp.where(lane < routes // 2, numbers[2:3], numbers[3:4])
        mine = owner == me
        rank_of = jnp.dot(
            jnp.broadcast_to(jnp.where(mine, 1.0, 0.0), (8, routes)).astype(jnp.bfloat16),
            before,
            preferred_element_type=jnp.float32,
        )[0:1]
        slot = jnp.where(mine, step_of * cap + rank_of, -1.0)
        held = jnp.where(mine, within, -1.0)
        cols = pl.ds(s * routes, routes)
        info_ref[:, cols] = jnp.concatenate([slot, held, jnp.zeros((6, routes), jnp.float32)], axis=0)
        low = nt_dot(down, both[:, :width])
        low = jnp.where(panel_of == held, low, 0.0)
        part_ref[:, cols] = jnp.sum(low.reshape(panels, 2 * rank, routes), axis=0)


def delta_kernel(count, slots, info_ref, low_ref, up_ref, *refs):
    out_refs, (lhs_ref,) = refs[:count], refs[count:]
    panels, rank, tile = up_ref.shape
    routes = info_ref.shape[1] // count

    @pl.when((pl.program_id(0) == 0) & (pl.program_id(1) == 0))
    def _():
        low = low_ref[...].astype(jnp.bfloat16).astype(jnp.float32)
        panel_of = (lax.broadcasted_iota(jnp.int32, (panels * rank, routes), 0) // rank).astype(jnp.float32)
        slot_of = lax.broadcasted_iota(jnp.int32, (slots, routes), 0).astype(jnp.float32)
        for s in range(count):
            cols = slice(s * routes, (s + 1) * routes)
            slot, held = info_ref[0:1, cols], info_ref[1:2, cols]
            place = jnp.where(slot_of == slot, 1.0, 0.0).astype(jnp.bfloat16)
            for p in range(2):
                wide = jnp.concatenate([low[p * rank : (p + 1) * rank, cols]] * panels, axis=0)
                wide = jnp.where(panel_of == held, wide, 0.0).astype(jnp.bfloat16)
                lhs_ref[p, s * slots : (s + 1) * slots, :] = nt_dot(place, wide).astype(jnp.bfloat16)

    p = pl.program_id(0)
    up = up_ref[...].reshape(panels * rank, tile)
    delta = jnp.dot(lhs_ref[p], up, preferred_element_type=jnp.float32).astype(jnp.bfloat16)
    for s in range(count):
        out_refs[s][...] = delta[s * slots : (s + 1) * slots]


def gate_kernel(count, group_ref, pick_ref, panel_ref, base_ref, mine_ref, other_ref, *refs):
    blocks, out_ref = refs[: 2 * count], refs[2 * count]
    slots = blocks[0].shape[0]
    group = group_ref[0]
    adapted = []
    for p in range(2):
        delta = None
        for s in range(count):
            part = jnp.dot(
                pick_ref[:, s * slots : (s + 1) * slots],
                blocks[p * count + s][...],
                preferred_element_type=jnp.float32,
            )
            delta = part if delta is None else delta + part
        scales = jnp.where(group == p, mine_ref[...], other_ref[...])
        scale = jnp.dot(panel_ref[...], scales, preferred_element_type=jnp.float32)
        adapted.append(scale * (base_ref[p].astype(jnp.float32) + delta))
    gate, value = adapted
    out_ref[...] = (gate / (1.0 + jnp.exp(-gate)) * value).astype(out_ref.dtype)


CHUNK = 24
LAG = 2
GAP = LAG * CHUNK
ROW_STEP = 8
QUEUE_ROWS = (160, 176, 200)


def chunk_rows(total):
    return [(at, min(CHUNK, total - at)) for at in range(0, total, CHUNK)]


def right_layout(n):
    gap = float(GAP)
    zero = jnp.zeros_like(n[0][0])
    place = {}

    def put(link, j, d, first, split=None, second=None):
        place[link, j, d] = (first, split, second)

    put(0, 0, 3, zero)
    put(0, 0, 2, n[0][3])
    put(0, 0, 1, n[0][3] + n[0][2])
    end = n[0][3] + n[0][2] + n[0][1]
    early = jnp.maximum(jnp.minimum(n[1][2], gap - n[1][3]), 0.0)
    far = jnp.maximum(n[1][3], gap)
    late = far + n[0][3] + n[1][2] - early
    put(1, 1, 3, zero)
    put(1, 0, 3, far)
    put(1, 1, 2, n[1][3], early, far + n[0][3] - early)
    put(1, 0, 2, late)
    end = jnp.maximum(end, late + n[0][2])
    one = jnp.maximum(n[2][3], gap)
    two = jnp.maximum(one + n[1][3], far + gap)
    put(2, 2, 3, zero)
    put(2, 1, 3, one)
    put(2, 0, 3, two)
    return place, jnp.maximum(end, two + n[0][3])


def relay_plan_kernel(steps, rows, me_ref, *refs):
    count = 4
    route_refs, (info_ref, forward_ref) = refs[:count], refs[count:]
    routes = 2 * steps * rows
    limit = forward_ref.shape[1]
    me = me_ref[0]
    before = jnp.where(
        lax.broadcasted_iota(jnp.int32, (routes, routes), 0) < lax.broadcasted_iota(jnp.int32, (routes, routes), 1),
        1.0,
        0.0,
    ).astype(jnp.bfloat16)
    owners = lax.broadcasted_iota(jnp.int32, (8, routes), 0).astype(jnp.float32)
    owner, order, tally = [], [], []
    info_ref[...] = jnp.full(info_ref.shape, -1.0, jnp.float32)
    for s in range(count):
        numbers = route_refs[s][...].astype(jnp.float32)
        owner.append(numbers[0:1])
        hits = jnp.where(owners == owner[s], 1.0, 0.0)
        ahead = jnp.dot(hits.astype(jnp.bfloat16), before, preferred_element_type=jnp.float32)
        order.append(jnp.sum(ahead * hits, axis=0, keepdims=True))
        tally.append(jnp.sum(hits, axis=1, keepdims=True))
        cols = slice(s * routes, (s + 1) * routes)
        info_ref[0:1, cols] = jnp.where(owner[s] == me.astype(jnp.float32), numbers[1:2], -1.0)
        if s == 0:
            info_ref[9:11, cols] = numbers[0:2]

    def position(place, link, d, s, turned, owners_from, owners_to):
        found = jnp.full((1, routes), -1.0, jnp.float32)
        for j in range(owners_from, owners_to):
            first, split, second = place[link, j, d]
            at = first + order[s]
            if split is not None:
                at = jnp.where(order[s] < split, at, second + order[s])
            found = jnp.where(owner[s] == float(3 - j if turned else j), at, found)
        return found

    for case in range(count):

        @pl.when(me == case)
        def _():
            longest = None
            for turned in (False, True):
                node = 3 - case if turned else case
                n = [[None] * count for _ in range(count)]
                for j in range(count):
                    for d in range(count):
                        s = (case - d) % count
                        if turned:
                            n[3 - j][3 - d] = tally[s][j : j + 1]
                        else:
                            n[j][d] = tally[s][j : j + 1]
                place, end = right_layout(n)
                longest = end if longest is None else jnp.maximum(longest, end)
                row = 1 if turned == (case % 2 == 1) else 4
                for d in range(node + 1, count):
                    s = (case - (3 - d if turned else d)) % count
                    cols = slice(s * routes, (s + 1) * routes)
                    info_ref[row : row + 1, cols] = position(place, node, d, s, turned, node, node + 1)
                    if node > 0:
                        info_ref[row + 1 : row + 2, cols] = position(place, node, d, s, turned, 0, node)
                        info_ref[row + 2 : row + 3, cols] = position(place, node - 1, d, s, turned, 0, node)
                if node > 0:
                    arrive = 7 if turned == (case % 2 == 0) else 8
                    info_ref[arrive : arrive + 1, 0:routes] = position(place, node - 1, node, 0, turned, 0, node)
            info_ref[11:12, 0:routes] = jnp.broadcast_to(longest, (1, routes))

    shape = forward_ref.shape[1:]
    same_half = lax.broadcasted_iota(jnp.int32, shape, 0) % 2 == lax.broadcasted_iota(jnp.int32, shape, 1) % 2
    for way in range(2):
        passed = nt_dot(placed(info_ref, 3 * way + 2, shape[0]), placed(info_ref, 3 * way + 3, shape[0]))
        forward_ref[way] = jnp.where(same_half, passed, 0.0).astype(jnp.bfloat16)


def relay_load_kernel(down_ref, up_ref, down_out, up_out, sems):
    copies = [pltpu.make_async_copy(down_ref, down_out, sems.at[2])]
    copies += [pltpu.make_async_copy(up_ref.at[:, p], up_out.at[p], sems.at[p]) for p in range(2)]
    for copy in copies:
        copy.start()
    for copy in copies:
        copy.wait()


def relay_low_kernel(info_ref, down_ref, *refs):
    state_refs, part_ref = refs[:-1], refs[-1]
    panels, _, rank, width = down_ref.shape
    routes = info_ref.shape[1] // len(state_refs)
    down = down_ref[...].reshape(panels * 2 * rank, width)
    panel_of = (lax.broadcasted_iota(jnp.int32, (panels * 2 * rank, routes), 0) // (2 * rank)).astype(jnp.float32)
    for s, state_ref in enumerate(state_refs):
        one = state_ref[...]
        cols = slice(s * routes, (s + 1) * routes)
        low = nt_dot(down, jnp.concatenate([one, one], axis=0))
        low = jnp.where(panel_of == info_ref[0:1, cols], low, 0.0)
        part_ref[:, cols] = jnp.sum(low.reshape(panels, 2 * rank, routes), axis=0)


def summed_low(own_ref, far_ref):
    low = own_ref[...] + far_ref[...]
    return low.astype(jnp.bfloat16).astype(jnp.float32)


def spread_low(low, info_ref, panels):
    rank = low.shape[0] // 2
    held = info_ref[0:1, :]
    panel_of = lax.broadcasted_iota(jnp.int32, (panels * rank, held.shape[1]), 0) // rank
    here = panel_of.astype(jnp.float32) == held
    wide = [jnp.concatenate([low[p * rank : (p + 1) * rank]] * panels, axis=0) for p in range(2)]
    return jnp.concatenate([jnp.where(here, part, 0.0) for part in wide], axis=0).astype(jnp.bfloat16)


def placed(info_ref, row, half_rows):
    at = info_ref[row : row + 1, :]
    slot_of = lax.broadcasted_iota(jnp.int32, (half_rows, at.shape[1]), 0) // 2
    return jnp.where(slot_of.astype(jnp.float32) == at, 1.0, 0.0).astype(jnp.bfloat16)


def low_rows(place, wide):
    rows = nt_dot(place, wide)
    half_of = lax.broadcasted_iota(jnp.int32, rows.shape, 0) % 2
    own_half = half_of == lax.broadcasted_iota(jnp.int32, rows.shape, 1) // (rows.shape[1] // 2)
    return jnp.where(own_half, rows, 0.0).astype(jnp.bfloat16)


def column_tiles(hidden, body):
    tile = min(1024, hidden)

    @pl.loop(0, hidden // tile)
    def _(i):
        body(pl.ds(pl.multiple_of(i * tile, tile), tile))


def relay_first_kernel(panels, info_ref, own_ref, far_ref, up_ref, *refs):
    chunk_refs, lhs_ref = refs[:-1], refs[-1]
    wide = spread_low(summed_low(own_ref, far_ref), info_ref, panels)
    own = jnp.concatenate([placed(info_ref, 1, 2 * GAP), placed(info_ref, 4, 2 * GAP)], axis=0)
    lhs_ref[...] = low_rows(own, wide)

    def body(cols):
        delta = jnp.dot(lhs_ref[...], up_ref[:, cols], preferred_element_type=jnp.float32).astype(jnp.bfloat16)
        for i, chunk_ref in enumerate(chunk_refs):
            chunk_ref[:, cols] = delta[2 * i * CHUNK : 2 * (i + 1) * CHUNK]

    column_tiles(up_ref.shape[1], body)


def relay_rows_kernel(panels, info_ref, own_ref, far_ref, lhs_ref, local_ref):
    routes = local_ref.shape[1]
    wide = spread_low(summed_low(own_ref, far_ref), info_ref, panels)
    for way in range(2):
        lhs_ref[way] = low_rows(placed(info_ref, 3 * way + 1, lhs_ref.shape[1]), wide)
    same = lax.broadcasted_iota(jnp.int32, (routes, routes), 0) == lax.broadcasted_iota(jnp.int32, (routes, routes), 1)
    same = jnp.where(same, 1.0, 0.0).astype(jnp.bfloat16)
    depth = wide.shape[0] // 2
    for p in range(2):
        local_ref[p] = nt_dot(same, wide[p * depth : (p + 1) * depth, :routes]).astype(jnp.bfloat16)


def relay_final_kernel(outer_ref, middle_ref, out_ref):
    rows, room = outer_ref.shape[0], out_ref.shape[0] // 2
    for i, ref in enumerate((outer_ref, middle_ref)):
        out_ref[i * room : i * room + rows, :] = ref[...]
        if rows < room:
            out_ref[i * room + rows : (i + 1) * room, :] = jnp.zeros((room - rows, ref.shape[1]), out_ref.dtype)


def relay_stack_kernel(*refs):
    depth = refs[0].shape[0]
    for i, part_ref in enumerate(refs[:-1]):
        refs[-1][i * depth : (i + 1) * depth, :] = part_ref[...]


def relay_chunk_kernel(first, count, known, lhs_ref, forward_ref, up_ref, *refs):
    came, out_refs = refs[:-2], refs[-2:]
    here = slice(2 * first, 2 * (first + count))

    def body(cols):
        lhs = jnp.concatenate([lhs_ref[0, here, :], lhs_ref[1, here, :]], axis=0)
        delta = jnp.dot(lhs, up_ref[:, cols], preferred_element_type=jnp.float32)
        for way in range(2):
            blocks = came[len(came) // 2 :] if way == 0 else came[: len(came) // 2]
            rows = jnp.concatenate([block[:, cols] for block in blocks], axis=0)
            passed = jnp.dot(forward_ref[way, here, : 2 * known], rows, preferred_element_type=jnp.float32)
            out_refs[way][:, cols] = (delta[2 * way * count : 2 * (way + 1) * count] + passed).astype(jnp.bfloat16)

    column_tiles(up_ref.shape[1], body)


def relay_pick_kernel(pick_ref, local_ref, up_ref, *refs):
    came, out_ref = refs[:-1], refs[-1]
    routes, depth = local_ref.shape[1:]

    def body(cols):
        rows = jnp.concatenate([block[:, cols] for block in came], axis=0)
        picked = jnp.dot(pick_ref[...], rows, preferred_element_type=jnp.float32)
        for p in range(2):
            up = up_ref[p * depth : (p + 1) * depth, cols]
            delta = jnp.dot(local_ref[p], up, preferred_element_type=jnp.float32)
            delta = delta.astype(jnp.bfloat16).astype(jnp.float32) + picked[p * routes : (p + 1) * routes]
            out_ref[p, :, cols] = delta.astype(out_ref.dtype)

    column_tiles(up_ref.shape[1], body)


def relay_gate_kernel(
    group_ref, pick_ref, panel_ref, base_ref, mine_ref, other_ref, early_ref, final_ref, out_ref
):
    routes = out_ref.shape[0]
    group = group_ref[0]

    def body(cols):
        scales = [
            jnp.dot(panel_ref[...], ref[:, cols], preferred_element_type=jnp.float32) for ref in (mine_ref, other_ref)
        ]
        picked = jnp.dot(pick_ref[...], final_ref[:, cols], preferred_element_type=jnp.float32)
        adapted = []
        for p in range(2):
            delta = early_ref[p, :, cols].astype(jnp.float32) + picked[p * routes : (p + 1) * routes]
            scale = jnp.where(group == p, scales[0], scales[1])
            adapted.append(scale * (base_ref[p, :, cols].astype(jnp.float32) + delta))
        gate, value = adapted
        out_ref[:, cols] = (gate / (1.0 + jnp.exp(-gate)) * value).astype(out_ref.dtype)

    column_tiles(out_ref.shape[1], body)


def relayed(seen, numbers, turn, magnitude, base, down, up):
    count = 4
    me, group = lax.axis_index("dp"), lax.axis_index("groups")
    steps, rows, hidden = base.shape[0], base.shape[1], base.shape[-1]
    panels, _, rank, _ = down.shape
    routes = 2 * steps * rows
    cap = max(2, (5 * rows + count - 1) // count)
    limit = max(
        3 * steps * cap,
        2 * routes,
        GAP + 2 * steps * cap,
        GAP + routes,
        2 * GAP + steps * cap,
    )
    limit = -(-limit // ROW_STEP) * ROW_STEP
    bf16, f32, i32 = jnp.bfloat16, jnp.float32, jnp.int32
    vmem = pl.BlockSpec(memory_space=pltpu.VMEM)
    smem = pl.BlockSpec(memory_space=pltpu.SMEM)

    def kernel(body, inputs, outputs, scalars=0, specs=None, scratch=(), cost=1):
        return pl.pallas_call(
            body,
            out_shape=[jax.ShapeDtypeStruct(shape, dtype) for shape, dtype in outputs],
            in_specs=specs or [smem] * scalars + [vmem] * (len(inputs) - scalars),
            out_specs=[vmem] * len(outputs),
            scratch_shapes=list(scratch),
            compiler_params=pltpu.CompilerParams(vmem_limit_bytes=VMEM_LIMIT),
            cost_estimate=pl.CostEstimate(flops=0, bytes_accessed=cost << 20, transcendentals=0),
        )(*inputs)

    info, forward = kernel(
        functools.partial(relay_plan_kernel, steps, rows),
        [me.reshape(1).astype(i32), *numbers],
        [((16, count * routes), f32), ((2, 2 * limit, 2 * limit), bf16)],
        scalars=1,
    )
    longest = info[8:16, 0:LANES]
    longest = jnp.maximum(longest, lax.ppermute(longest, "groups", [(0, 1), (1, 0)]))[3, 0]
    totals = [total for total in QUEUE_ROWS if total < limit] + [limit]
    branch = sum((longest > total).astype(i32) for total in totals[:-1])
    owner, within = info[9, :routes].astype(i32), info[10, :routes].astype(i32)
    behind = (me - owner) % count
    panel = (jnp.arange(count * panels, dtype=i32)[None, :] == (behind * panels + within)[:, None]).astype(bf16)
    slot = jnp.arange(2 * limit, dtype=i32)
    half_of = jnp.arange(2, dtype=i32)[:, None, None] == (slot % 2)[None, None, :]

    def arrives(at):
        hit = half_of & ((slot // 2)[None, None, :] == at.astype(i32)[None, :, None])
        return hit.astype(bf16).reshape(2 * routes, 2 * limit)

    from_outer, from_middle = arrives(info[7, :routes]), arrives(info[8, :routes])
    down, up, base, magnitude, _ = lax.optimization_barrier((down, up, base, magnitude, longest))
    down_rows, up_rows = kernel(
        relay_load_kernel,
        [down, up],
        [(down.shape, bf16), ((2, panels, rank, hidden), bf16)],
        specs=[pl.BlockSpec(memory_space=pl.ANY)] * 2,
        scratch=[pltpu.SemaphoreType.DMA((3,))],
    )
    up_rows = up_rows.reshape(2 * panels * rank, hidden)
    base_rows = base.transpose(3, 2, 0, 1, 4).reshape(2, routes, hidden)
    half = lax.dynamic_index_in_dim(magnitude, group, axis=1, keepdims=False)
    ready = (down_rows, up_rows, base_rows, half, info, forward, branch, panel, from_outer, from_middle, *seen)
    ready = lax.optimization_barrier(ready)
    down_rows, up_rows, base_rows, half, info, forward, branch, panel, from_outer, from_middle, *seen = ready

    [part] = kernel(relay_low_kernel, [info, down_rows, *seen], [((2 * rank, count * routes), f32)])
    scales = [half] + [turn(half, s) for s in range(1, count)]
    chip = part + lax.ppermute(part, "pair", [(0, 1), (1, 0)])
    lows = [chip, lax.ppermute(chip, "expert", [(0, 1), (1, 0)])]

    first = kernel(
        functools.partial(relay_first_kernel, panels),
        [info, *lows, up_rows],
        [((2 * CHUNK, hidden), bf16)] * (2 * LAG),
        scratch=[pltpu.VMEM((4 * GAP, 2 * panels * rank), bf16)],
    )
    outer_first, middle_first = first[:LAG], first[LAG:]

    def flow(total, operands):
        outer_first, middle_first, info, lows, forward, up_rows, from_outer, from_middle, scales = operands
        chunks = chunk_rows(total)
        got_outer, got_middle = [], []
        info, *lows = lax.optimization_barrier((info, *lows, outer_first[0]))[:-1]
        lhs, local = kernel(
            functools.partial(relay_rows_kernel, panels),
            [info, *lows],
            [((2, 2 * limit, 2 * panels * rank), bf16), ((2, routes, panels * rank), bf16)],
        )
        for k, (start, size) in enumerate(chunks):
            if k < LAG:
                outer, middle = outer_first[k], middle_first[k]
            else:
                known = k + 1 - LAG
                outer, middle = kernel(
                    functools.partial(relay_chunk_kernel, start, size, chunks[known][0]),
                    [lhs, forward, up_rows, *got_outer[:known], *got_middle[:known]],
                    [((2 * size, hidden), bf16)] * 2,
                    cost=4 + k,
                )
            got_middle.append(lax.ppermute(middle, "dp", [(1, 2), (2, 1)]))
            got_outer.append(lax.ppermute(outer, "dp", [(0, 1), (1, 0), (2, 3), (3, 2)]))
        *scales, _ = lax.optimization_barrier((*scales, got_outer[0]))
        [mine] = kernel(relay_stack_kernel, scales, [((count * panels, hidden), bf16)])
        other = lax.ppermute(mine, "groups", [(0, 1), (1, 0)])
        last, size = chunks[-1]
        early = jnp.concatenate([from_outer[:, : 2 * last], from_middle[:, : 2 * last]], axis=1)
        late = [part[:, 2 * last : 2 * (last + size)] for part in (from_outer, from_middle)]
        late = jnp.concatenate([jnp.pad(part, ((0, 0), (0, 2 * (CHUNK - size)))) for part in late], axis=1)
        [picked] = kernel(
            relay_pick_kernel,
            [early, local, up_rows, *got_outer[:-1], *got_middle[:-1]],
            [((2, routes, hidden), bf16)],
            cost=16,
        )
        [final] = kernel(relay_final_kernel, [got_outer[-1], got_middle[-1]], [((4 * CHUNK, hidden), bf16)])
        return picked, final, late, mine, other

    operands = (outer_first, middle_first, info, lows, forward, up_rows, from_outer, from_middle, scales)
    picked, final, late, mine, other = lax.switch(
        branch, [functools.partial(flow, total) for total in totals], operands
    )
    [out] = kernel(
        relay_gate_kernel,
        [group.reshape(1).astype(i32), late, panel, base_rows, mine, other, picked, final],
        [((routes, hidden), bf16)],
        scalars=1,
    )
    return out.reshape(2, steps, rows, hidden).transpose(1, 2, 0, 3)


def on_device(states, base, route_panels, down, up, magnitude):
    count = lax.axis_size("dp")
    me = lax.axis_index("dp")
    group = lax.axis_index("groups")
    steps, rows, width = states.shape
    hidden = base.shape[-1]
    panels, _, rank, _ = down.shape
    routes = 2 * steps * rows
    cap = max(2, (5 * rows + count - 1) // count)
    slots = -(-steps * cap // ROW_TILE) * ROW_TILE
    bf16, f32, i32 = jnp.bfloat16, jnp.float32, jnp.int32

    def turn(x, shift):
        return lax.ppermute(x, "dp", [(i, (i + shift) % count) for i in range(count)])

    if (count, lax.axis_size("expert"), lax.axis_size("pair")) == (4, 2, 2):
        one = states.reshape(steps * rows, width)
        flat = route_panels.transpose(2, 0, 1).reshape(1, routes)
        number = jnp.concatenate([flat // panels, flat % panels], axis=0).astype(bf16)
        number = jnp.pad(number, ((0, ROW_TILE - 2), (0, 0)))
        seen = [one] + [turn(one, s) for s in range(1, count)]
        numbers = [number] + [turn(number, s) for s in range(1, count)]
        return relayed(seen, numbers, turn, magnitude, base, down, up)

    pairs = route_panels.reshape(steps * rows, 2)
    numbers = jnp.concatenate([pairs // panels, pairs % panels], axis=1).astype(bf16)
    sent = jnp.concatenate(
        [states.reshape(steps * rows, width), jnp.pad(numbers, ((0, 0), (0, LANES - 4)))], axis=1
    )
    seen = [sent] + [turn(sent, s) for s in range(1, count)]

    half = lax.dynamic_index_in_dim(magnitude, group, axis=1, keepdims=False)
    mine = jnp.concatenate([half] + [turn(half, s) for s in range(1, count)], axis=0)
    other = lax.ppermute(mine, "groups", [(0, 1), (1, 0)])

    vmem = pl.BlockSpec(memory_space=pltpu.VMEM)
    smem = pl.BlockSpec(memory_space=pltpu.SMEM)
    params = pltpu.CompilerParams(vmem_limit_bytes=VMEM_LIMIT)
    part, info = pl.pallas_call(
        functools.partial(low_kernel, count, steps, rows, cap, slots),
        out_shape=(
            jax.ShapeDtypeStruct((2 * rank, count * routes), f32),
            jax.ShapeDtypeStruct((8, count * routes), f32),
        ),
        in_specs=[smem] + [vmem] * (1 + count),
        out_specs=(vmem, vmem),
        compiler_params=params,
    )(me.reshape(1).astype(i32), down, *seen)

    low = lax.psum(part, ("expert", "pair"))

    tile = min(1024, hidden)
    col_tiles = hidden // tile
    whole = lambda shape: pl.BlockSpec(shape, lambda p, n: (0,) * len(shape))
    deltas = pl.pallas_call(
        functools.partial(delta_kernel, count, slots),
        out_shape=[jax.ShapeDtypeStruct((slots, 2 * hidden), bf16)] * count,
        grid=(2, col_tiles),
        in_specs=[whole(info.shape)]
        + [whole(low.shape)]
        + [pl.BlockSpec((panels, None, rank, tile), lambda p, n: (0, p, 0, n))],
        out_specs=[pl.BlockSpec((slots, tile), lambda p, n: (0, p * col_tiles + n))] * count,
        scratch_shapes=[pltpu.VMEM((2, count * slots, panels * rank), bf16)],
        compiler_params=params,
    )(info, low, up)
    got = [deltas[0]] + [turn(deltas[s], count - s) for s in range(1, count)]

    ordered = route_panels.transpose(2, 0, 1).reshape(2, steps, rows)
    owner, within = ordered // panels, ordered % panels
    by_step = owner.transpose(1, 0, 2).reshape(steps, 2 * rows)
    earlier = jnp.tril(jnp.ones((2 * rows, 2 * rows), jnp.bool_), -1)
    rank_of = jnp.sum((by_step[:, :, None] == by_step[:, None, :]) & earlier[None], axis=2, dtype=i32)
    slot = rank_of + jnp.arange(steps, dtype=i32)[:, None] * cap
    slot = slot.reshape(steps, 2, rows).transpose(1, 0, 2).reshape(routes)
    owner, within = owner.reshape(routes), within.reshape(routes)
    ahead = (owner - me) % count
    behind = (me - owner) % count
    pick = (jnp.arange(count * slots, dtype=i32)[None, :] == (ahead * slots + slot)[:, None]).astype(bf16)
    panel = (jnp.arange(count * panels, dtype=i32)[None, :] == (behind * panels + within)[:, None]).astype(bf16)
    base_rows = base.transpose(3, 2, 0, 1, 4).reshape(2, routes, hidden)

    tile = min(512, hidden)
    col_tiles = hidden // tile
    whole = lambda shape: pl.BlockSpec(shape, lambda n: (0,) * len(shape))
    col = lambda depth, p: pl.BlockSpec((depth, tile), lambda n, p=p: (0, p * col_tiles + n))
    out = pl.pallas_call(
        functools.partial(gate_kernel, count),
        out_shape=jax.ShapeDtypeStruct((routes, hidden), bf16),
        grid=(col_tiles,),
        in_specs=[smem, whole(pick.shape), whole(panel.shape)]
        + [pl.BlockSpec((2, routes, tile), lambda n: (0, 0, n))]
        + [col(count * panels, 0)] * 2
        + [col(slots, 0)] * count
        + [col(slots, 1)] * count,
        out_specs=col(routes, 0),
        compiler_params=params,
    )(group.reshape(1).astype(i32), pick, panel, base_rows, mine, other, *got, *got)
    return out.reshape(2, steps, rows, hidden).transpose(1, 2, 0, 3)


def solution(mesh):
    return jax.shard_map(
        on_device,
        mesh=mesh,
        in_specs=(
            P(None, ("groups", "dp"), ("expert", "pair")),
            P(None, ("groups", "dp"), None, None, ("expert", "pair")),
            P(None, ("groups", "dp"), None),
            P("dp", None, None, ("expert", "pair")),
            P("dp", None, None, ("expert", "pair")),
            P("dp", None, ("expert", "pair")),
        ),
        out_specs=P(None, ("groups", "dp"), None, ("expert", "pair")),
        check_vma=False,
    )
```

```python
import functools

import jax
import jax.numpy as jnp
from jax import lax
from jax.experimental import pallas as pl
from jax.experimental.pallas import tpu as pltpu
from jax.sharding import PartitionSpec as P

LANES = 128
ROW_TILE = 16
VMEM_LIMIT = 10 * 1024 * 1024
RELAY_VMEM_LIMIT = 24 * 1024 * 1024


def nt_dot(a, b):
    return lax.dot_general(a, b, (((1,), (1,)), ((), ())), preferred_element_type=jnp.float32)


def earlier_in_step(steps, rows):
    routes = 2 * steps * rows
    first = lax.broadcasted_iota(jnp.int32, (routes, routes), 0)
    second = lax.broadcasted_iota(jnp.int32, (routes, routes), 1)
    same = (first // rows) % steps == (second // rows) % steps
    return jnp.where(same & (first < second), 1.0, 0.0).astype(jnp.bfloat16)


def low_kernel(count, steps, rows, cap, slots, me_ref, down_ref, *refs):
    state_refs, (part_ref, info_ref) = refs[:count], refs[count:]
    panels, _, rank, width = down_ref.shape
    routes = 2 * steps * rows
    me = me_ref[0].astype(jnp.float32)
    down = down_ref[...].reshape(panels * 2 * rank, width)
    pick = jnp.where(
        lax.broadcasted_iota(jnp.int32, (8, LANES), 0) == lax.broadcasted_iota(jnp.int32, (8, LANES), 1), 1.0, 0.0
    ).astype(jnp.bfloat16)
    before = earlier_in_step(steps, rows)
    lane = lax.broadcasted_iota(jnp.int32, (1, routes), 1)
    step_of = ((lane // rows) % steps).astype(jnp.float32)
    panel_of = (lax.broadcasted_iota(jnp.int32, (panels * 2 * rank, routes), 0) // (2 * rank)).astype(jnp.float32)
    for s in range(count):
        one = state_refs[s][...]
        both = jnp.concatenate([one, one], axis=0)
        numbers = nt_dot(pick, both[:, width:])
        owner = jnp.where(lane < routes // 2, numbers[0:1], numbers[1:2])
        within = jnp.where(lane < routes // 2, numbers[2:3], numbers[3:4])
        mine = owner == me
        rank_of = jnp.dot(
            jnp.broadcast_to(jnp.where(mine, 1.0, 0.0), (8, routes)).astype(jnp.bfloat16),
            before,
            preferred_element_type=jnp.float32,
        )[0:1]
        slot = jnp.where(mine, step_of * cap + rank_of, -1.0)
        held = jnp.where(mine, within, -1.0)
        cols = pl.ds(s * routes, routes)
        info_ref[:, cols] = jnp.concatenate([slot, held, jnp.zeros((6, routes), jnp.float32)], axis=0)
        low = nt_dot(down, both[:, :width])
        low = jnp.where(panel_of == held, low, 0.0)
        part_ref[:, cols] = jnp.sum(low.reshape(panels, 2 * rank, routes), axis=0)


def delta_kernel(count, slots, info_ref, low_ref, up_ref, *refs):
    out_refs, (lhs_ref,) = refs[:count], refs[count:]
    panels, rank, tile = up_ref.shape
    routes = info_ref.shape[1] // count

    @pl.when((pl.program_id(0) == 0) & (pl.program_id(1) == 0))
    def _():
        low = low_ref[...].astype(jnp.bfloat16).astype(jnp.float32)
        panel_of = (lax.broadcasted_iota(jnp.int32, (panels * rank, routes), 0) // rank).astype(jnp.float32)
        slot_of = lax.broadcasted_iota(jnp.int32, (slots, routes), 0).astype(jnp.float32)
        for s in range(count):
            cols = slice(s * routes, (s + 1) * routes)
            slot, held = info_ref[0:1, cols], info_ref[1:2, cols]
            place = jnp.where(slot_of == slot, 1.0, 0.0).astype(jnp.bfloat16)
            for p in range(2):
                wide = jnp.concatenate([low[p * rank : (p + 1) * rank, cols]] * panels, axis=0)
                wide = jnp.where(panel_of == held, wide, 0.0).astype(jnp.bfloat16)
                lhs_ref[p, s * slots : (s + 1) * slots, :] = nt_dot(place, wide).astype(jnp.bfloat16)

    p = pl.program_id(0)
    up = up_ref[...].reshape(panels * rank, tile)
    delta = jnp.dot(lhs_ref[p], up, preferred_element_type=jnp.float32).astype(jnp.bfloat16)
    for s in range(count):
        out_refs[s][...] = delta[s * slots : (s + 1) * slots]


def gate_kernel(count, group_ref, pick_ref, panel_ref, base_ref, mine_ref, other_ref, *refs):
    blocks, out_ref = refs[: 2 * count], refs[2 * count]
    slots = blocks[0].shape[0]
    group = group_ref[0]
    adapted = []
    for p in range(2):
        delta = None
        for s in range(count):
            part = jnp.dot(
                pick_ref[:, s * slots : (s + 1) * slots],
                blocks[p * count + s][...],
                preferred_element_type=jnp.float32,
            )
            delta = part if delta is None else delta + part
        scales = jnp.where(group == p, mine_ref[...], other_ref[...])
        scale = jnp.dot(panel_ref[...], scales, preferred_element_type=jnp.float32)
        adapted.append(scale * (base_ref[p].astype(jnp.float32) + delta))
    gate, value = adapted
    out_ref[...] = (gate / (1.0 + jnp.exp(-gate)) * value).astype(out_ref.dtype)


CHUNK = 24
LAG = 2
GAP = LAG * CHUNK
ROW_STEP = 8
MAGNITUDE_ROWS = 16
QUEUE_ROWS = (144, 168, 192, 216)


def chunk_rows(total):
    return [(at, min(CHUNK, total - at)) for at in range(0, total, CHUNK)]


def right_layout(n):
    gap = float(GAP)
    zero = jnp.zeros_like(n[0][0])
    place = {}

    def put(link, j, d, first, split=None, second=None):
        place[link, j, d] = (first, split, second)

    put(0, 0, 3, zero)
    put(0, 0, 2, n[0][3])
    put(0, 0, 1, n[0][3] + n[0][2])
    end = n[0][3] + n[0][2] + n[0][1]
    early = jnp.maximum(jnp.minimum(n[1][2], gap - n[1][3]), 0.0)
    far = jnp.maximum(n[1][3], gap)
    late = far + n[0][3] + n[1][2] - early
    put(1, 1, 3, zero)
    put(1, 0, 3, far)
    put(1, 1, 2, n[1][3], early, far + n[0][3] - early)
    put(1, 0, 2, late)
    end = jnp.maximum(end, late + n[0][2])
    one = jnp.maximum(n[2][3] + float(MAGNITUDE_ROWS), gap)
    two = jnp.maximum(one + n[1][3], far + gap)
    put(2, 2, 3, zero, zero + float(GAP - MAGNITUDE_ROWS), zero + float(MAGNITUDE_ROWS))
    put(2, 1, 3, one)
    put(2, 0, 3, two)
    return place, jnp.maximum(end, two + n[0][3])


def relay_plan_kernel(steps, rows, panels, me_ref, part_ref, *refs):
    count = 4
    route_refs, outs = refs[:3], refs[3:]
    info_ref, longest_ref, forward_ref, first_ref, held_ref, arrive_ref, panel_ref = outs
    routes = 2 * steps * rows
    limit = forward_ref.shape[1]
    me = me_ref[0]
    before = jnp.where(
        lax.broadcasted_iota(jnp.int32, (routes, routes), 0) < lax.broadcasted_iota(jnp.int32, (routes, routes), 1),
        1.0,
        0.0,
    ).astype(jnp.bfloat16)
    owners = lax.broadcasted_iota(jnp.int32, (8, routes), 0).astype(jnp.float32)
    same = lax.broadcasted_iota(jnp.int32, (routes, routes), 0) == lax.broadcasted_iota(jnp.int32, (routes, routes), 1)
    same = jnp.where(same, 1.0, 0.0).astype(jnp.bfloat16)
    owner, order, tally = [], [], []
    info_ref[...] = jnp.full(info_ref.shape, -1.0, jnp.float32)
    came = [ref[...].astype(jnp.float32) for ref in route_refs]
    came = came[:2] + [came[2][: came[0].shape[0]], came[2][came[0].shape[0] :]]
    for s in range(count):
        numbers = sum(jnp.where((part_ref[0] ^ i) == s, came[i], 0.0) for i in range(count))
        owner.append(numbers[0:1])
        hits = jnp.where(owners == owner[s], 1.0, 0.0)
        ahead = jnp.dot(hits.astype(jnp.bfloat16), before, preferred_element_type=jnp.float32)
        order.append(jnp.sum(ahead * hits, axis=0, keepdims=True))
        tally.append(jnp.sum(hits, axis=1, keepdims=True))
        cols = slice(s * routes, (s + 1) * routes)
        info_ref[0:1, cols] = jnp.where(owner[s] == me.astype(jnp.float32), numbers[1:2], -1.0)
        if s == 0:
            within = numbers[1:2]

    def position(place, link, d, s, turned, owners_from, owners_to):
        found = jnp.full((1, routes), -1.0, jnp.float32)
        for j in range(owners_from, owners_to):
            first, split, second = place[link, j, d]
            at = first + order[s]
            if split is not None:
                at = jnp.where(order[s] < split, at, second + order[s])
            found = jnp.where(owner[s] == float(3 - j if turned else j), at, found)
        return found

    for case in range(count):

        @pl.when(me == case)
        def _():
            longest = None
            for turned in (False, True):
                node = 3 - case if turned else case
                n = [[None] * count for _ in range(count)]
                for j in range(count):
                    for d in range(count):
                        s = (case - d) % count
                        if turned:
                            n[3 - j][3 - d] = tally[s][j : j + 1]
                        else:
                            n[j][d] = tally[s][j : j + 1]
                place, end = right_layout(n)
                longest = end if longest is None else jnp.maximum(longest, end)
                row = 1 if turned == (case % 2 == 1) else 4
                for d in range(node + 1, count):
                    s = (case - (3 - d if turned else d)) % count
                    cols = slice(s * routes, (s + 1) * routes)
                    info_ref[row : row + 1, cols] = position(place, node, d, s, turned, node, node + 1)
                    if node > 0:
                        info_ref[row + 1 : row + 2, cols] = position(place, node, d, s, turned, 0, node)
                        info_ref[row + 2 : row + 3, cols] = position(place, node - 1, d, s, turned, 0, node)
                if node > 0:
                    arrive = 7 if turned == (case % 2 == 0) else 8
                    info_ref[arrive : arrive + 1, 0:routes] = position(place, node - 1, node, 0, turned, 0, node)
            longest_ref[...] = jnp.broadcast_to(longest, longest_ref.shape)
            blocks = [j ^ case for j in range(count)]
            if case in (0, count - 1):
                blocks = [block ^ 1 if block >= 2 else block for block in blocks]
            block_of = sum(jnp.where(owner[0] == float(j), float(blocks[j]), 0.0) for j in range(count))
            stands = block_of * panels + within
            depth = count * panels
            rows_of = lax.broadcasted_iota(jnp.int32, (depth, routes), 0).astype(jnp.float32)
            panel_ref[...] = nt_dot(same, jnp.where(rows_of == stands, 1.0, 0.0).astype(jnp.bfloat16)).astype(
                jnp.bfloat16
            )

    shape = forward_ref.shape[1:]
    same_half = lax.broadcasted_iota(jnp.int32, shape, 0) % 2 == lax.broadcasted_iota(jnp.int32, shape, 1) % 2
    for way in range(2):
        passed = nt_dot(placed(info_ref, 3 * way + 2, shape[0]), placed(info_ref, 3 * way + 3, shape[0]))
        forward_ref[way] = jnp.where(same_half, passed, 0.0).astype(jnp.bfloat16)
        for i in range(LAG):
            rows = pl.ds(2 * CHUNK * (2 * i + way), 2 * CHUNK)
            first_ref[rows, :] = placed(info_ref, 3 * way + 1, 2 * CHUNK, i * CHUNK)
        stands = placed(info_ref, 7 + way, shape[0])[:, :routes]
        stands = nt_dot(same, stands)
        for p in range(2):
            half = lax.broadcasted_iota(jnp.int32, stands.shape, 1) % 2 == p
            arrive_ref[way, p * routes : (p + 1) * routes, :] = jnp.where(half, stands, 0.0).astype(jnp.bfloat16)
    panel = jnp.broadcast_to(info_ref[0:1, :], (8, info_ref.shape[1])).astype(jnp.bfloat16)
    panel = nt_dot(first_ref[...], panel)[:, 0:1]
    half_row = lax.broadcasted_iota(jnp.int32, held_ref.shape, 0)
    lane = lax.broadcasted_iota(jnp.int32, held_ref.shape, 1)
    both = held_ref.shape[1] // panels
    here = ((lane % both) // (both // 2) == half_row % 2) & ((lane // both).astype(jnp.float32) == panel)
    held_ref[...] = jnp.where(here, 1.0, 0.0).astype(jnp.bfloat16)


def relay_load_kernel(down_ref, up_ref, down_out, up_out, sems):
    copies = [
        pltpu.make_async_copy(down_ref, down_out, sems.at[0]),
        pltpu.make_async_copy(up_ref, up_out, sems.at[1]),
    ]
    for copy in copies:
        copy.start()
    for copy in copies:
        copy.wait()


def relay_branch_kernel(totals, own_ref, other_ref, out_ref):
    longest = jnp.max(jnp.maximum(own_ref[...], other_ref[...]))
    out_ref[0] = sum((longest > float(total)).astype(jnp.int32) for total in totals[:-1])


def relay_low_kernel(info_ref, down_ref, half_ref, beside_ref, *refs):
    state_refs, (part_ref, join_ref) = refs[:-2], refs[-2:]
    panels, _, rank, width = down_ref.shape
    routes = info_ref.shape[1] // len(state_refs)
    down = down_ref[...].reshape(panels * 2 * rank, width)
    panel_of = (lax.broadcasted_iota(jnp.int32, (panels * 2 * rank, routes), 0) // (2 * rank)).astype(jnp.float32)
    join_ref[:panels, :] = beside_ref[...]
    join_ref[panels:, :] = half_ref[...]
    for s, state_ref in enumerate(state_refs):
        one = state_ref[...]
        cols = slice(s * routes, (s + 1) * routes)
        low = nt_dot(down, jnp.concatenate([one, one], axis=0))
        low = jnp.where(panel_of == info_ref[0:1, cols], low, 0.0)
        part_ref[:, cols] = jnp.sum(low.reshape(panels, 2 * rank, routes), axis=0)


def summed_low(own_ref, core_ref, far_ref, diag_ref):
    low = (own_ref[...] + core_ref[...]) + (far_ref[...] + diag_ref[...])
    return low.astype(jnp.bfloat16).astype(jnp.float32)


def spread_low(low, info_ref, panels):
    held = info_ref[0:1, :]
    panel_of = lax.broadcasted_iota(jnp.int32, (panels * low.shape[0], held.shape[1]), 0) // low.shape[0]
    wide = jnp.concatenate([low] * panels, axis=0)
    return jnp.where(panel_of.astype(jnp.float32) == held, wide, 0.0).astype(jnp.bfloat16)


def placed(info_ref, row, half_rows, start=0):
    at = info_ref[row : row + 1, :] - float(start)
    slot_of = lax.broadcasted_iota(jnp.int32, (half_rows, at.shape[1]), 0) // 2
    return jnp.where(slot_of.astype(jnp.float32) == at, 1.0, 0.0).astype(jnp.bfloat16)


def low_rows(place, wide, panels, half_of):
    rows = nt_dot(place, wide)
    both = rows.shape[1] // panels
    own_half = half_of == (lax.broadcasted_iota(jnp.int32, rows.shape, 1) % both) // (both // 2)
    return jnp.where(own_half, rows, 0.0).astype(jnp.bfloat16)


def column_tiles(hidden, body, most=512):
    tile = min(most, hidden)

    @pl.loop(0, hidden // tile)
    def _(i):
        body(pl.ds(pl.multiple_of(i * tile, tile), tile))


def relay_first_kernel(
    index, first_ref, held_ref, own_ref, core_ref, far_ref, diag_ref, up_ref, *refs
):
    across_refs, (outer_ref, middle_ref, lhs_ref) = refs[:-3], refs[-3:]
    low = summed_low(own_ref, core_ref, far_ref, diag_ref).astype(jnp.bfloat16)
    here = slice(4 * CHUNK * index, 4 * CHUNK * (index + 1))
    rows = nt_dot(first_ref[here, :], low).astype(jnp.bfloat16)
    shape = (low.shape[0], held_ref.shape[1])
    source = lax.broadcasted_iota(jnp.int32, shape, 1) % shape[0]
    spread = jnp.where(lax.broadcasted_iota(jnp.int32, shape, 0) == source, 1.0, 0.0).astype(jnp.bfloat16)
    wide = jnp.dot(rows, spread, preferred_element_type=jnp.float32).astype(jnp.bfloat16)
    lhs_ref[...] = wide * held_ref[here, :]

    def body(cols):
        delta = jnp.dot(lhs_ref[...], up_ref[:, cols], preferred_element_type=jnp.float32).astype(jnp.bfloat16)
        outer_ref[:, cols] = delta[: 2 * CHUNK]
        middle_ref[:, cols] = delta[2 * CHUNK :]
        for across_ref in across_refs:
            at = 2 * CHUNK - across_ref.shape[0]
            outer_ref[at:, cols] = delta[at : 2 * CHUNK] + across_ref[:, cols]

    column_tiles(up_ref.shape[1], body, 1024)


def relay_rows_kernel(panels, info_ref, own_ref, core_ref, far_ref, diag_ref, lhs_ref, local_ref):
    wide = spread_low(summed_low(own_ref, core_ref, far_ref, diag_ref), info_ref, panels)
    for way in range(2):
        half_of = lax.broadcasted_iota(jnp.int32, lhs_ref.shape[1:], 0) % 2
        lhs_ref[way] = low_rows(placed(info_ref, 3 * way + 1, lhs_ref.shape[1]), wide, panels, half_of)
    routes = local_ref.shape[0] // 2
    shape = (2 * routes, routes)
    same = lax.broadcasted_iota(jnp.int32, shape, 0) % routes == lax.broadcasted_iota(jnp.int32, shape, 1)
    half_of = lax.broadcasted_iota(jnp.int32, local_ref.shape, 0) // routes
    local_ref[...] = low_rows(jnp.where(same, 1.0, 0.0).astype(jnp.bfloat16), wide[:, :routes], panels, half_of)


def relay_stack_kernel(me_ref, half_ref, beside_ref, across_ref, second_ref, out_ref):
    depth = half_ref.shape[0]
    out_ref[:depth] = half_ref[...]
    out_ref[depth : 2 * depth] = beside_ref[...]
    end = (me_ref[0] == 0) | (me_ref[0] == 3)

    @pl.when(end)
    def _():
        out_ref[2 * depth :] = second_ref[second_ref.shape[0] - 2 * depth :]

    @pl.when(jnp.logical_not(end))
    def _():
        out_ref[2 * depth :] = across_ref[...]


def relay_chunk_kernel(first, count, known, lhs_ref, forward_ref, up_ref, *refs):
    came, out_refs = refs[:-2], refs[-2:]
    here = slice(2 * first, 2 * (first + count))

    def body(cols):
        lhs = jnp.concatenate([lhs_ref[0, here, :], lhs_ref[1, here, :]], axis=0)
        delta = jnp.dot(lhs, up_ref[:, cols], preferred_element_type=jnp.float32)
        for way in range(2):
            blocks = came[len(came) // 2 :] if way == 0 else came[: len(came) // 2]
            rows = jnp.concatenate([block[:, cols] for block in blocks], axis=0)
            passed = jnp.dot(forward_ref[way, here, : 2 * known], rows, preferred_element_type=jnp.float32)
            out_refs[way][:, cols] = (delta[2 * way * count : 2 * (way + 1) * count] + passed).astype(jnp.bfloat16)

    column_tiles(up_ref.shape[1], body)


def relay_pick_kernel(known, arrive_ref, local_ref, up_ref, *refs):
    came, out_ref = refs[:-1], refs[-1]
    routes = out_ref.shape[1]

    def body(cols):
        delta = jnp.dot(local_ref[...], up_ref[:, cols], preferred_element_type=jnp.float32)
        delta = delta.astype(jnp.bfloat16).astype(jnp.float32)
        for way in range(2):
            blocks = came[way * len(came) // 2 : (way + 1) * len(came) // 2]
            rows = jnp.concatenate([block[:, cols] for block in blocks], axis=0)
            delta += jnp.dot(arrive_ref[way, :, : 2 * known], rows, preferred_element_type=jnp.float32)
        for p in range(2):
            out_ref[p, :, cols] = delta[p * routes : (p + 1) * routes].astype(out_ref.dtype)

    column_tiles(up_ref.shape[1], body)


def relay_gate_kernel(
    known, group_ref, arrive_ref, panel_ref, mine_ref, other_ref, base_ref, early_ref, outer_ref, middle_ref, out_ref, pick_ref
):
    rows = out_ref.shape[0]
    routes = 2 * rows
    size = outer_ref.shape[0]
    group = group_ref[0]
    shape = (size, arrive_ref.shape[2])
    last = lax.broadcasted_iota(jnp.int32, shape, 1) == 2 * known + lax.broadcasted_iota(jnp.int32, shape, 0)
    last = jnp.where(last, 1.0, 0.0).astype(jnp.bfloat16)
    for way in range(2):
        pick_ref[:, way * size : (way + 1) * size] = nt_dot(arrive_ref[way], last).astype(jnp.bfloat16)

    def body(cols):
        scales = [
            jnp.dot(panel_ref[...], ref[:, cols], preferred_element_type=jnp.float32) for ref in (mine_ref, other_ref)
        ]
        late = jnp.concatenate([outer_ref[:, cols], middle_ref[:, cols]], axis=0)
        picked = jnp.dot(pick_ref[...], late, preferred_element_type=jnp.float32)
        adapted = []
        for p in range(2):
            delta = early_ref[p, :, cols].astype(jnp.float32) + picked[p * routes : (p + 1) * routes]
            scale = jnp.where(group == p, scales[0], scales[1])
            adapted.append(scale * (base_ref[p, :, cols].astype(jnp.float32) + delta))
        gate, value = adapted
        hidden = (gate / (1.0 + jnp.exp(-gate)) * value).astype(out_ref.dtype)
        for k in range(2):
            out_ref[:, k, cols] = hidden[k * rows : (k + 1) * rows]

    column_tiles(out_ref.shape[2], body)


def relay_base_kernel(base_ref, out_ref):
    rows = base_ref.shape[0]

    def body(cols):
        for k in range(2):
            for p in range(2):
                out_ref[p, k * rows : (k + 1) * rows, cols] = base_ref[:, k, p, cols]

    column_tiles(base_ref.shape[3], body)


def relayed(seen, numbers, which, magnitude, base, down, up):
    count = 4
    me, group = lax.axis_index("dp"), lax.axis_index("groups")
    steps, rows, hidden = base.shape[0], base.shape[1], base.shape[-1]
    panels, _, rank, _ = down.shape
    routes = 2 * steps * rows
    cap = max(2, (5 * rows + count - 1) // count)
    limit = max(
        3 * steps * cap,
        2 * routes,
        GAP + 2 * steps * cap,
        GAP + routes,
        2 * GAP + steps * cap,
    )
    limit = -(-limit // ROW_STEP) * ROW_STEP
    bf16, f32, i32 = jnp.bfloat16, jnp.float32, jnp.int32
    vmem = pl.BlockSpec(memory_space=pltpu.VMEM)
    smem = pl.BlockSpec(memory_space=pltpu.SMEM)

    def kernel(body, inputs, outputs, scalars=0, specs=None, out_specs=None, scratch=(), cost=1):
        return pl.pallas_call(
            body,
            out_shape=[jax.ShapeDtypeStruct(shape, dtype) for shape, dtype in outputs],
            in_specs=specs or [smem] * scalars + [vmem] * (len(inputs) - scalars),
            out_specs=out_specs or [vmem] * len(outputs),
            scratch_shapes=list(scratch),
            compiler_params=pltpu.CompilerParams(vmem_limit_bytes=RELAY_VMEM_LIMIT),
            cost_estimate=pl.CostEstimate(flops=0, bytes_accessed=cost << 20, transcendentals=0),
        )(*inputs)

    base = base.reshape(steps * rows, 2, 2, hidden)
    outer_pairs, middle_pair = [(0, 1), (1, 0), (2, 3), (3, 2)], [(1, 2), (2, 1)]
    half = lax.dynamic_index_in_dim(magnitude, group, axis=1, keepdims=False)
    beside = lax.ppermute(half, "dp", outer_pairs)
    half, *numbers = lax.optimization_barrier((half, *numbers))
    info, longest, forward, first, held, arrive, panel = kernel(
        functools.partial(relay_plan_kernel, steps, rows, panels),
        [me.reshape(1).astype(i32), which.reshape(1).astype(i32), *numbers],
        [
            ((16, count * routes), f32),
            ((8, LANES), f32),
            ((2, 2 * limit, 2 * limit), bf16),
            ((4 * GAP, count * routes), bf16),
            ((4 * GAP, 2 * panels * rank), bf16),
            ((2, 2 * routes, 2 * limit), bf16),
            ((routes, count * panels), bf16),
        ],
        scalars=2,
        cost=128,
    )
    down, up, longest = lax.optimization_barrier((down, up, longest))
    down, up_rows = kernel(
        relay_load_kernel,
        [down, up.reshape(panels * 2 * rank, hidden)],
        [(down.shape, bf16), ((panels * 2 * rank, hidden), bf16)],
        specs=[pl.BlockSpec(memory_space=pltpu.HBM)] * 2,
        scratch=[pltpu.SemaphoreType.DMA((2,))],
    )
    totals = [total for total in QUEUE_ROWS if total < limit] + [limit]
    [branch] = kernel(
        functools.partial(relay_branch_kernel, totals),
        [longest, lax.ppermute(longest, "groups", [(0, 1), (1, 0)])],
        [((1,), i32)],
        out_specs=[smem],
    )

    down, up_rows, branch, *seen = lax.optimization_barrier((down, up_rows, branch, *seen))
    part, join = kernel(
        relay_low_kernel,
        [info, down, half, beside, *seen],
        [((2 * rank, count * routes), f32), ((2 * panels, hidden), bf16)],
    )
    lows = [part]
    for mask in (1, 2, 3):
        lows.append(lax.ppermute(part, ("expert", "pair"), [(i, i ^ mask) for i in range(4)]))
    across = lax.ppermute(join, "dp", middle_pair)

    def early(index, first, held, lows, up_rows, *across):
        return kernel(
            functools.partial(relay_first_kernel, index),
            [first, held, *lows, up_rows, *across],
            [((2 * CHUNK, hidden), bf16)] * 2,
            scratch=[pltpu.VMEM((4 * CHUNK, 2 * panels * rank), bf16)],
        )

    outer_first, middle_first = early(0, first, held, lows, up_rows)

    def flow(total, operands):
        (outer_first, middle_first, first, held, info, lows, forward, up_rows) = operands[:8]
        arrive, panel, base, half, beside, across = operands[8:]
        chunks = chunk_rows(total)
        got_outer, got_middle = [], []
        for k, (start, size) in enumerate(chunks):
            if k == 0:
                outer, middle = outer_first, middle_first
            elif k < LAG:
                outer, middle = early(k, first, held, lows, up_rows, across)
            else:
                if k == LAG:
                    info, base, *lows = lax.optimization_barrier((info, base, *lows, outer))[:-1]
                    [base_rows] = kernel(relay_base_kernel, [base], [((2, routes, hidden), bf16)])
                    base_rows, info = lax.optimization_barrier((base_rows, info))
                    lhs, local = kernel(
                        functools.partial(relay_rows_kernel, panels),
                        [info, *lows],
                        [((2, 2 * limit, 2 * panels * rank), bf16), ((2 * routes, 2 * panels * rank), bf16)],
                    )
                known = k + 1 - LAG
                outer, middle = kernel(
                    functools.partial(relay_chunk_kernel, start, size, chunks[known][0]),
                    [lhs, forward, up_rows, *got_outer[:known], *got_middle[:known]],
                    [((2 * size, hidden), bf16)] * 2,
                    cost=4 + k,
                )
            got_middle.append(lax.ppermute(middle, "dp", middle_pair))
            got_outer.append(lax.ppermute(outer, "dp", outer_pairs))
        [mine] = kernel(
            relay_stack_kernel,
            [me.reshape(1).astype(i32), half, beside, across, got_outer[1]],
            [((count * panels, hidden), bf16)],
            scalars=1,
        )
        other = lax.ppermute(mine, "groups", [(0, 1), (1, 0)])
        last, size = chunks[-1]
        [picked] = kernel(
            functools.partial(relay_pick_kernel, last),
            [arrive, local, up_rows, *got_outer[:-1], *got_middle[:-1]],
            [((2, routes, hidden), bf16)],
        )
        picked, *final = lax.optimization_barrier((picked, got_outer[-1], got_middle[-1]))
        [out] = kernel(
            functools.partial(relay_gate_kernel, last),
            [group.reshape(1).astype(i32), arrive, panel, mine, other, base_rows, picked, *final],
            [((steps * rows, 2, hidden), bf16)],
            scalars=1,
            scratch=[pltpu.VMEM((2 * routes, 4 * size), bf16)],
        )
        return out

    operands = (
        outer_first, middle_first, first, held, info, lows, forward, up_rows,
        arrive, panel, base, half, beside, across,
    )
    out = lax.switch(branch[0], [functools.partial(flow, total) for total in totals], operands)
    return out.reshape(steps, rows, 2, hidden)


def on_device(states, base, route_panels, down, up, magnitude):
    count = lax.axis_size("dp")
    me = lax.axis_index("dp")
    group = lax.axis_index("groups")
    steps, rows, width = states.shape
    hidden = base.shape[-1]
    panels, _, rank, _ = down.shape
    routes = 2 * steps * rows
    cap = max(2, (5 * rows + count - 1) // count)
    slots = -(-steps * cap // ROW_TILE) * ROW_TILE
    bf16, f32, i32 = jnp.bfloat16, jnp.float32, jnp.int32

    def turn(x, shift):
        return lax.ppermute(x, "dp", [(i, (i + shift) % count) for i in range(count)])

    if (count, lax.axis_size("expert"), lax.axis_size("pair")) == (4, 2, 2):
        one = states.reshape(steps * rows, width)
        flat = route_panels.transpose(2, 0, 1).reshape(1, routes)
        number = jnp.concatenate([flat // panels, flat % panels], axis=0).astype(bf16)
        number = jnp.pad(number, ((0, ROW_TILE - 2), (0, 0)))
        which = 2 * lax.axis_index("expert") + lax.axis_index("pair")
        one, number = lax.optimization_barrier((one, number))
        far = [(4 * d + e, 4 * ((d + e) % count) + e) for d in range(count) for e in range(4)]
        near = lax.ppermute(number, ("dp", "expert", "pair"), far)
        beside = lax.ppermute(near, "pair", [(0, 1), (1, 0)])
        both = lax.ppermute(jnp.concatenate([near, beside], axis=0), "expert", [(0, 1), (1, 0)])
        one, near = lax.optimization_barrier((one, near))
        seen = [one] + [turn(one, s) for s in range(1, count)]
        return relayed(seen, [near, beside, both], which, magnitude, base, down, up)

    pairs = route_panels.reshape(steps * rows, 2)
    numbers = jnp.concatenate([pairs // panels, pairs % panels], axis=1).astype(bf16)
    sent = jnp.concatenate(
        [states.reshape(steps * rows, width), jnp.pad(numbers, ((0, 0), (0, LANES - 4)))], axis=1
    )
    seen = [sent] + [turn(sent, s) for s in range(1, count)]

    half = lax.dynamic_index_in_dim(magnitude, group, axis=1, keepdims=False)
    mine = jnp.concatenate([half] + [turn(half, s) for s in range(1, count)], axis=0)
    other = lax.ppermute(mine, "groups", [(0, 1), (1, 0)])

    vmem = pl.BlockSpec(memory_space=pltpu.VMEM)
    smem = pl.BlockSpec(memory_space=pltpu.SMEM)
    params = pltpu.CompilerParams(vmem_limit_bytes=VMEM_LIMIT)
    part, info = pl.pallas_call(
        functools.partial(low_kernel, count, steps, rows, cap, slots),
        out_shape=(
            jax.ShapeDtypeStruct((2 * rank, count * routes), f32),
            jax.ShapeDtypeStruct((8, count * routes), f32),
        ),
        in_specs=[smem] + [vmem] * (1 + count),
        out_specs=(vmem, vmem),
        compiler_params=params,
    )(me.reshape(1).astype(i32), down, *seen)

    low = lax.psum(part, ("expert", "pair"))

    tile = min(1024, hidden)
    col_tiles = hidden // tile
    whole = lambda shape: pl.BlockSpec(shape, lambda p, n: (0,) * len(shape))
    deltas = pl.pallas_call(
        functools.partial(delta_kernel, count, slots),
        out_shape=[jax.ShapeDtypeStruct((slots, 2 * hidden), bf16)] * count,
        grid=(2, col_tiles),
        in_specs=[whole(info.shape)]
        + [whole(low.shape)]
        + [pl.BlockSpec((panels, None, rank, tile), lambda p, n: (0, p, 0, n))],
        out_specs=[pl.BlockSpec((slots, tile), lambda p, n: (0, p * col_tiles + n))] * count,
        scratch_shapes=[pltpu.VMEM((2, count * slots, panels * rank), bf16)],
        compiler_params=params,
    )(info, low, up)
    got = [deltas[0]] + [turn(deltas[s], count - s) for s in range(1, count)]

    ordered = route_panels.transpose(2, 0, 1).reshape(2, steps, rows)
    owner, within = ordered // panels, ordered % panels
    by_step = owner.transpose(1, 0, 2).reshape(steps, 2 * rows)
    earlier = jnp.tril(jnp.ones((2 * rows, 2 * rows), jnp.bool_), -1)
    rank_of = jnp.sum((by_step[:, :, None] == by_step[:, None, :]) & earlier[None], axis=2, dtype=i32)
    slot = rank_of + jnp.arange(steps, dtype=i32)[:, None] * cap
    slot = slot.reshape(steps, 2, rows).transpose(1, 0, 2).reshape(routes)
    owner, within = owner.reshape(routes), within.reshape(routes)
    ahead = (owner - me) % count
    behind = (me - owner) % count
    pick = (jnp.arange(count * slots, dtype=i32)[None, :] == (ahead * slots + slot)[:, None]).astype(bf16)
    panel = (jnp.arange(count * panels, dtype=i32)[None, :] == (behind * panels + within)[:, None]).astype(bf16)
    base_rows = base.transpose(3, 2, 0, 1, 4).reshape(2, routes, hidden)

    tile = min(512, hidden)
    col_tiles = hidden // tile
    whole = lambda shape: pl.BlockSpec(shape, lambda n: (0,) * len(shape))
    col = lambda depth, p: pl.BlockSpec((depth, tile), lambda n, p=p: (0, p * col_tiles + n))
    out = pl.pallas_call(
        functools.partial(gate_kernel, count),
        out_shape=jax.ShapeDtypeStruct((routes, hidden), bf16),
        grid=(col_tiles,),
        in_specs=[smem, whole(pick.shape), whole(panel.shape)]
        + [pl.BlockSpec((2, routes, tile), lambda n: (0, 0, n))]
        + [col(count * panels, 0)] * 2
        + [col(slots, 0)] * count
        + [col(slots, 1)] * count,
        out_specs=col(routes, 0),
        compiler_params=params,
    )(group.reshape(1).astype(i32), pick, panel, base_rows, mine, other, *got, *got)
    return out.reshape(2, steps, rows, hidden).transpose(1, 2, 0, 3)


def solution(mesh):
    return jax.shard_map(
        on_device,
        mesh=mesh,
        in_specs=(
            P(None, ("groups", "dp"), ("expert", "pair")),
            P(None, ("groups", "dp"), None, None, ("expert", "pair")),
            P(None, ("groups", "dp"), None),
            P("dp", None, None, ("expert", "pair")),
            P("dp", None, None, ("expert", "pair")),
            P("dp", None, ("expert", "pair")),
        ),
        out_specs=P(None, ("groups", "dp"), None, ("expert", "pair")),
        check_vma=False,
    )
```

```python
import functools

import jax
import jax.numpy as jnp
from jax import lax
from jax.experimental import pallas as pl
from jax.experimental.pallas import tpu as pltpu
from jax.sharding import PartitionSpec as P

LANES = 128
ROW_TILE = 16
VMEM_LIMIT = 10 * 1024 * 1024
RELAY_VMEM_LIMIT = 24 * 1024 * 1024


def nt_dot(a, b):
    return lax.dot_general(a, b, (((1,), (1,)), ((), ())), preferred_element_type=jnp.float32)


def earlier_in_step(steps, rows):
    routes = 2 * steps * rows
    first = lax.broadcasted_iota(jnp.int32, (routes, routes), 0)
    second = lax.broadcasted_iota(jnp.int32, (routes, routes), 1)
    same = (first // rows) % steps == (second // rows) % steps
    return jnp.where(same & (first < second), 1.0, 0.0).astype(jnp.bfloat16)


def low_kernel(count, steps, rows, cap, slots, me_ref, down_ref, *refs):
    state_refs, (part_ref, info_ref) = refs[:count], refs[count:]
    panels, _, rank, width = down_ref.shape
    routes = 2 * steps * rows
    me = me_ref[0].astype(jnp.float32)
    down = down_ref[...].reshape(panels * 2 * rank, width)
    pick = jnp.where(
        lax.broadcasted_iota(jnp.int32, (8, LANES), 0) == lax.broadcasted_iota(jnp.int32, (8, LANES), 1), 1.0, 0.0
    ).astype(jnp.bfloat16)
    before = earlier_in_step(steps, rows)
    lane = lax.broadcasted_iota(jnp.int32, (1, routes), 1)
    step_of = ((lane // rows) % steps).astype(jnp.float32)
    panel_of = (lax.broadcasted_iota(jnp.int32, (panels * 2 * rank, routes), 0) // (2 * rank)).astype(jnp.float32)
    for s in range(count):
        one = state_refs[s][...]
        both = jnp.concatenate([one, one], axis=0)
        numbers = nt_dot(pick, both[:, width:])
        owner = jnp.where(lane < routes // 2, numbers[0:1], numbers[1:2])
        within = jnp.where(lane < routes // 2, numbers[2:3], numbers[3:4])
        mine = owner == me
        rank_of = jnp.dot(
            jnp.broadcast_to(jnp.where(mine, 1.0, 0.0), (8, routes)).astype(jnp.bfloat16),
            before,
            preferred_element_type=jnp.float32,
        )[0:1]
        slot = jnp.where(mine, step_of * cap + rank_of, -1.0)
        held = jnp.where(mine, within, -1.0)
        cols = pl.ds(s * routes, routes)
        info_ref[:, cols] = jnp.concatenate([slot, held, jnp.zeros((6, routes), jnp.float32)], axis=0)
        low = nt_dot(down, both[:, :width])
        low = jnp.where(panel_of == held, low, 0.0)
        part_ref[:, cols] = jnp.sum(low.reshape(panels, 2 * rank, routes), axis=0)


def delta_kernel(count, slots, info_ref, low_ref, up_ref, *refs):
    out_refs, (lhs_ref,) = refs[:count], refs[count:]
    panels, rank, tile = up_ref.shape
    routes = info_ref.shape[1] // count

    @pl.when((pl.program_id(0) == 0) & (pl.program_id(1) == 0))
    def _():
        low = low_ref[...].astype(jnp.bfloat16).astype(jnp.float32)
        panel_of = (lax.broadcasted_iota(jnp.int32, (panels * rank, routes), 0) // rank).astype(jnp.float32)
        slot_of = lax.broadcasted_iota(jnp.int32, (slots, routes), 0).astype(jnp.float32)
        for s in range(count):
            cols = slice(s * routes, (s + 1) * routes)
            slot, held = info_ref[0:1, cols], info_ref[1:2, cols]
            place = jnp.where(slot_of == slot, 1.0, 0.0).astype(jnp.bfloat16)
            for p in range(2):
                wide = jnp.concatenate([low[p * rank : (p + 1) * rank, cols]] * panels, axis=0)
                wide = jnp.where(panel_of == held, wide, 0.0).astype(jnp.bfloat16)
                lhs_ref[p, s * slots : (s + 1) * slots, :] = nt_dot(place, wide).astype(jnp.bfloat16)

    p = pl.program_id(0)
    up = up_ref[...].reshape(panels * rank, tile)
    delta = jnp.dot(lhs_ref[p], up, preferred_element_type=jnp.float32).astype(jnp.bfloat16)
    for s in range(count):
        out_refs[s][...] = delta[s * slots : (s + 1) * slots]


def gate_kernel(count, group_ref, pick_ref, panel_ref, base_ref, mine_ref, other_ref, *refs):
    blocks, out_ref = refs[: 2 * count], refs[2 * count]
    slots = blocks[0].shape[0]
    group = group_ref[0]
    adapted = []
    for p in range(2):
        delta = None
        for s in range(count):
            part = jnp.dot(
                pick_ref[:, s * slots : (s + 1) * slots],
                blocks[p * count + s][...],
                preferred_element_type=jnp.float32,
            )
            delta = part if delta is None else delta + part
        scales = jnp.where(group == p, mine_ref[...], other_ref[...])
        scale = jnp.dot(panel_ref[...], scales, preferred_element_type=jnp.float32)
        adapted.append(scale * (base_ref[p].astype(jnp.float32) + delta))
    gate, value = adapted
    out_ref[...] = (gate / (1.0 + jnp.exp(-gate)) * value).astype(out_ref.dtype)


CHUNK = 24
LAG = 2
GAP = LAG * CHUNK
ROW_STEP = 8
MAGNITUDE_ROWS = 16
QUEUE_ROWS = (160, 168, 184, 208)
LONG_ROWS = 208


def chunk_rows(total):
    return [(at, min(CHUNK, total - at)) for at in range(0, total, CHUNK)]


def right_layout(n):
    gap = float(GAP)
    zero = jnp.zeros_like(n[0][0])
    place = {}

    def put(link, j, d, first, split=None, second=None):
        place[link, j, d] = (first, split, second)

    put(0, 0, 3, zero)
    put(0, 0, 2, n[0][3])
    put(0, 0, 1, n[0][3] + n[0][2])
    end = n[0][3] + n[0][2] + n[0][1]
    early = jnp.maximum(jnp.minimum(n[1][2], gap - n[1][3]), 0.0)
    far = jnp.maximum(n[1][3], gap)
    late = far + n[0][3] + n[1][2] - early
    put(1, 1, 3, zero)
    put(1, 0, 3, far)
    put(1, 1, 2, n[1][3], early, far + n[0][3] - early)
    put(1, 0, 2, late)
    end = jnp.maximum(end, late + n[0][2])
    one = jnp.maximum(n[2][3] + float(MAGNITUDE_ROWS), gap)
    two = jnp.maximum(one + n[1][3], far + gap)
    put(2, 2, 3, zero, zero + float(GAP - MAGNITUDE_ROWS), zero + float(MAGNITUDE_ROWS))
    put(2, 1, 3, one)
    put(2, 0, 3, two)
    return place, jnp.maximum(end, two + n[0][3])


def relay_plan_kernel(steps, rows, panels, me_ref, part_ref, *refs):
    count = 4
    route_refs, outs = refs[:3], refs[3:]
    info_ref, longest_ref, forward_ref, first_ref, held_ref, arrive_ref, panel_ref = outs
    routes = 2 * steps * rows
    limit = forward_ref.shape[1]
    me = me_ref[0]
    before = jnp.where(
        lax.broadcasted_iota(jnp.int32, (routes, routes), 0) < lax.broadcasted_iota(jnp.int32, (routes, routes), 1),
        1.0,
        0.0,
    ).astype(jnp.bfloat16)
    owners = lax.broadcasted_iota(jnp.int32, (8, routes), 0).astype(jnp.float32)
    same = lax.broadcasted_iota(jnp.int32, (routes, routes), 0) == lax.broadcasted_iota(jnp.int32, (routes, routes), 1)
    same = jnp.where(same, 1.0, 0.0).astype(jnp.bfloat16)
    owner, order, tally = [], [], []
    info_ref[...] = jnp.full(info_ref.shape, -1.0, jnp.float32)
    came = [ref[...].astype(jnp.float32) for ref in route_refs]
    came = came[:2] + [came[2][: came[0].shape[0]], came[2][came[0].shape[0] :]]
    for s in range(count):
        numbers = sum(jnp.where((part_ref[0] ^ i) == s, came[i], 0.0) for i in range(count))
        owner.append(numbers[0:1])
        hits = jnp.where(owners == owner[s], 1.0, 0.0)
        ahead = jnp.dot(hits.astype(jnp.bfloat16), before, preferred_element_type=jnp.float32)
        order.append(jnp.sum(ahead * hits, axis=0, keepdims=True))
        tally.append(jnp.sum(hits, axis=1, keepdims=True))
        cols = slice(s * routes, (s + 1) * routes)
        info_ref[0:1, cols] = jnp.where(owner[s] == me.astype(jnp.float32), numbers[1:2], -1.0)
        if s == 0:
            within = numbers[1:2]

    def position(place, link, d, s, turned, owners_from, owners_to):
        found = jnp.full((1, routes), -1.0, jnp.float32)
        for j in range(owners_from, owners_to):
            first, split, second = place[link, j, d]
            at = first + order[s]
            if split is not None:
                at = jnp.where(order[s] < split, at, second + order[s])
            found = jnp.where(owner[s] == float(3 - j if turned else j), at, found)
        return found

    for case in range(count):

        @pl.when(me == case)
        def _():
            longest = None
            for turned in (False, True):
                node = 3 - case if turned else case
                n = [[None] * count for _ in range(count)]
                for j in range(count):
                    for d in range(count):
                        s = (case - d) % count
                        if turned:
                            n[3 - j][3 - d] = tally[s][j : j + 1]
                        else:
                            n[j][d] = tally[s][j : j + 1]
                place, end = right_layout(n)
                longest = end if longest is None else jnp.maximum(longest, end)
                row = 1 if turned == (case % 2 == 1) else 4
                for d in range(node + 1, count):
                    s = (case - (3 - d if turned else d)) % count
                    cols = slice(s * routes, (s + 1) * routes)
                    info_ref[row : row + 1, cols] = position(place, node, d, s, turned, node, node + 1)
                    if node > 0:
                        info_ref[row + 1 : row + 2, cols] = position(place, node, d, s, turned, 0, node)
                        info_ref[row + 2 : row + 3, cols] = position(place, node - 1, d, s, turned, 0, node)
                if node > 0:
                    arrive = 7 if turned == (case % 2 == 0) else 8
                    info_ref[arrive : arrive + 1, 0:routes] = position(place, node - 1, node, 0, turned, 0, node)
            longest_ref[...] = jnp.broadcast_to(longest, longest_ref.shape)
            blocks = [j ^ case for j in range(count)]
            if case in (0, count - 1):
                blocks = [block ^ 1 if block >= 2 else block for block in blocks]
            block_of = sum(jnp.where(owner[0] == float(j), float(blocks[j]), 0.0) for j in range(count))
            stands = block_of * panels + within
            depth = count * panels
            rows_of = lax.broadcasted_iota(jnp.int32, (depth, routes), 0).astype(jnp.float32)
            panel_ref[...] = nt_dot(same, jnp.where(rows_of == stands, 1.0, 0.0).astype(jnp.bfloat16)).astype(
                jnp.bfloat16
            )

    shape = forward_ref.shape[1:]
    same_half = lax.broadcasted_iota(jnp.int32, shape, 0) % 2 == lax.broadcasted_iota(jnp.int32, shape, 1) % 2
    for way in range(2):
        passed = nt_dot(placed(info_ref, 3 * way + 2, shape[0]), placed(info_ref, 3 * way + 3, shape[0]))
        forward_ref[way] = jnp.where(same_half, passed, 0.0).astype(jnp.bfloat16)
        for i in range(LAG):
            rows = pl.ds(2 * CHUNK * (2 * i + way), 2 * CHUNK)
            first_ref[rows, :] = placed(info_ref, 3 * way + 1, 2 * CHUNK, i * CHUNK)
        stands = placed(info_ref, 7 + way, shape[0])[:, :routes]
        stands = nt_dot(same, stands)
        for p in range(2):
            half = lax.broadcasted_iota(jnp.int32, stands.shape, 1) % 2 == p
            arrive_ref[way, p * routes : (p + 1) * routes, :] = jnp.where(half, stands, 0.0).astype(jnp.bfloat16)
    panel = jnp.broadcast_to(info_ref[0:1, :], (8, info_ref.shape[1])).astype(jnp.bfloat16)
    panel = nt_dot(first_ref[...], panel)[:, 0:1]
    half_row = lax.broadcasted_iota(jnp.int32, held_ref.shape, 0)
    lane = lax.broadcasted_iota(jnp.int32, held_ref.shape, 1)
    both = held_ref.shape[1] // panels
    here = ((lane % both) // (both // 2) == half_row % 2) & ((lane // both).astype(jnp.float32) == panel)
    held_ref[...] = jnp.where(here, 1.0, 0.0).astype(jnp.bfloat16)


def relay_load_kernel(down_ref, up_ref, down_out, up_out, sems):
    copies = [
        pltpu.make_async_copy(down_ref, down_out, sems.at[0]),
        pltpu.make_async_copy(up_ref, up_out, sems.at[1]),
    ]
    for copy in copies:
        copy.start()
    for copy in copies:
        copy.wait()


def relay_branch_kernel(totals, own_ref, other_ref, out_ref):
    longest = jnp.max(jnp.maximum(own_ref[...], other_ref[...]))
    out_ref[0] = sum((longest > float(total)).astype(jnp.int32) for total in totals[:-1])


def relay_low_kernel(info_ref, down_ref, half_ref, beside_ref, *refs):
    state_refs, (part_ref, join_ref) = refs[:-2], refs[-2:]
    panels, _, rank, width = down_ref.shape
    routes = info_ref.shape[1] // len(state_refs)
    down = down_ref[...].reshape(panels * 2 * rank, width)
    panel_of = (lax.broadcasted_iota(jnp.int32, (panels * 2 * rank, routes), 0) // (2 * rank)).astype(jnp.float32)
    join_ref[:panels, :] = beside_ref[...]
    join_ref[panels:, :] = half_ref[...]
    lows = nt_dot(down, jnp.concatenate([state_ref[...] for state_ref in state_refs], axis=0))
    rows = routes // 2
    for s in range(len(state_refs)):
        cols = slice(s * routes, (s + 1) * routes)
        low = lows[:, s * rows : (s + 1) * rows]
        low = jnp.where(panel_of == info_ref[0:1, cols], jnp.concatenate([low, low], axis=1), 0.0)
        part_ref[:, cols] = jnp.sum(low.reshape(panels, 2 * rank, routes), axis=0)


def summed_low(own_ref, core_ref, far_ref, diag_ref):
    low = (own_ref[...] + core_ref[...]) + (far_ref[...] + diag_ref[...])
    return low.astype(jnp.bfloat16).astype(jnp.float32)


def spread_low(low, info_ref, panels):
    held = info_ref[0:1, :]
    panel_of = lax.broadcasted_iota(jnp.int32, (panels * low.shape[0], held.shape[1]), 0) // low.shape[0]
    wide = jnp.concatenate([low] * panels, axis=0)
    return jnp.where(panel_of.astype(jnp.float32) == held, wide, 0.0).astype(jnp.bfloat16)


def placed(info_ref, row, half_rows, start=0):
    at = info_ref[row : row + 1, :] - float(start)
    slot_of = lax.broadcasted_iota(jnp.int32, (half_rows, at.shape[1]), 0) // 2
    return jnp.where(slot_of.astype(jnp.float32) == at, 1.0, 0.0).astype(jnp.bfloat16)


def low_rows(place, wide, panels, half_of):
    rows = nt_dot(place, wide)
    both = rows.shape[1] // panels
    own_half = half_of == (lax.broadcasted_iota(jnp.int32, rows.shape, 1) % both) // (both // 2)
    return jnp.where(own_half, rows, 0.0).astype(jnp.bfloat16)


def column_tiles(hidden, body, most=512):
    tile = min(most, hidden)

    @pl.loop(0, hidden // tile)
    def _(i):
        body(pl.ds(pl.multiple_of(i * tile, tile), tile))


def relay_first_kernel(
    index, first_ref, held_ref, own_ref, core_ref, far_ref, diag_ref, up_ref, *refs
):
    across_refs, (outer_ref, middle_ref, lhs_ref) = refs[:-3], refs[-3:]
    low = summed_low(own_ref, core_ref, far_ref, diag_ref).astype(jnp.bfloat16)
    here = slice(4 * CHUNK * index, 4 * CHUNK * (index + 1))
    rows = nt_dot(first_ref[here, :], low).astype(jnp.bfloat16)
    shape = (low.shape[0], held_ref.shape[1])
    source = lax.broadcasted_iota(jnp.int32, shape, 1) % shape[0]
    spread = jnp.where(lax.broadcasted_iota(jnp.int32, shape, 0) == source, 1.0, 0.0).astype(jnp.bfloat16)
    wide = jnp.dot(rows, spread, preferred_element_type=jnp.float32).astype(jnp.bfloat16)
    lhs_ref[...] = wide * held_ref[here, :]

    def body(cols):
        delta = jnp.dot(lhs_ref[...], up_ref[:, cols], preferred_element_type=jnp.float32).astype(jnp.bfloat16)
        outer_ref[:, cols] = delta[: 2 * CHUNK]
        middle_ref[:, cols] = delta[2 * CHUNK :]
        for across_ref in across_refs:
            at = 2 * CHUNK - across_ref.shape[0]
            outer_ref[at:, cols] = delta[at : 2 * CHUNK] + across_ref[:, cols]

    column_tiles(up_ref.shape[1], body, 1024)


def relay_rows_kernel(panels, info_ref, own_ref, core_ref, far_ref, diag_ref, lhs_ref, local_ref):
    wide = spread_low(summed_low(own_ref, core_ref, far_ref, diag_ref), info_ref, panels)
    for way in range(2):
        half_of = lax.broadcasted_iota(jnp.int32, lhs_ref.shape[1:], 0) % 2
        lhs_ref[way] = low_rows(placed(info_ref, 3 * way + 1, lhs_ref.shape[1]), wide, panels, half_of)
    routes = local_ref.shape[0] // 2
    shape = (2 * routes, routes)
    same = lax.broadcasted_iota(jnp.int32, shape, 0) % routes == lax.broadcasted_iota(jnp.int32, shape, 1)
    half_of = lax.broadcasted_iota(jnp.int32, local_ref.shape, 0) // routes
    local_ref[...] = low_rows(jnp.where(same, 1.0, 0.0).astype(jnp.bfloat16), wide[:, :routes], panels, half_of)


def relay_stack_kernel(me_ref, half_ref, beside_ref, across_ref, second_ref, out_ref):
    depth = half_ref.shape[0]
    out_ref[:depth] = half_ref[...]
    out_ref[depth : 2 * depth] = beside_ref[...]
    end = (me_ref[0] == 0) | (me_ref[0] == 3)

    @pl.when(end)
    def _():
        out_ref[2 * depth :] = second_ref[second_ref.shape[0] - 2 * depth :]

    @pl.when(jnp.logical_not(end))
    def _():
        out_ref[2 * depth :] = across_ref[...]


def relay_chunk_kernel(first, count, known, tile, lhs_ref, forward_ref, up_ref, *refs):
    came, out_refs = refs[:-2], refs[-2:]
    here = slice(2 * first, 2 * (first + count))

    def body(cols):
        lhs = jnp.concatenate([lhs_ref[0, here, :], lhs_ref[1, here, :]], axis=0)
        delta = jnp.dot(lhs, up_ref[:, cols], preferred_element_type=jnp.float32)
        for way in range(2):
            blocks = came[len(came) // 2 :] if way == 0 else came[: len(came) // 2]
            rows = jnp.concatenate([block[:, cols] for block in blocks], axis=0)
            passed = jnp.dot(forward_ref[way, here, : 2 * known], rows, preferred_element_type=jnp.float32)
            out_refs[way][:, cols] = (delta[2 * way * count : 2 * (way + 1) * count] + passed).astype(jnp.bfloat16)

    column_tiles(up_ref.shape[1], body, tile)


def relay_pick_kernel(known, tile, arrive_ref, local_ref, up_ref, *refs):
    came, out_ref = refs[:-1], refs[-1]
    routes = out_ref.shape[1]

    def body(cols):
        delta = jnp.dot(local_ref[...], up_ref[:, cols], preferred_element_type=jnp.float32)
        delta = delta.astype(jnp.bfloat16).astype(jnp.float32)
        for way in range(2):
            blocks = came[way * len(came) // 2 : (way + 1) * len(came) // 2]
            rows = jnp.concatenate([block[:, cols] for block in blocks], axis=0)
            delta += jnp.dot(arrive_ref[way, :, : 2 * known], rows, preferred_element_type=jnp.float32)
        for p in range(2):
            out_ref[p, :, cols] = delta[p * routes : (p + 1) * routes].astype(out_ref.dtype)

    column_tiles(up_ref.shape[1], body, tile)


def relay_gate_kernel(
    known, group_ref, arrive_ref, panel_ref, mine_ref, other_ref, base_ref, early_ref, outer_ref, middle_ref, out_ref, pick_ref
):
    rows = out_ref.shape[0]
    routes = 2 * rows
    size = outer_ref.shape[0]
    group = group_ref[0]
    shape = (size, arrive_ref.shape[2])
    last = lax.broadcasted_iota(jnp.int32, shape, 1) == 2 * known + lax.broadcasted_iota(jnp.int32, shape, 0)
    last = jnp.where(last, 1.0, 0.0).astype(jnp.bfloat16)
    for way in range(2):
        pick_ref[:, way * size : (way + 1) * size] = nt_dot(arrive_ref[way], last).astype(jnp.bfloat16)

    def body(cols):
        scales = [
            jnp.dot(panel_ref[...], ref[:, cols], preferred_element_type=jnp.float32) for ref in (mine_ref, other_ref)
        ]
        late = jnp.concatenate([outer_ref[:, cols], middle_ref[:, cols]], axis=0)
        picked = jnp.dot(pick_ref[...], late, preferred_element_type=jnp.float32)
        adapted = []
        for p in range(2):
            delta = early_ref[p, :, cols].astype(jnp.float32) + picked[p * routes : (p + 1) * routes]
            scale = jnp.where(group == p, scales[0], scales[1])
            adapted.append(scale * (base_ref[p, :, cols].astype(jnp.float32) + delta))
        gate, value = adapted
        hidden = (gate / (1.0 + jnp.exp(-gate)) * value).astype(out_ref.dtype)
        for k in range(2):
            out_ref[:, k, cols] = hidden[k * rows : (k + 1) * rows]

    column_tiles(out_ref.shape[2], body, 1024)


def relay_base_kernel(base_ref, out_ref):
    rows = base_ref.shape[0]

    def body(cols):
        for k in range(2):
            for p in range(2):
                out_ref[p, k * rows : (k + 1) * rows, cols] = base_ref[:, k, p, cols]

    column_tiles(base_ref.shape[3], body)


def relayed(seen, numbers, which, magnitude, base, down, up):
    count = 4
    me, group = lax.axis_index("dp"), lax.axis_index("groups")
    steps, rows, hidden = base.shape[0], base.shape[1], base.shape[-1]
    panels, _, rank, _ = down.shape
    routes = 2 * steps * rows
    cap = max(2, (5 * rows + count - 1) // count)
    limit = max(
        3 * steps * cap,
        2 * routes,
        GAP + 2 * steps * cap,
        GAP + routes,
        2 * GAP + steps * cap,
    )
    limit = -(-limit // ROW_STEP) * ROW_STEP
    bf16, f32, i32 = jnp.bfloat16, jnp.float32, jnp.int32
    vmem = pl.BlockSpec(memory_space=pltpu.VMEM)
    smem = pl.BlockSpec(memory_space=pltpu.SMEM)

    def kernel(body, inputs, outputs, scalars=0, specs=None, out_specs=None, scratch=(), cost=1):
        return pl.pallas_call(
            body,
            out_shape=[jax.ShapeDtypeStruct(shape, dtype) for shape, dtype in outputs],
            in_specs=specs or [smem] * scalars + [vmem] * (len(inputs) - scalars),
            out_specs=out_specs or [vmem] * len(outputs),
            scratch_shapes=list(scratch),
            compiler_params=pltpu.CompilerParams(vmem_limit_bytes=RELAY_VMEM_LIMIT),
            cost_estimate=pl.CostEstimate(flops=0, bytes_accessed=cost << 20, transcendentals=0),
        )(*inputs)

    base = base.reshape(steps * rows, 2, 2, hidden)
    outer_pairs, middle_pair = [(0, 1), (1, 0), (2, 3), (3, 2)], [(1, 2), (2, 1)]
    half = lax.dynamic_index_in_dim(magnitude, group, axis=1, keepdims=False)
    beside = lax.ppermute(half, "dp", outer_pairs)
    half, *numbers = lax.optimization_barrier((half, *numbers))
    info, longest, forward, first, held, arrive, panel = kernel(
        functools.partial(relay_plan_kernel, steps, rows, panels),
        [me.reshape(1).astype(i32), which.reshape(1).astype(i32), *numbers],
        [
            ((16, count * routes), f32),
            ((8, LANES), f32),
            ((2, 2 * limit, 2 * limit), bf16),
            ((4 * GAP, count * routes), bf16),
            ((4 * GAP, 2 * panels * rank), bf16),
            ((2, 2 * routes, 2 * limit), bf16),
            ((routes, count * panels), bf16),
        ],
        scalars=2,
        cost=128,
    )
    down, up, longest = lax.optimization_barrier((down, up, longest))
    down, up_rows = kernel(
        relay_load_kernel,
        [down, up.reshape(panels * 2 * rank, hidden)],
        [(down.shape, bf16), ((panels * 2 * rank, hidden), bf16)],
        specs=[pl.BlockSpec(memory_space=pltpu.HBM)] * 2,
        scratch=[pltpu.SemaphoreType.DMA((2,))],
    )
    totals = [total for total in QUEUE_ROWS if total < limit] + [limit]
    [branch] = kernel(
        functools.partial(relay_branch_kernel, totals),
        [longest, lax.ppermute(longest, "groups", [(0, 1), (1, 0)])],
        [((1,), i32)],
        out_specs=[smem],
    )

    down, up_rows, branch, *seen = lax.optimization_barrier((down, up_rows, branch, *seen))
    part, join = kernel(
        relay_low_kernel,
        [info, down, half, beside, *seen],
        [((2 * rank, count * routes), f32), ((2 * panels, hidden), bf16)],
    )
    lows = [part]
    for mask in (1, 2, 3):
        lows.append(lax.ppermute(part, ("expert", "pair"), [(i, i ^ mask) for i in range(4)]))
    across = lax.ppermute(join, "dp", middle_pair)

    def early(index, first, held, lows, up_rows, *across):
        return kernel(
            functools.partial(relay_first_kernel, index),
            [first, held, *lows, up_rows, *across],
            [((2 * CHUNK, hidden), bf16)] * 2,
            scratch=[pltpu.VMEM((4 * CHUNK, 2 * panels * rank), bf16)],
        )

    outer_first, middle_first = early(0, first, held, lows, up_rows)

    def flow(total, operands):
        (outer_first, middle_first, first, held, info, lows, forward, up_rows) = operands[:8]
        arrive, panel, base, half, beside, across = operands[8:]
        chunks = chunk_rows(total)
        tile = 512 if total < LONG_ROWS else 256
        got_outer, got_middle = [], []
        for k, (start, size) in enumerate(chunks):
            if k == 0:
                outer, middle = outer_first, middle_first
            elif k < LAG:
                outer, middle = early(k, first, held, lows, up_rows, across)
            else:
                if k == LAG:
                    info, base, *lows = lax.optimization_barrier((info, base, *lows, outer))[:-1]
                    [base_rows] = kernel(relay_base_kernel, [base], [((2, routes, hidden), bf16)])
                    base_rows, info = lax.optimization_barrier((base_rows, info))
                    lhs, local = kernel(
                        functools.partial(relay_rows_kernel, panels),
                        [info, *lows],
                        [((2, 2 * limit, 2 * panels * rank), bf16), ((2 * routes, 2 * panels * rank), bf16)],
                    )
                known = k + 1 - LAG
                outer, middle = kernel(
                    functools.partial(relay_chunk_kernel, start, size, chunks[known][0], tile),
                    [lhs, forward, up_rows, *got_outer[:known], *got_middle[:known]],
                    [((2 * size, hidden), bf16)] * 2,
                    cost=4 + k,
                )
            got_middle.append(lax.ppermute(middle, "dp", middle_pair))
            got_outer.append(lax.ppermute(outer, "dp", outer_pairs))
        [mine] = kernel(
            relay_stack_kernel,
            [me.reshape(1).astype(i32), half, beside, across, got_outer[1]],
            [((count * panels, hidden), bf16)],
            scalars=1,
        )
        other = lax.ppermute(mine, "groups", [(0, 1), (1, 0)])
        last, size = chunks[-1]
        [picked] = kernel(
            functools.partial(relay_pick_kernel, last, tile),
            [arrive, local, up_rows, *got_outer[:-1], *got_middle[:-1]],
            [((2, routes, hidden), bf16)],
        )
        picked, *final = lax.optimization_barrier((picked, got_outer[-1], got_middle[-1]))
        [out] = kernel(
            functools.partial(relay_gate_kernel, last),
            [group.reshape(1).astype(i32), arrive, panel, mine, other, base_rows, picked, *final],
            [((steps * rows, 2, hidden), bf16)],
            scalars=1,
            scratch=[pltpu.VMEM((2 * routes, 4 * size), bf16)],
        )
        return out

    operands = (
        outer_first, middle_first, first, held, info, lows, forward, up_rows,
        arrive, panel, base, half, beside, across,
    )
    out = lax.switch(branch[0], [functools.partial(flow, total) for total in totals], operands)
    return out.reshape(steps, rows, 2, hidden)


def on_device(states, base, route_panels, down, up, magnitude):
    count = lax.axis_size("dp")
    me = lax.axis_index("dp")
    group = lax.axis_index("groups")
    steps, rows, width = states.shape
    hidden = base.shape[-1]
    panels, _, rank, _ = down.shape
    routes = 2 * steps * rows
    cap = max(2, (5 * rows + count - 1) // count)
    slots = -(-steps * cap // ROW_TILE) * ROW_TILE
    bf16, f32, i32 = jnp.bfloat16, jnp.float32, jnp.int32

    def turn(x, shift):
        return lax.ppermute(x, "dp", [(i, (i + shift) % count) for i in range(count)])

    if (count, lax.axis_size("expert"), lax.axis_size("pair")) == (4, 2, 2):
        one = states.reshape(steps * rows, width)
        which = 2 * lax.axis_index("expert") + lax.axis_index("pair")
        far = [(4 * d + e, 4 * ((d + e) % count) + e) for d in range(count) for e in range(4)]
        near = lax.ppermute(route_panels, ("dp", "expert", "pair"), far)
        one, near = lax.optimization_barrier((one, near))
        flat = near.transpose(2, 0, 1).reshape(1, routes)
        near = jnp.concatenate([flat // panels, flat % panels], axis=0).astype(bf16)
        near = jnp.pad(near, ((0, ROW_TILE - 2), (0, 0)))
        beside = lax.ppermute(near, "pair", [(0, 1), (1, 0)])
        both = lax.ppermute(jnp.concatenate([near, beside], axis=0), "expert", [(0, 1), (1, 0)])
        seen = [one] + [turn(one, s) for s in range(1, count)]
        return relayed(seen, [near, beside, both], which, magnitude, base, down, up)

    pairs = route_panels.reshape(steps * rows, 2)
    numbers = jnp.concatenate([pairs // panels, pairs % panels], axis=1).astype(bf16)
    sent = jnp.concatenate(
        [states.reshape(steps * rows, width), jnp.pad(numbers, ((0, 0), (0, LANES - 4)))], axis=1
    )
    seen = [sent] + [turn(sent, s) for s in range(1, count)]

    half = lax.dynamic_index_in_dim(magnitude, group, axis=1, keepdims=False)
    mine = jnp.concatenate([half] + [turn(half, s) for s in range(1, count)], axis=0)
    other = lax.ppermute(mine, "groups", [(0, 1), (1, 0)])

    vmem = pl.BlockSpec(memory_space=pltpu.VMEM)
    smem = pl.BlockSpec(memory_space=pltpu.SMEM)
    params = pltpu.CompilerParams(vmem_limit_bytes=VMEM_LIMIT)
    part, info = pl.pallas_call(
        functools.partial(low_kernel, count, steps, rows, cap, slots),
        out_shape=(
            jax.ShapeDtypeStruct((2 * rank, count * routes), f32),
            jax.ShapeDtypeStruct((8, count * routes), f32),
        ),
        in_specs=[smem] + [vmem] * (1 + count),
        out_specs=(vmem, vmem),
        compiler_params=params,
    )(me.reshape(1).astype(i32), down, *seen)

    low = lax.psum(part, ("expert", "pair"))

    tile = min(1024, hidden)
    col_tiles = hidden // tile
    whole = lambda shape: pl.BlockSpec(shape, lambda p, n: (0,) * len(shape))
    deltas = pl.pallas_call(
        functools.partial(delta_kernel, count, slots),
        out_shape=[jax.ShapeDtypeStruct((slots, 2 * hidden), bf16)] * count,
        grid=(2, col_tiles),
        in_specs=[whole(info.shape)]
        + [whole(low.shape)]
        + [pl.BlockSpec((panels, None, rank, tile), lambda p, n: (0, p, 0, n))],
        out_specs=[pl.BlockSpec((slots, tile), lambda p, n: (0, p * col_tiles + n))] * count,
        scratch_shapes=[pltpu.VMEM((2, count * slots, panels * rank), bf16)],
        compiler_params=params,
    )(info, low, up)
    got = [deltas[0]] + [turn(deltas[s], count - s) for s in range(1, count)]

    ordered = route_panels.transpose(2, 0, 1).reshape(2, steps, rows)
    owner, within = ordered // panels, ordered % panels
    by_step = owner.transpose(1, 0, 2).reshape(steps, 2 * rows)
    earlier = jnp.tril(jnp.ones((2 * rows, 2 * rows), jnp.bool_), -1)
    rank_of = jnp.sum((by_step[:, :, None] == by_step[:, None, :]) & earlier[None], axis=2, dtype=i32)
    slot = rank_of + jnp.arange(steps, dtype=i32)[:, None] * cap
    slot = slot.reshape(steps, 2, rows).transpose(1, 0, 2).reshape(routes)
    owner, within = owner.reshape(routes), within.reshape(routes)
    ahead = (owner - me) % count
    behind = (me - owner) % count
    pick = (jnp.arange(count * slots, dtype=i32)[None, :] == (ahead * slots + slot)[:, None]).astype(bf16)
    panel = (jnp.arange(count * panels, dtype=i32)[None, :] == (behind * panels + within)[:, None]).astype(bf16)
    base_rows = base.transpose(3, 2, 0, 1, 4).reshape(2, routes, hidden)

    tile = min(512, hidden)
    col_tiles = hidden // tile
    whole = lambda shape: pl.BlockSpec(shape, lambda n: (0,) * len(shape))
    col = lambda depth, p: pl.BlockSpec((depth, tile), lambda n, p=p: (0, p * col_tiles + n))
    out = pl.pallas_call(
        functools.partial(gate_kernel, count),
        out_shape=jax.ShapeDtypeStruct((routes, hidden), bf16),
        grid=(col_tiles,),
        in_specs=[smem, whole(pick.shape), whole(panel.shape)]
        + [pl.BlockSpec((2, routes, tile), lambda n: (0, 0, n))]
        + [col(count * panels, 0)] * 2
        + [col(slots, 0)] * count
        + [col(slots, 1)] * count,
        out_specs=col(routes, 0),
        compiler_params=params,
    )(group.reshape(1).astype(i32), pick, panel, base_rows, mine, other, *got, *got)
    return out.reshape(2, steps, rows, hidden).transpose(1, 2, 0, 3)


def solution(mesh):
    return jax.shard_map(
        on_device,
        mesh=mesh,
        in_specs=(
            P(None, ("groups", "dp"), ("expert", "pair")),
            P(None, ("groups", "dp"), None, None, ("expert", "pair")),
            P(None, ("groups", "dp"), None),
            P("dp", None, None, ("expert", "pair")),
            P("dp", None, None, ("expert", "pair")),
            P("dp", None, ("expert", "pair")),
        ),
        out_specs=P(None, ("groups", "dp"), None, ("expert", "pair")),
        check_vma=False,
    )
```

```python
import functools

import jax
import jax.numpy as jnp
from jax import lax
from jax.experimental import pallas as pl
from jax.experimental.pallas import tpu as pltpu
from jax.sharding import PartitionSpec as P

LANES = 128
ROW_TILE = 16
VMEM_LIMIT = 10 * 1024 * 1024
RELAY_VMEM_LIMIT = 24 * 1024 * 1024


def nt_dot(a, b):
    return lax.dot_general(a, b, (((1,), (1,)), ((), ())), preferred_element_type=jnp.float32)


def earlier_in_step(steps, rows):
    routes = 2 * steps * rows
    first = lax.broadcasted_iota(jnp.int32, (routes, routes), 0)
    second = lax.broadcasted_iota(jnp.int32, (routes, routes), 1)
    same = (first // rows) % steps == (second // rows) % steps
    return jnp.where(same & (first < second), 1.0, 0.0).astype(jnp.bfloat16)


def low_kernel(count, steps, rows, cap, slots, me_ref, down_ref, *refs):
    state_refs, (part_ref, info_ref) = refs[:count], refs[count:]
    panels, _, rank, width = down_ref.shape
    routes = 2 * steps * rows
    me = me_ref[0].astype(jnp.float32)
    down = down_ref[...].reshape(panels * 2 * rank, width)
    pick = jnp.where(
        lax.broadcasted_iota(jnp.int32, (8, LANES), 0) == lax.broadcasted_iota(jnp.int32, (8, LANES), 1), 1.0, 0.0
    ).astype(jnp.bfloat16)
    before = earlier_in_step(steps, rows)
    lane = lax.broadcasted_iota(jnp.int32, (1, routes), 1)
    step_of = ((lane // rows) % steps).astype(jnp.float32)
    panel_of = (lax.broadcasted_iota(jnp.int32, (panels * 2 * rank, routes), 0) // (2 * rank)).astype(jnp.float32)
    for s in range(count):
        one = state_refs[s][...]
        both = jnp.concatenate([one, one], axis=0)
        numbers = nt_dot(pick, both[:, width:])
        owner = jnp.where(lane < routes // 2, numbers[0:1], numbers[1:2])
        within = jnp.where(lane < routes // 2, numbers[2:3], numbers[3:4])
        mine = owner == me
        rank_of = jnp.dot(
            jnp.broadcast_to(jnp.where(mine, 1.0, 0.0), (8, routes)).astype(jnp.bfloat16),
            before,
            preferred_element_type=jnp.float32,
        )[0:1]
        slot = jnp.where(mine, step_of * cap + rank_of, -1.0)
        held = jnp.where(mine, within, -1.0)
        cols = pl.ds(s * routes, routes)
        info_ref[:, cols] = jnp.concatenate([slot, held, jnp.zeros((6, routes), jnp.float32)], axis=0)
        low = nt_dot(down, both[:, :width])
        low = jnp.where(panel_of == held, low, 0.0)
        part_ref[:, cols] = jnp.sum(low.reshape(panels, 2 * rank, routes), axis=0)


def delta_kernel(count, slots, info_ref, low_ref, up_ref, *refs):
    out_refs, (lhs_ref,) = refs[:count], refs[count:]
    panels, rank, tile = up_ref.shape
    routes = info_ref.shape[1] // count

    @pl.when((pl.program_id(0) == 0) & (pl.program_id(1) == 0))
    def _():
        low = low_ref[...].astype(jnp.bfloat16).astype(jnp.float32)
        panel_of = (lax.broadcasted_iota(jnp.int32, (panels * rank, routes), 0) // rank).astype(jnp.float32)
        slot_of = lax.broadcasted_iota(jnp.int32, (slots, routes), 0).astype(jnp.float32)
        for s in range(count):
            cols = slice(s * routes, (s + 1) * routes)
            slot, held = info_ref[0:1, cols], info_ref[1:2, cols]
            place = jnp.where(slot_of == slot, 1.0, 0.0).astype(jnp.bfloat16)
            for p in range(2):
                wide = jnp.concatenate([low[p * rank : (p + 1) * rank, cols]] * panels, axis=0)
                wide = jnp.where(panel_of == held, wide, 0.0).astype(jnp.bfloat16)
                lhs_ref[p, s * slots : (s + 1) * slots, :] = nt_dot(place, wide).astype(jnp.bfloat16)

    p = pl.program_id(0)
    up = up_ref[...].reshape(panels * rank, tile)
    delta = jnp.dot(lhs_ref[p], up, preferred_element_type=jnp.float32).astype(jnp.bfloat16)
    for s in range(count):
        out_refs[s][...] = delta[s * slots : (s + 1) * slots]


def gate_kernel(count, group_ref, pick_ref, panel_ref, base_ref, mine_ref, other_ref, *refs):
    blocks, out_ref = refs[: 2 * count], refs[2 * count]
    slots = blocks[0].shape[0]
    group = group_ref[0]
    adapted = []
    for p in range(2):
        delta = None
        for s in range(count):
            part = jnp.dot(
                pick_ref[:, s * slots : (s + 1) * slots],
                blocks[p * count + s][...],
                preferred_element_type=jnp.float32,
            )
            delta = part if delta is None else delta + part
        scales = jnp.where(group == p, mine_ref[...], other_ref[...])
        scale = jnp.dot(panel_ref[...], scales, preferred_element_type=jnp.float32)
        adapted.append(scale * (base_ref[p].astype(jnp.float32) + delta))
    gate, value = adapted
    out_ref[...] = (gate / (1.0 + jnp.exp(-gate)) * value).astype(out_ref.dtype)


CHUNK = 24
LAG = 2
GAP = LAG * CHUNK
ROW_STEP = 8
MAGNITUDE_ROWS = 16
QUEUE_ROWS = (144, 168, 192, 208)
LONG_ROWS = 208


def chunk_rows(total):
    return [(at, min(CHUNK, total - at)) for at in range(0, total, CHUNK)]


def right_layout(n):
    gap = float(GAP)
    zero = jnp.zeros_like(n[0][0])
    place = {}

    def put(link, j, d, first, split=None, second=None):
        place[link, j, d] = (first, split, second)

    put(0, 0, 3, zero)
    put(0, 0, 2, n[0][3])
    put(0, 0, 1, n[0][3] + n[0][2])
    end = n[0][3] + n[0][2] + n[0][1]
    early = jnp.maximum(jnp.minimum(n[1][2], gap - n[1][3]), 0.0)
    far = jnp.maximum(n[1][3], gap)
    late = far + n[0][3] + n[1][2] - early
    put(1, 1, 3, zero)
    put(1, 0, 3, far)
    put(1, 1, 2, n[1][3], early, far + n[0][3] - early)
    put(1, 0, 2, late)
    end = jnp.maximum(end, late + n[0][2])
    one = jnp.maximum(n[2][3] + float(MAGNITUDE_ROWS), gap)
    two = jnp.maximum(one + n[1][3], far + gap)
    put(2, 2, 3, zero, zero + float(GAP - MAGNITUDE_ROWS), zero + float(MAGNITUDE_ROWS))
    put(2, 1, 3, one)
    put(2, 0, 3, two)
    return place, jnp.maximum(end, two + n[0][3])


def relay_plan_kernel(steps, rows, panels, me_ref, part_ref, *refs):
    count = 4
    route_refs, outs = refs[:3], refs[3:]
    info_ref, longest_ref, forward_ref, first_ref, held_ref, arrive_ref, panel_ref = outs
    routes = 2 * steps * rows
    limit = forward_ref.shape[1]
    me = me_ref[0]
    before = jnp.where(
        lax.broadcasted_iota(jnp.int32, (routes, routes), 0) < lax.broadcasted_iota(jnp.int32, (routes, routes), 1),
        1.0,
        0.0,
    ).astype(jnp.bfloat16)
    owners = lax.broadcasted_iota(jnp.int32, (8, routes), 0).astype(jnp.float32)
    same = lax.broadcasted_iota(jnp.int32, (routes, routes), 0) == lax.broadcasted_iota(jnp.int32, (routes, routes), 1)
    same = jnp.where(same, 1.0, 0.0).astype(jnp.bfloat16)
    owner, order, tally = [], [], []
    info_ref[...] = jnp.full(info_ref.shape, -1.0, jnp.float32)
    came = [ref[...].astype(jnp.float32) for ref in route_refs]
    came = came[:2] + [came[2][: came[0].shape[0]], came[2][came[0].shape[0] :]]
    for s in range(count):
        numbers = sum(jnp.where((part_ref[0] ^ i) == s, came[i], 0.0) for i in range(count))
        owner.append(numbers[0:1])
        hits = jnp.where(owners == owner[s], 1.0, 0.0)
        ahead = jnp.dot(hits.astype(jnp.bfloat16), before, preferred_element_type=jnp.float32)
        order.append(jnp.sum(ahead * hits, axis=0, keepdims=True))
        tally.append(jnp.sum(hits, axis=1, keepdims=True))
        cols = slice(s * routes, (s + 1) * routes)
        info_ref[0:1, cols] = jnp.where(owner[s] == me.astype(jnp.float32), numbers[1:2], -1.0)
        if s == 0:
            within = numbers[1:2]

    def position(place, link, d, s, turned, owners_from, owners_to):
        found = jnp.full((1, routes), -1.0, jnp.float32)
        for j in range(owners_from, owners_to):
            first, split, second = place[link, j, d]
            at = first + order[s]
            if split is not None:
                at = jnp.where(order[s] < split, at, second + order[s])
            found = jnp.where(owner[s] == float(3 - j if turned else j), at, found)
        return found

    for case in range(count):

        @pl.when(me == case)
        def _():
            longest = None
            for turned in (False, True):
                node = 3 - case if turned else case
                n = [[None] * count for _ in range(count)]
                for j in range(count):
                    for d in range(count):
                        s = (case - d) % count
                        if turned:
                            n[3 - j][3 - d] = tally[s][j : j + 1]
                        else:
                            n[j][d] = tally[s][j : j + 1]
                place, end = right_layout(n)
                longest = end if longest is None else jnp.maximum(longest, end)
                row = 1 if turned == (case % 2 == 1) else 4
                for d in range(node + 1, count):
                    s = (case - (3 - d if turned else d)) % count
                    cols = slice(s * routes, (s + 1) * routes)
                    info_ref[row : row + 1, cols] = position(place, node, d, s, turned, node, node + 1)
                    if node > 0:
                        info_ref[row + 1 : row + 2, cols] = position(place, node, d, s, turned, 0, node)
                        info_ref[row + 2 : row + 3, cols] = position(place, node - 1, d, s, turned, 0, node)
                if node > 0:
                    arrive = 7 if turned == (case % 2 == 0) else 8
                    info_ref[arrive : arrive + 1, 0:routes] = position(place, node - 1, node, 0, turned, 0, node)
            longest_ref[...] = jnp.broadcast_to(longest, longest_ref.shape)
            blocks = [j ^ case for j in range(count)]
            if case in (0, count - 1):
                blocks = [block ^ 1 if block >= 2 else block for block in blocks]
            block_of = sum(jnp.where(owner[0] == float(j), float(blocks[j]), 0.0) for j in range(count))
            stands = block_of * panels + within
            depth = count * panels
            rows_of = lax.broadcasted_iota(jnp.int32, (depth, routes), 0).astype(jnp.float32)
            panel_ref[...] = nt_dot(same, jnp.where(rows_of == stands, 1.0, 0.0).astype(jnp.bfloat16)).astype(
                jnp.bfloat16
            )

    shape = forward_ref.shape[1:]
    same_half = lax.broadcasted_iota(jnp.int32, shape, 0) % 2 == lax.broadcasted_iota(jnp.int32, shape, 1) % 2
    for way in range(2):
        passed = nt_dot(placed(info_ref, 3 * way + 2, shape[0]), placed(info_ref, 3 * way + 3, shape[0]))
        forward_ref[way] = jnp.where(same_half, passed, 0.0).astype(jnp.bfloat16)
        for i in range(LAG):
            rows = pl.ds(2 * CHUNK * (2 * i + way), 2 * CHUNK)
            first_ref[rows, :] = placed(info_ref, 3 * way + 1, 2 * CHUNK, i * CHUNK)
        stands = placed(info_ref, 7 + way, shape[0])[:, :routes]
        stands = nt_dot(same, stands)
        for p in range(2):
            half = lax.broadcasted_iota(jnp.int32, stands.shape, 1) % 2 == p
            arrive_ref[way, p * routes : (p + 1) * routes, :] = jnp.where(half, stands, 0.0).astype(jnp.bfloat16)
    panel = jnp.broadcast_to(info_ref[0:1, :], (8, info_ref.shape[1])).astype(jnp.bfloat16)
    panel = nt_dot(first_ref[...], panel)[:, 0:1]
    half_row = lax.broadcasted_iota(jnp.int32, held_ref.shape, 0)
    lane = lax.broadcasted_iota(jnp.int32, held_ref.shape, 1)
    both = held_ref.shape[1] // panels
    here = ((lane % both) // (both // 2) == half_row % 2) & ((lane // both).astype(jnp.float32) == panel)
    held_ref[...] = jnp.where(here, 1.0, 0.0).astype(jnp.bfloat16)


def relay_load_kernel(down_ref, up_ref, down_out, up_out, sems):
    copies = [
        pltpu.make_async_copy(down_ref, down_out, sems.at[0]),
        pltpu.make_async_copy(up_ref, up_out, sems.at[1]),
    ]
    for copy in copies:
        copy.start()
    for copy in copies:
        copy.wait()


def relay_branch_kernel(totals, own_ref, other_ref, out_ref):
    longest = jnp.max(jnp.maximum(own_ref[...], other_ref[...]))
    out_ref[0] = sum((longest > float(total)).astype(jnp.int32) for total in totals[:-1])


def relay_low_kernel(info_ref, down_ref, half_ref, beside_ref, *refs):
    state_refs, (part_ref, join_ref) = refs[:-2], refs[-2:]
    panels, _, rank, width = down_ref.shape
    routes = info_ref.shape[1] // len(state_refs)
    down = down_ref[...].reshape(panels * 2 * rank, width)
    panel_of = (lax.broadcasted_iota(jnp.int32, (panels * 2 * rank, routes), 0) // (2 * rank)).astype(jnp.float32)
    join_ref[:panels, :] = beside_ref[...]
    join_ref[panels:, :] = half_ref[...]
    lows = nt_dot(down, jnp.concatenate([state_ref[...] for state_ref in state_refs], axis=0))
    rows = routes // 2
    for s in range(len(state_refs)):
        cols = slice(s * routes, (s + 1) * routes)
        low = lows[:, s * rows : (s + 1) * rows]
        low = jnp.where(panel_of == info_ref[0:1, cols], jnp.concatenate([low, low], axis=1), 0.0)
        part_ref[:, cols] = jnp.sum(low.reshape(panels, 2 * rank, routes), axis=0)


def summed_low(own_ref, core_ref, far_ref, diag_ref):
    low = (own_ref[...] + core_ref[...]) + (far_ref[...] + diag_ref[...])
    return low.astype(jnp.bfloat16).astype(jnp.float32)


def spread_low(low, info_ref, panels):
    held = info_ref[0:1, :]
    panel_of = lax.broadcasted_iota(jnp.int32, (panels * low.shape[0], held.shape[1]), 0) // low.shape[0]
    wide = jnp.concatenate([low] * panels, axis=0)
    return jnp.where(panel_of.astype(jnp.float32) == held, wide, 0.0).astype(jnp.bfloat16)


def placed(info_ref, row, half_rows, start=0):
    at = info_ref[row : row + 1, :] - float(start)
    slot_of = lax.broadcasted_iota(jnp.int32, (half_rows, at.shape[1]), 0) // 2
    return jnp.where(slot_of.astype(jnp.float32) == at, 1.0, 0.0).astype(jnp.bfloat16)


def low_rows(place, wide, panels, half_of):
    rows = nt_dot(place, wide)
    both = rows.shape[1] // panels
    own_half = half_of == (lax.broadcasted_iota(jnp.int32, rows.shape, 1) % both) // (both // 2)
    return jnp.where(own_half, rows, 0.0).astype(jnp.bfloat16)


def column_tiles(hidden, body, most=512):
    tile = min(most, hidden)

    @pl.loop(0, hidden // tile)
    def _(i):
        body(pl.ds(pl.multiple_of(i * tile, tile), tile))


def relay_first_kernel(
    index, first_ref, held_ref, own_ref, core_ref, far_ref, diag_ref, up_ref, *refs
):
    across_refs, (outer_ref, middle_ref, lhs_ref) = refs[:-3], refs[-3:]
    low = summed_low(own_ref, core_ref, far_ref, diag_ref).astype(jnp.bfloat16)
    here = slice(4 * CHUNK * index, 4 * CHUNK * (index + 1))
    rows = nt_dot(first_ref[here, :], low).astype(jnp.bfloat16)
    shape = (low.shape[0], held_ref.shape[1])
    source = lax.broadcasted_iota(jnp.int32, shape, 1) % shape[0]
    spread = jnp.where(lax.broadcasted_iota(jnp.int32, shape, 0) == source, 1.0, 0.0).astype(jnp.bfloat16)
    wide = jnp.dot(rows, spread, preferred_element_type=jnp.float32).astype(jnp.bfloat16)
    lhs_ref[...] = wide * held_ref[here, :]

    def body(cols):
        delta = jnp.dot(lhs_ref[...], up_ref[:, cols], preferred_element_type=jnp.float32).astype(jnp.bfloat16)
        outer_ref[:, cols] = delta[: 2 * CHUNK]
        middle_ref[:, cols] = delta[2 * CHUNK :]
        for across_ref in across_refs:
            at = 2 * CHUNK - across_ref.shape[0]
            outer_ref[at:, cols] = delta[at : 2 * CHUNK] + across_ref[:, cols]

    column_tiles(up_ref.shape[1], body, 1024)


def relay_rows_kernel(panels, info_ref, own_ref, core_ref, far_ref, diag_ref, lhs_ref, local_ref):
    wide = spread_low(summed_low(own_ref, core_ref, far_ref, diag_ref), info_ref, panels)
    for way in range(2):
        half_of = lax.broadcasted_iota(jnp.int32, lhs_ref.shape[1:], 0) % 2
        lhs_ref[way] = low_rows(placed(info_ref, 3 * way + 1, lhs_ref.shape[1]), wide, panels, half_of)
    routes = local_ref.shape[0] // 2
    shape = (2 * routes, routes)
    same = lax.broadcasted_iota(jnp.int32, shape, 0) % routes == lax.broadcasted_iota(jnp.int32, shape, 1)
    half_of = lax.broadcasted_iota(jnp.int32, local_ref.shape, 0) // routes
    local_ref[...] = low_rows(jnp.where(same, 1.0, 0.0).astype(jnp.bfloat16), wide[:, :routes], panels, half_of)


def relay_stack_kernel(me_ref, half_ref, beside_ref, across_ref, second_ref, out_ref):
    depth = half_ref.shape[0]
    out_ref[:depth] = half_ref[...]
    out_ref[depth : 2 * depth] = beside_ref[...]
    end = (me_ref[0] == 0) | (me_ref[0] == 3)

    @pl.when(end)
    def _():
        out_ref[2 * depth :] = second_ref[second_ref.shape[0] - 2 * depth :]

    @pl.when(jnp.logical_not(end))
    def _():
        out_ref[2 * depth :] = across_ref[...]


def relay_chunk_kernel(first, count, known, tile, lhs_ref, forward_ref, up_ref, *refs):
    came, out_refs = refs[:-2], refs[-2:]
    here = slice(2 * first, 2 * (first + count))

    def body(cols):
        lhs = jnp.concatenate([lhs_ref[0, here, :], lhs_ref[1, here, :]], axis=0)
        delta = jnp.dot(lhs, up_ref[:, cols], preferred_element_type=jnp.float32)
        for way in range(2):
            blocks = came[len(came) // 2 :] if way == 0 else came[: len(came) // 2]
            rows = jnp.concatenate([block[:, cols] for block in blocks], axis=0)
            passed = jnp.dot(forward_ref[way, here, : 2 * known], rows, preferred_element_type=jnp.float32)
            out_refs[way][:, cols] = (delta[2 * way * count : 2 * (way + 1) * count] + passed).astype(jnp.bfloat16)

    column_tiles(up_ref.shape[1], body, tile)


def relay_pick_kernel(known, tile, arrive_ref, local_ref, up_ref, *refs):
    came, out_ref = refs[:-1], refs[-1]
    routes = out_ref.shape[1]

    def body(cols):
        delta = jnp.dot(local_ref[...], up_ref[:, cols], preferred_element_type=jnp.float32)
        delta = delta.astype(jnp.bfloat16).astype(jnp.float32)
        for way in range(2):
            blocks = came[way * len(came) // 2 : (way + 1) * len(came) // 2]
            rows = jnp.concatenate([block[:, cols] for block in blocks], axis=0)
            delta += jnp.dot(arrive_ref[way, :, : 2 * known], rows, preferred_element_type=jnp.float32)
        for p in range(2):
            out_ref[p, :, cols] = delta[p * routes : (p + 1) * routes].astype(out_ref.dtype)

    column_tiles(up_ref.shape[1], body, tile)


def relay_gate_kernel(
    known, tile, group_ref, arrive_ref, panel_ref, mine_ref, other_ref, base_ref, early_ref, outer_ref, middle_ref, out_ref, pick_ref
):
    rows = out_ref.shape[0]
    routes = 2 * rows
    size = outer_ref.shape[0]
    group = group_ref[0]
    shape = (size, arrive_ref.shape[2])
    last = lax.broadcasted_iota(jnp.int32, shape, 1) == 2 * known + lax.broadcasted_iota(jnp.int32, shape, 0)
    last = jnp.where(last, 1.0, 0.0).astype(jnp.bfloat16)
    for way in range(2):
        pick_ref[:, way * size : (way + 1) * size] = nt_dot(arrive_ref[way], last).astype(jnp.bfloat16)

    def body(cols):
        scales = [
            jnp.dot(panel_ref[...], ref[:, cols], preferred_element_type=jnp.float32) for ref in (mine_ref, other_ref)
        ]
        late = jnp.concatenate([outer_ref[:, cols], middle_ref[:, cols]], axis=0)
        picked = jnp.dot(pick_ref[...], late, preferred_element_type=jnp.float32)
        adapted = []
        for p in range(2):
            delta = early_ref[p, :, cols].astype(jnp.float32) + picked[p * routes : (p + 1) * routes]
            scale = jnp.where(group == p, scales[0], scales[1])
            adapted.append(scale * (base_ref[p, :, cols].astype(jnp.float32) + delta))
        gate, value = adapted
        hidden = (gate / (1.0 + jnp.exp(-gate)) * value).astype(out_ref.dtype)
        for k in range(2):
            out_ref[:, k, cols] = hidden[k * rows : (k + 1) * rows]

    column_tiles(out_ref.shape[2], body, tile)


def relay_base_kernel(base_ref, out_ref):
    rows = base_ref.shape[0]

    def body(cols):
        for k in range(2):
            for p in range(2):
                out_ref[p, k * rows : (k + 1) * rows, cols] = base_ref[:, k, p, cols]

    column_tiles(base_ref.shape[3], body)


def relayed(seen, numbers, which, magnitude, base, down, up):
    count = 4
    me, group = lax.axis_index("dp"), lax.axis_index("groups")
    steps, rows, hidden = base.shape[0], base.shape[1], base.shape[-1]
    panels, _, rank, _ = down.shape
    routes = 2 * steps * rows
    cap = max(2, (5 * rows + count - 1) // count)
    limit = max(
        3 * steps * cap,
        2 * routes,
        GAP + 2 * steps * cap,
        GAP + routes,
        2 * GAP + steps * cap,
    )
    limit = -(-limit // ROW_STEP) * ROW_STEP
    bf16, f32, i32 = jnp.bfloat16, jnp.float32, jnp.int32
    vmem = pl.BlockSpec(memory_space=pltpu.VMEM)
    smem = pl.BlockSpec(memory_space=pltpu.SMEM)

    def kernel(body, inputs, outputs, scalars=0, specs=None, out_specs=None, scratch=(), cost=1):
        return pl.pallas_call(
            body,
            out_shape=[jax.ShapeDtypeStruct(shape, dtype) for shape, dtype in outputs],
            in_specs=specs or [smem] * scalars + [vmem] * (len(inputs) - scalars),
            out_specs=out_specs or [vmem] * len(outputs),
            scratch_shapes=list(scratch),
            compiler_params=pltpu.CompilerParams(vmem_limit_bytes=RELAY_VMEM_LIMIT),
            cost_estimate=pl.CostEstimate(flops=0, bytes_accessed=cost << 20, transcendentals=0),
        )(*inputs)

    base = base.reshape(steps * rows, 2, 2, hidden)
    outer_pairs, middle_pair = [(0, 1), (1, 0), (2, 3), (3, 2)], [(1, 2), (2, 1)]
    half = lax.dynamic_index_in_dim(magnitude, group, axis=1, keepdims=False)
    beside = lax.ppermute(half, "dp", outer_pairs)
    half, *numbers = lax.optimization_barrier((half, *numbers))
    info, longest, forward, first, held, arrive, panel = kernel(
        functools.partial(relay_plan_kernel, steps, rows, panels),
        [me.reshape(1).astype(i32), which.reshape(1).astype(i32), *numbers],
        [
            ((16, count * routes), f32),
            ((8, LANES), f32),
            ((2, 2 * limit, 2 * limit), bf16),
            ((4 * GAP, count * routes), bf16),
            ((4 * GAP, 2 * panels * rank), bf16),
            ((2, 2 * routes, 2 * limit), bf16),
            ((routes, count * panels), bf16),
        ],
        scalars=2,
        cost=128,
    )
    down, up, longest = lax.optimization_barrier((down, up, longest))
    down, up_rows = kernel(
        relay_load_kernel,
        [down, up.reshape(panels * 2 * rank, hidden)],
        [(down.shape, bf16), ((panels * 2 * rank, hidden), bf16)],
        specs=[pl.BlockSpec(memory_space=pltpu.HBM)] * 2,
        scratch=[pltpu.SemaphoreType.DMA((2,))],
    )
    totals = [total for total in QUEUE_ROWS if total < limit] + [limit]
    [branch] = kernel(
        functools.partial(relay_branch_kernel, totals),
        [longest, lax.ppermute(longest, "groups", [(0, 1), (1, 0)])],
        [((1,), i32)],
        out_specs=[smem],
    )

    down, up_rows, branch, *seen = lax.optimization_barrier((down, up_rows, branch, *seen))
    part, join = kernel(
        relay_low_kernel,
        [info, down, half, beside, *seen],
        [((2 * rank, count * routes), f32), ((2 * panels, hidden), bf16)],
    )
    lows = [part]
    for mask in (1, 2, 3):
        lows.append(lax.ppermute(part, ("expert", "pair"), [(i, i ^ mask) for i in range(4)]))
    across = lax.ppermute(join, "dp", middle_pair)

    def early(index, first, held, lows, up_rows, *across):
        return kernel(
            functools.partial(relay_first_kernel, index),
            [first, held, *lows, up_rows, *across],
            [((2 * CHUNK, hidden), bf16)] * 2,
            scratch=[pltpu.VMEM((4 * CHUNK, 2 * panels * rank), bf16)],
        )

    outer_first, middle_first = early(0, first, held, lows, up_rows)

    def flow(total, operands):
        (outer_first, middle_first, first, held, info, lows, forward, up_rows) = operands[:8]
        arrive, panel, base, half, beside, across = operands[8:]
        chunks = chunk_rows(total)
        tile = 512 if total < LONG_ROWS else 256
        got_outer, got_middle = [], []
        for k, (start, size) in enumerate(chunks):
            if k == 0:
                outer, middle = outer_first, middle_first
            elif k < LAG:
                outer, middle = early(k, first, held, lows, up_rows, across)
            else:
                if k == LAG:
                    info, base, *lows = lax.optimization_barrier((info, base, *lows, outer))[:-1]
                    [base_rows] = kernel(relay_base_kernel, [base], [((2, routes, hidden), bf16)])
                    base_rows, info = lax.optimization_barrier((base_rows, info))
                    lhs, local = kernel(
                        functools.partial(relay_rows_kernel, panels),
                        [info, *lows],
                        [((2, 2 * limit, 2 * panels * rank), bf16), ((2 * routes, 2 * panels * rank), bf16)],
                    )
                known = k + 1 - LAG
                outer, middle = kernel(
                    functools.partial(relay_chunk_kernel, start, size, chunks[known][0], tile),
                    [lhs, forward, up_rows, *got_outer[:known], *got_middle[:known]],
                    [((2 * size, hidden), bf16)] * 2,
                    cost=4 + k,
                )
            got_middle.append(lax.ppermute(middle, "dp", middle_pair))
            got_outer.append(lax.ppermute(outer, "dp", outer_pairs))
        [mine] = kernel(
            relay_stack_kernel,
            [me.reshape(1).astype(i32), half, beside, across, got_outer[1]],
            [((count * panels, hidden), bf16)],
            scalars=1,
        )
        other = lax.ppermute(mine, "groups", [(0, 1), (1, 0)])
        last, size = chunks[-1]
        [picked] = kernel(
            functools.partial(relay_pick_kernel, last, tile),
            [arrive, local, up_rows, *got_outer[:-1], *got_middle[:-1]],
            [((2, routes, hidden), bf16)],
        )
        picked, *final = lax.optimization_barrier((picked, got_outer[-1], got_middle[-1]))
        [out] = kernel(
            functools.partial(relay_gate_kernel, last, 4 * tile),
            [group.reshape(1).astype(i32), arrive, panel, mine, other, base_rows, picked, *final],
            [((steps * rows, 2, hidden), bf16)],
            scalars=1,
            scratch=[pltpu.VMEM((2 * routes, 4 * size), bf16)],
        )
        return out

    operands = (
        outer_first, middle_first, first, held, info, lows, forward, up_rows,
        arrive, panel, base, half, beside, across,
    )
    out = lax.switch(branch[0], [functools.partial(flow, total) for total in totals], operands)
    return out.reshape(steps, rows, 2, hidden)


def on_device(states, base, route_panels, down, up, magnitude):
    count = lax.axis_size("dp")
    me = lax.axis_index("dp")
    group = lax.axis_index("groups")
    steps, rows, width = states.shape
    hidden = base.shape[-1]
    panels, _, rank, _ = down.shape
    routes = 2 * steps * rows
    cap = max(2, (5 * rows + count - 1) // count)
    slots = -(-steps * cap // ROW_TILE) * ROW_TILE
    bf16, f32, i32 = jnp.bfloat16, jnp.float32, jnp.int32

    def turn(x, shift):
        return lax.ppermute(x, "dp", [(i, (i + shift) % count) for i in range(count)])

    if (count, lax.axis_size("expert"), lax.axis_size("pair")) == (4, 2, 2):
        one = states.reshape(steps * rows, width)
        which = 2 * lax.axis_index("expert") + lax.axis_index("pair")
        far = [(4 * d + e, 4 * ((d + e) % count) + e) for d in range(count) for e in range(4)]
        near = lax.ppermute(route_panels, ("dp", "expert", "pair"), far)
        one, near = lax.optimization_barrier((one, near))
        flat = near.transpose(2, 0, 1).reshape(1, routes)
        near = jnp.concatenate([flat // panels, flat % panels], axis=0).astype(bf16)
        near = jnp.pad(near, ((0, ROW_TILE - 2), (0, 0)))
        beside = lax.ppermute(near, "pair", [(0, 1), (1, 0)])
        both = lax.ppermute(jnp.concatenate([near, beside], axis=0), "expert", [(0, 1), (1, 0)])
        seen = [one] + [turn(one, s) for s in range(1, count)]
        return relayed(seen, [near, beside, both], which, magnitude, base, down, up)

    pairs = route_panels.reshape(steps * rows, 2)
    numbers = jnp.concatenate([pairs // panels, pairs % panels], axis=1).astype(bf16)
    sent = jnp.concatenate(
        [states.reshape(steps * rows, width), jnp.pad(numbers, ((0, 0), (0, LANES - 4)))], axis=1
    )
    seen = [sent] + [turn(sent, s) for s in range(1, count)]

    half = lax.dynamic_index_in_dim(magnitude, group, axis=1, keepdims=False)
    mine = jnp.concatenate([half] + [turn(half, s) for s in range(1, count)], axis=0)
    other = lax.ppermute(mine, "groups", [(0, 1), (1, 0)])

    vmem = pl.BlockSpec(memory_space=pltpu.VMEM)
    smem = pl.BlockSpec(memory_space=pltpu.SMEM)
    params = pltpu.CompilerParams(vmem_limit_bytes=VMEM_LIMIT)
    part, info = pl.pallas_call(
        functools.partial(low_kernel, count, steps, rows, cap, slots),
        out_shape=(
            jax.ShapeDtypeStruct((2 * rank, count * routes), f32),
            jax.ShapeDtypeStruct((8, count * routes), f32),
        ),
        in_specs=[smem] + [vmem] * (1 + count),
        out_specs=(vmem, vmem),
        compiler_params=params,
    )(me.reshape(1).astype(i32), down, *seen)

    low = lax.psum(part, ("expert", "pair"))

    tile = min(1024, hidden)
    col_tiles = hidden // tile
    whole = lambda shape: pl.BlockSpec(shape, lambda p, n: (0,) * len(shape))
    deltas = pl.pallas_call(
        functools.partial(delta_kernel, count, slots),
        out_shape=[jax.ShapeDtypeStruct((slots, 2 * hidden), bf16)] * count,
        grid=(2, col_tiles),
        in_specs=[whole(info.shape)]
        + [whole(low.shape)]
        + [pl.BlockSpec((panels, None, rank, tile), lambda p, n: (0, p, 0, n))],
        out_specs=[pl.BlockSpec((slots, tile), lambda p, n: (0, p * col_tiles + n))] * count,
        scratch_shapes=[pltpu.VMEM((2, count * slots, panels * rank), bf16)],
        compiler_params=params,
    )(info, low, up)
    got = [deltas[0]] + [turn(deltas[s], count - s) for s in range(1, count)]

    ordered = route_panels.transpose(2, 0, 1).reshape(2, steps, rows)
    owner, within = ordered // panels, ordered % panels
    by_step = owner.transpose(1, 0, 2).reshape(steps, 2 * rows)
    earlier = jnp.tril(jnp.ones((2 * rows, 2 * rows), jnp.bool_), -1)
    rank_of = jnp.sum((by_step[:, :, None] == by_step[:, None, :]) & earlier[None], axis=2, dtype=i32)
    slot = rank_of + jnp.arange(steps, dtype=i32)[:, None] * cap
    slot = slot.reshape(steps, 2, rows).transpose(1, 0, 2).reshape(routes)
    owner, within = owner.reshape(routes), within.reshape(routes)
    ahead = (owner - me) % count
    behind = (me - owner) % count
    pick = (jnp.arange(count * slots, dtype=i32)[None, :] == (ahead * slots + slot)[:, None]).astype(bf16)
    panel = (jnp.arange(count * panels, dtype=i32)[None, :] == (behind * panels + within)[:, None]).astype(bf16)
    base_rows = base.transpose(3, 2, 0, 1, 4).reshape(2, routes, hidden)

    tile = min(512, hidden)
    col_tiles = hidden // tile
    whole = lambda shape: pl.BlockSpec(shape, lambda n: (0,) * len(shape))
    col = lambda depth, p: pl.BlockSpec((depth, tile), lambda n, p=p: (0, p * col_tiles + n))
    out = pl.pallas_call(
        functools.partial(gate_kernel, count),
        out_shape=jax.ShapeDtypeStruct((routes, hidden), bf16),
        grid=(col_tiles,),
        in_specs=[smem, whole(pick.shape), whole(panel.shape)]
        + [pl.BlockSpec((2, routes, tile), lambda n: (0, 0, n))]
        + [col(count * panels, 0)] * 2
        + [col(slots, 0)] * count
        + [col(slots, 1)] * count,
        out_specs=col(routes, 0),
        compiler_params=params,
    )(group.reshape(1).astype(i32), pick, panel, base_rows, mine, other, *got, *got)
    return out.reshape(2, steps, rows, hidden).transpose(1, 2, 0, 3)


def solution(mesh):
    return jax.shard_map(
        on_device,
        mesh=mesh,
        in_specs=(
            P(None, ("groups", "dp"), ("expert", "pair")),
            P(None, ("groups", "dp"), None, None, ("expert", "pair")),
            P(None, ("groups", "dp"), None),
            P("dp", None, None, ("expert", "pair")),
            P("dp", None, None, ("expert", "pair")),
            P("dp", None, ("expert", "pair")),
        ),
        out_specs=P(None, ("groups", "dp"), None, ("expert", "pair")),
        check_vma=False,
    )
```

```python
import functools

import jax
import jax.numpy as jnp
from jax import lax
from jax.experimental import pallas as pl
from jax.experimental.pallas import tpu as pltpu
from jax.sharding import PartitionSpec as P

LANES = 128
ROW_TILE = 16
VMEM_LIMIT = 10 * 1024 * 1024
RELAY_VMEM_LIMIT = 24 * 1024 * 1024


def nt_dot(a, b):
    return lax.dot_general(a, b, (((1,), (1,)), ((), ())), preferred_element_type=jnp.float32)


def earlier_in_step(steps, rows):
    routes = 2 * steps * rows
    first = lax.broadcasted_iota(jnp.int32, (routes, routes), 0)
    second = lax.broadcasted_iota(jnp.int32, (routes, routes), 1)
    same = (first // rows) % steps == (second // rows) % steps
    return jnp.where(same & (first < second), 1.0, 0.0).astype(jnp.bfloat16)


def low_kernel(count, steps, rows, cap, slots, me_ref, down_ref, *refs):
    state_refs, (part_ref, info_ref) = refs[:count], refs[count:]
    panels, _, rank, width = down_ref.shape
    routes = 2 * steps * rows
    me = me_ref[0].astype(jnp.float32)
    down = down_ref[...].reshape(panels * 2 * rank, width)
    pick = jnp.where(
        lax.broadcasted_iota(jnp.int32, (8, LANES), 0) == lax.broadcasted_iota(jnp.int32, (8, LANES), 1), 1.0, 0.0
    ).astype(jnp.bfloat16)
    before = earlier_in_step(steps, rows)
    lane = lax.broadcasted_iota(jnp.int32, (1, routes), 1)
    step_of = ((lane // rows) % steps).astype(jnp.float32)
    panel_of = (lax.broadcasted_iota(jnp.int32, (panels * 2 * rank, routes), 0) // (2 * rank)).astype(jnp.float32)
    for s in range(count):
        one = state_refs[s][...]
        both = jnp.concatenate([one, one], axis=0)
        numbers = nt_dot(pick, both[:, width:])
        owner = jnp.where(lane < routes // 2, numbers[0:1], numbers[1:2])
        within = jnp.where(lane < routes // 2, numbers[2:3], numbers[3:4])
        mine = owner == me
        rank_of = jnp.dot(
            jnp.broadcast_to(jnp.where(mine, 1.0, 0.0), (8, routes)).astype(jnp.bfloat16),
            before,
            preferred_element_type=jnp.float32,
        )[0:1]
        slot = jnp.where(mine, step_of * cap + rank_of, -1.0)
        held = jnp.where(mine, within, -1.0)
        cols = pl.ds(s * routes, routes)
        info_ref[:, cols] = jnp.concatenate([slot, held, jnp.zeros((6, routes), jnp.float32)], axis=0)
        low = nt_dot(down, both[:, :width])
        low = jnp.where(panel_of == held, low, 0.0)
        part_ref[:, cols] = jnp.sum(low.reshape(panels, 2 * rank, routes), axis=0)


def delta_kernel(count, slots, info_ref, low_ref, up_ref, *refs):
    out_refs, (lhs_ref,) = refs[:count], refs[count:]
    panels, rank, tile = up_ref.shape
    routes = info_ref.shape[1] // count

    @pl.when((pl.program_id(0) == 0) & (pl.program_id(1) == 0))
    def _():
        low = low_ref[...].astype(jnp.bfloat16).astype(jnp.float32)
        panel_of = (lax.broadcasted_iota(jnp.int32, (panels * rank, routes), 0) // rank).astype(jnp.float32)
        slot_of = lax.broadcasted_iota(jnp.int32, (slots, routes), 0).astype(jnp.float32)
        for s in range(count):
            cols = slice(s * routes, (s + 1) * routes)
            slot, held = info_ref[0:1, cols], info_ref[1:2, cols]
            place = jnp.where(slot_of == slot, 1.0, 0.0).astype(jnp.bfloat16)
            for p in range(2):
                wide = jnp.concatenate([low[p * rank : (p + 1) * rank, cols]] * panels, axis=0)
                wide = jnp.where(panel_of == held, wide, 0.0).astype(jnp.bfloat16)
                lhs_ref[p, s * slots : (s + 1) * slots, :] = nt_dot(place, wide).astype(jnp.bfloat16)

    p = pl.program_id(0)
    up = up_ref[...].reshape(panels * rank, tile)
    delta = jnp.dot(lhs_ref[p], up, preferred_element_type=jnp.float32).astype(jnp.bfloat16)
    for s in range(count):
        out_refs[s][...] = delta[s * slots : (s + 1) * slots]


def gate_kernel(count, group_ref, pick_ref, panel_ref, base_ref, mine_ref, other_ref, *refs):
    blocks, out_ref = refs[: 2 * count], refs[2 * count]
    slots = blocks[0].shape[0]
    group = group_ref[0]
    adapted = []
    for p in range(2):
        delta = None
        for s in range(count):
            part = jnp.dot(
                pick_ref[:, s * slots : (s + 1) * slots],
                blocks[p * count + s][...],
                preferred_element_type=jnp.float32,
            )
            delta = part if delta is None else delta + part
        scales = jnp.where(group == p, mine_ref[...], other_ref[...])
        scale = jnp.dot(panel_ref[...], scales, preferred_element_type=jnp.float32)
        adapted.append(scale * (base_ref[p].astype(jnp.float32) + delta))
    gate, value = adapted
    out_ref[...] = (gate / (1.0 + jnp.exp(-gate)) * value).astype(out_ref.dtype)


CHUNK = 24
LAG = 2
GAP = LAG * CHUNK
ROW_STEP = 8
MAGNITUDE_ROWS = 16
QUEUE_ROWS = (160, 168, 184, 208)
LONG_ROWS = 208


def chunk_rows(total):
    return [(at, min(CHUNK, total - at)) for at in range(0, total, CHUNK)]


def right_layout(n):
    gap = float(GAP)
    zero = jnp.zeros_like(n[0][0])
    place = {}

    def put(link, j, d, first, split=None, second=None):
        place[link, j, d] = (first, split, second)

    put(0, 0, 3, zero)
    put(0, 0, 2, n[0][3])
    put(0, 0, 1, n[0][3] + n[0][2])
    end = n[0][3] + n[0][2] + n[0][1]
    early = jnp.maximum(jnp.minimum(n[1][2], gap - n[1][3]), 0.0)
    far = jnp.maximum(n[1][3], gap)
    late = far + n[0][3] + n[1][2] - early
    put(1, 1, 3, zero)
    put(1, 0, 3, far)
    put(1, 1, 2, n[1][3], early, far + n[0][3] - early)
    put(1, 0, 2, late)
    end = jnp.maximum(end, late + n[0][2])
    one = jnp.maximum(n[2][3] + float(MAGNITUDE_ROWS), gap)
    two = jnp.maximum(one + n[1][3], far + gap)
    put(2, 2, 3, zero, zero + float(GAP - MAGNITUDE_ROWS), zero + float(MAGNITUDE_ROWS))
    put(2, 1, 3, one)
    put(2, 0, 3, two)
    return place, jnp.maximum(end, two + n[0][3])


def relay_plan_kernel(steps, rows, panels, me_ref, part_ref, *refs):
    count = 4
    route_refs, outs = refs[:3], refs[3:]
    info_ref, longest_ref, forward_ref, first_ref, held_ref, arrive_ref, panel_ref = outs
    routes = 2 * steps * rows
    limit = forward_ref.shape[1]
    me = me_ref[0]
    before = jnp.where(
        lax.broadcasted_iota(jnp.int32, (routes, routes), 0) < lax.broadcasted_iota(jnp.int32, (routes, routes), 1),
        1.0,
        0.0,
    ).astype(jnp.bfloat16)
    owners = lax.broadcasted_iota(jnp.int32, (8, routes), 0).astype(jnp.float32)
    same = lax.broadcasted_iota(jnp.int32, (routes, routes), 0) == lax.broadcasted_iota(jnp.int32, (routes, routes), 1)
    same = jnp.where(same, 1.0, 0.0).astype(jnp.bfloat16)
    owner, order, tally = [], [], []
    info_ref[...] = jnp.full(info_ref.shape, -1.0, jnp.float32)
    came = [ref[...].astype(jnp.float32) for ref in route_refs]
    came = came[:2] + [came[2][: came[0].shape[0]], came[2][came[0].shape[0] :]]
    for s in range(count):
        numbers = sum(jnp.where((part_ref[0] ^ i) == s, came[i], 0.0) for i in range(count))
        owner.append(numbers[0:1])
        hits = jnp.where(owners == owner[s], 1.0, 0.0)
        ahead = jnp.dot(hits.astype(jnp.bfloat16), before, preferred_element_type=jnp.float32)
        order.append(jnp.sum(ahead * hits, axis=0, keepdims=True))
        tally.append(jnp.sum(hits, axis=1, keepdims=True))
        cols = slice(s * routes, (s + 1) * routes)
        info_ref[0:1, cols] = jnp.where(owner[s] == me.astype(jnp.float32), numbers[1:2], -1.0)
        if s == 0:
            within = numbers[1:2]

    def position(place, link, d, s, turned, owners_from, owners_to):
        found = jnp.full((1, routes), -1.0, jnp.float32)
        for j in range(owners_from, owners_to):
            first, split, second = place[link, j, d]
            at = first + order[s]
            if split is not None:
                at = jnp.where(order[s] < split, at, second + order[s])
            found = jnp.where(owner[s] == float(3 - j if turned else j), at, found)
        return found

    for case in range(count):

        @pl.when(me == case)
        def _():
            longest = None
            for turned in (False, True):
                node = 3 - case if turned else case
                n = [[None] * count for _ in range(count)]
                for j in range(count):
                    for d in range(count):
                        s = (case - d) % count
                        if turned:
                            n[3 - j][3 - d] = tally[s][j : j + 1]
                        else:
                            n[j][d] = tally[s][j : j + 1]
                place, end = right_layout(n)
                longest = end if longest is None else jnp.maximum(longest, end)
                row = 1 if turned == (case % 2 == 1) else 4
                for d in range(node + 1, count):
                    s = (case - (3 - d if turned else d)) % count
                    cols = slice(s * routes, (s + 1) * routes)
                    info_ref[row : row + 1, cols] = position(place, node, d, s, turned, node, node + 1)
                    if node > 0:
                        info_ref[row + 1 : row + 2, cols] = position(place, node, d, s, turned, 0, node)
                        info_ref[row + 2 : row + 3, cols] = position(place, node - 1, d, s, turned, 0, node)
                if node > 0:
                    arrive = 7 if turned == (case % 2 == 0) else 8
                    info_ref[arrive : arrive + 1, 0:routes] = position(place, node - 1, node, 0, turned, 0, node)
            longest_ref[...] = jnp.broadcast_to(longest, longest_ref.shape)
            blocks = [j ^ case for j in range(count)]
            if case in (0, count - 1):
                blocks = [block ^ 1 if block >= 2 else block for block in blocks]
            block_of = sum(jnp.where(owner[0] == float(j), float(blocks[j]), 0.0) for j in range(count))
            stands = block_of * panels + within
            depth = count * panels
            rows_of = lax.broadcasted_iota(jnp.int32, (depth, routes), 0).astype(jnp.float32)
            panel_ref[...] = nt_dot(same, jnp.where(rows_of == stands, 1.0, 0.0).astype(jnp.bfloat16)).astype(
                jnp.bfloat16
            )

    shape = forward_ref.shape[1:]
    same_half = lax.broadcasted_iota(jnp.int32, shape, 0) % 2 == lax.broadcasted_iota(jnp.int32, shape, 1) % 2
    for way in range(2):
        passed = nt_dot(placed(info_ref, 3 * way + 2, shape[0]), placed(info_ref, 3 * way + 3, shape[0]))
        forward_ref[way] = jnp.where(same_half, passed, 0.0).astype(jnp.bfloat16)
        for i in range(LAG):
            rows = pl.ds(2 * CHUNK * (2 * i + way), 2 * CHUNK)
            first_ref[rows, :] = placed(info_ref, 3 * way + 1, 2 * CHUNK, i * CHUNK)
        stands = placed(info_ref, 7 + way, shape[0])[:, :routes]
        stands = nt_dot(same, stands)
        for p in range(2):
            half = lax.broadcasted_iota(jnp.int32, stands.shape, 1) % 2 == p
            arrive_ref[way, p * routes : (p + 1) * routes, :] = jnp.where(half, stands, 0.0).astype(jnp.bfloat16)
    panel = jnp.broadcast_to(info_ref[0:1, :], (8, info_ref.shape[1])).astype(jnp.bfloat16)
    panel = nt_dot(first_ref[...], panel)[:, 0:1]
    half_row = lax.broadcasted_iota(jnp.int32, held_ref.shape, 0)
    lane = lax.broadcasted_iota(jnp.int32, held_ref.shape, 1)
    both = held_ref.shape[1] // panels
    here = ((lane % both) // (both // 2) == half_row % 2) & ((lane // both).astype(jnp.float32) == panel)
    held_ref[...] = jnp.where(here, 1.0, 0.0).astype(jnp.bfloat16)


def relay_load_kernel(down_ref, up_ref, down_out, up_out, sems):
    copies = [
        pltpu.make_async_copy(down_ref, down_out, sems.at[0]),
        pltpu.make_async_copy(up_ref, up_out, sems.at[1]),
    ]
    for copy in copies:
        copy.start()
    for copy in copies:
        copy.wait()


def relay_branch_kernel(totals, own_ref, other_ref, out_ref):
    longest = jnp.max(jnp.maximum(own_ref[...], other_ref[...]))
    out_ref[0] = sum((longest > float(total)).astype(jnp.int32) for total in totals[:-1])


def relay_low_kernel(info_ref, down_ref, half_ref, beside_ref, *refs):
    state_refs, (part_ref, join_ref) = refs[:-2], refs[-2:]
    panels, _, rank, width = down_ref.shape
    routes = info_ref.shape[1] // len(state_refs)
    down = down_ref[...].reshape(panels * 2 * rank, width)
    panel_of = (lax.broadcasted_iota(jnp.int32, (panels * 2 * rank, routes), 0) // (2 * rank)).astype(jnp.float32)
    join_ref[:panels, :] = beside_ref[...]
    join_ref[panels:, :] = half_ref[...]
    lows = nt_dot(down, jnp.concatenate([state_ref[...] for state_ref in state_refs], axis=0))
    rows = routes // 2
    for s in range(len(state_refs)):
        cols = slice(s * routes, (s + 1) * routes)
        low = lows[:, s * rows : (s + 1) * rows]
        low = jnp.where(panel_of == info_ref[0:1, cols], jnp.concatenate([low, low], axis=1), 0.0)
        part_ref[:, cols] = jnp.sum(low.reshape(panels, 2 * rank, routes), axis=0)


def summed_low(own_ref, core_ref, far_ref, diag_ref):
    low = (own_ref[...] + core_ref[...]) + (far_ref[...] + diag_ref[...])
    return low.astype(jnp.bfloat16).astype(jnp.float32)


def spread_low(low, info_ref, panels):
    held = info_ref[0:1, :]
    panel_of = lax.broadcasted_iota(jnp.int32, (panels * low.shape[0], held.shape[1]), 0) // low.shape[0]
    wide = jnp.concatenate([low] * panels, axis=0)
    return jnp.where(panel_of.astype(jnp.float32) == held, wide, 0.0).astype(jnp.bfloat16)


def placed(info_ref, row, half_rows, start=0):
    at = info_ref[row : row + 1, :] - float(start)
    slot_of = lax.broadcasted_iota(jnp.int32, (half_rows, at.shape[1]), 0) // 2
    return jnp.where(slot_of.astype(jnp.float32) == at, 1.0, 0.0).astype(jnp.bfloat16)


def low_rows(place, wide, panels, half_of):
    rows = nt_dot(place, wide)
    both = rows.shape[1] // panels
    own_half = half_of == (lax.broadcasted_iota(jnp.int32, rows.shape, 1) % both) // (both // 2)
    return jnp.where(own_half, rows, 0.0).astype(jnp.bfloat16)


def column_tiles(hidden, body, most=512):
    tile = min(most, hidden)

    @pl.loop(0, hidden // tile)
    def _(i):
        body(pl.ds(pl.multiple_of(i * tile, tile), tile))


def relay_first_kernel(
    index, first_ref, held_ref, own_ref, core_ref, far_ref, diag_ref, up_ref, *refs
):
    across_refs, (outer_ref, middle_ref, lhs_ref) = refs[:-3], refs[-3:]
    low = summed_low(own_ref, core_ref, far_ref, diag_ref).astype(jnp.bfloat16)
    here = slice(4 * CHUNK * index, 4 * CHUNK * (index + 1))
    rows = nt_dot(first_ref[here, :], low).astype(jnp.bfloat16)
    shape = (low.shape[0], held_ref.shape[1])
    source = lax.broadcasted_iota(jnp.int32, shape, 1) % shape[0]
    spread = jnp.where(lax.broadcasted_iota(jnp.int32, shape, 0) == source, 1.0, 0.0).astype(jnp.bfloat16)
    wide = jnp.dot(rows, spread, preferred_element_type=jnp.float32).astype(jnp.bfloat16)
    lhs_ref[...] = wide * held_ref[here, :]

    def body(cols):
        delta = jnp.dot(lhs_ref[...], up_ref[:, cols], preferred_element_type=jnp.float32).astype(jnp.bfloat16)
        outer_ref[:, cols] = delta[: 2 * CHUNK]
        middle_ref[:, cols] = delta[2 * CHUNK :]
        for across_ref in across_refs:
            at = 2 * CHUNK - across_ref.shape[0]
            outer_ref[at:, cols] = delta[at : 2 * CHUNK] + across_ref[:, cols]

    column_tiles(up_ref.shape[1], body, 1024)


def relay_rows_kernel(panels, info_ref, own_ref, core_ref, far_ref, diag_ref, lhs_ref, local_ref):
    wide = spread_low(summed_low(own_ref, core_ref, far_ref, diag_ref), info_ref, panels)
    for way in range(2):
        half_of = lax.broadcasted_iota(jnp.int32, lhs_ref.shape[1:], 0) % 2
        lhs_ref[way] = low_rows(placed(info_ref, 3 * way + 1, lhs_ref.shape[1]), wide, panels, half_of)
    routes = local_ref.shape[0] // 2
    shape = (2 * routes, routes)
    same = lax.broadcasted_iota(jnp.int32, shape, 0) % routes == lax.broadcasted_iota(jnp.int32, shape, 1)
    half_of = lax.broadcasted_iota(jnp.int32, local_ref.shape, 0) // routes
    local_ref[...] = low_rows(jnp.where(same, 1.0, 0.0).astype(jnp.bfloat16), wide[:, :routes], panels, half_of)


def relay_stack_kernel(me_ref, half_ref, beside_ref, across_ref, second_ref, out_ref):
    depth = half_ref.shape[0]
    out_ref[:depth] = half_ref[...]
    out_ref[depth : 2 * depth] = beside_ref[...]
    end = (me_ref[0] == 0) | (me_ref[0] == 3)

    @pl.when(end)
    def _():
        out_ref[2 * depth :] = second_ref[second_ref.shape[0] - 2 * depth :]

    @pl.when(jnp.logical_not(end))
    def _():
        out_ref[2 * depth :] = across_ref[...]


def relay_chunk_kernel(first, count, known, tile, lhs_ref, forward_ref, up_ref, *refs):
    came, out_refs = refs[:-2], refs[-2:]
    here = slice(2 * first, 2 * (first + count))

    def body(cols):
        lhs = jnp.concatenate([lhs_ref[0, here, :], lhs_ref[1, here, :]], axis=0)
        delta = jnp.dot(lhs, up_ref[:, cols], preferred_element_type=jnp.float32)
        for way in range(2):
            blocks = came[len(came) // 2 :] if way == 0 else came[: len(came) // 2]
            rows = jnp.concatenate([block[:, cols] for block in blocks], axis=0)
            passed = jnp.dot(forward_ref[way, here, : 2 * known], rows, preferred_element_type=jnp.float32)
            out_refs[way][:, cols] = (delta[2 * way * count : 2 * (way + 1) * count] + passed).astype(jnp.bfloat16)

    column_tiles(up_ref.shape[1], body, tile)


def relay_pick_kernel(known, tile, arrive_ref, local_ref, up_ref, *refs):
    came, out_ref = refs[:-1], refs[-1]
    routes = out_ref.shape[1]

    def body(cols):
        delta = jnp.dot(local_ref[...], up_ref[:, cols], preferred_element_type=jnp.float32)
        delta = delta.astype(jnp.bfloat16).astype(jnp.float32)
        for way in range(2):
            blocks = came[way * len(came) // 2 : (way + 1) * len(came) // 2]
            rows = jnp.concatenate([block[:, cols] for block in blocks], axis=0)
            delta += jnp.dot(arrive_ref[way, :, : 2 * known], rows, preferred_element_type=jnp.float32)
        for p in range(2):
            out_ref[p, :, cols] = delta[p * routes : (p + 1) * routes].astype(out_ref.dtype)

    column_tiles(up_ref.shape[1], body, tile)


def relay_gate_kernel(
    known, group_ref, arrive_ref, panel_ref, mine_ref, other_ref, base_ref, early_ref, outer_ref, middle_ref, out_ref, pick_ref
):
    rows = out_ref.shape[0]
    routes = 2 * rows
    size = outer_ref.shape[0]
    group = group_ref[0]
    shape = (size, arrive_ref.shape[2])
    last = lax.broadcasted_iota(jnp.int32, shape, 1) == 2 * known + lax.broadcasted_iota(jnp.int32, shape, 0)
    last = jnp.where(last, 1.0, 0.0).astype(jnp.bfloat16)
    for way in range(2):
        pick_ref[:, way * size : (way + 1) * size] = nt_dot(arrive_ref[way], last).astype(jnp.bfloat16)

    def body(cols):
        late = jnp.concatenate([outer_ref[:, cols], middle_ref[:, cols]], axis=0)
        picked = jnp.dot(pick_ref[...], late, preferred_element_type=jnp.float32)
        adapted = []
        for p in range(2):
            delta = early_ref[p, :, cols].astype(jnp.float32) + picked[p * routes : (p + 1) * routes]
            scales = jnp.where(group == p, mine_ref[:, cols], other_ref[:, cols])
            scale = jnp.dot(panel_ref[...], scales, preferred_element_type=jnp.float32)
            adapted.append(scale * (base_ref[p, :, cols].astype(jnp.float32) + delta))
        gate, value = adapted
        hidden = (gate / (1.0 + jnp.exp(-gate)) * value).astype(out_ref.dtype)
        for k in range(2):
            out_ref[:, k, cols] = hidden[k * rows : (k + 1) * rows]

    column_tiles(out_ref.shape[2], body, 1024)


def relay_base_kernel(base_ref, out_ref):
    rows = base_ref.shape[0]

    def body(cols):
        for k in range(2):
            for p in range(2):
                out_ref[p, k * rows : (k + 1) * rows, cols] = base_ref[:, k, p, cols]

    column_tiles(base_ref.shape[3], body)


def relayed(seen, numbers, which, magnitude, base, down, up):
    count = 4
    me, group = lax.axis_index("dp"), lax.axis_index("groups")
    steps, rows, hidden = base.shape[0], base.shape[1], base.shape[-1]
    panels, _, rank, _ = down.shape
    routes = 2 * steps * rows
    cap = max(2, (5 * rows + count - 1) // count)
    limit = max(
        3 * steps * cap,
        2 * routes,
        GAP + 2 * steps * cap,
        GAP + routes,
        2 * GAP + steps * cap,
    )
    limit = -(-limit // ROW_STEP) * ROW_STEP
    bf16, f32, i32 = jnp.bfloat16, jnp.float32, jnp.int32
    vmem = pl.BlockSpec(memory_space=pltpu.VMEM)
    smem = pl.BlockSpec(memory_space=pltpu.SMEM)

    def kernel(body, inputs, outputs, scalars=0, specs=None, out_specs=None, scratch=(), cost=1):
        return pl.pallas_call(
            body,
            out_shape=[jax.ShapeDtypeStruct(shape, dtype) for shape, dtype in outputs],
            in_specs=specs or [smem] * scalars + [vmem] * (len(inputs) - scalars),
            out_specs=out_specs or [vmem] * len(outputs),
            scratch_shapes=list(scratch),
            compiler_params=pltpu.CompilerParams(vmem_limit_bytes=RELAY_VMEM_LIMIT),
            cost_estimate=pl.CostEstimate(flops=0, bytes_accessed=cost << 20, transcendentals=0),
        )(*inputs)

    base = base.reshape(steps * rows, 2, 2, hidden)
    outer_pairs, middle_pair = [(0, 1), (1, 0), (2, 3), (3, 2)], [(1, 2), (2, 1)]
    half = lax.dynamic_index_in_dim(magnitude, group, axis=1, keepdims=False)
    beside = lax.ppermute(half, "dp", outer_pairs)
    half, *numbers = lax.optimization_barrier((half, *numbers))
    info, longest, forward, first, held, arrive, panel = kernel(
        functools.partial(relay_plan_kernel, steps, rows, panels),
        [me.reshape(1).astype(i32), which.reshape(1).astype(i32), *numbers],
        [
            ((16, count * routes), f32),
            ((8, LANES), f32),
            ((2, 2 * limit, 2 * limit), bf16),
            ((4 * GAP, count * routes), bf16),
            ((4 * GAP, 2 * panels * rank), bf16),
            ((2, 2 * routes, 2 * limit), bf16),
            ((routes, count * panels), bf16),
        ],
        scalars=2,
        cost=128,
    )
    down, up, longest = lax.optimization_barrier((down, up, longest))
    down, up_rows = kernel(
        relay_load_kernel,
        [down, up.reshape(panels * 2 * rank, hidden)],
        [(down.shape, bf16), ((panels * 2 * rank, hidden), bf16)],
        specs=[pl.BlockSpec(memory_space=pltpu.HBM)] * 2,
        scratch=[pltpu.SemaphoreType.DMA((2,))],
    )
    totals = [total for total in QUEUE_ROWS if total < limit] + [limit]
    [branch] = kernel(
        functools.partial(relay_branch_kernel, totals),
        [longest, lax.ppermute(longest, "groups", [(0, 1), (1, 0)])],
        [((1,), i32)],
        out_specs=[smem],
    )

    down, up_rows, branch, *seen = lax.optimization_barrier((down, up_rows, branch, *seen))
    part, join = kernel(
        relay_low_kernel,
        [info, down, half, beside, *seen],
        [((2 * rank, count * routes), f32), ((2 * panels, hidden), bf16)],
    )
    lows = [part]
    for mask in (1, 2, 3):
        lows.append(lax.ppermute(part, ("expert", "pair"), [(i, i ^ mask) for i in range(4)]))
    across = lax.ppermute(join, "dp", middle_pair)

    def early(index, first, held, lows, up_rows, *across):
        return kernel(
            functools.partial(relay_first_kernel, index),
            [first, held, *lows, up_rows, *across],
            [((2 * CHUNK, hidden), bf16)] * 2,
            scratch=[pltpu.VMEM((4 * CHUNK, 2 * panels * rank), bf16)],
        )

    outer_first, middle_first = early(0, first, held, lows, up_rows)

    def flow(total, operands):
        (outer_first, middle_first, first, held, info, lows, forward, up_rows) = operands[:8]
        arrive, panel, base, half, beside, across = operands[8:]
        chunks = chunk_rows(total)
        tile = 512 if total < LONG_ROWS else 256
        got_outer, got_middle = [], []
        for k, (start, size) in enumerate(chunks):
            if k == 0:
                outer, middle = outer_first, middle_first
            elif k < LAG:
                outer, middle = early(k, first, held, lows, up_rows, across)
            else:
                if k == LAG:
                    info, base, *lows = lax.optimization_barrier((info, base, *lows, outer))[:-1]
                    [base_rows] = kernel(relay_base_kernel, [base], [((2, routes, hidden), bf16)])
                    base_rows, info = lax.optimization_barrier((base_rows, info))
                    lhs, local = kernel(
                        functools.partial(relay_rows_kernel, panels),
                        [info, *lows],
                        [((2, 2 * limit, 2 * panels * rank), bf16), ((2 * routes, 2 * panels * rank), bf16)],
                    )
                known = k + 1 - LAG
                outer, middle = kernel(
                    functools.partial(relay_chunk_kernel, start, size, chunks[known][0], tile),
                    [lhs, forward, up_rows, *got_outer[:known], *got_middle[:known]],
                    [((2 * size, hidden), bf16)] * 2,
                    cost=4 + k,
                )
            got_middle.append(lax.ppermute(middle, "dp", middle_pair))
            got_outer.append(lax.ppermute(outer, "dp", outer_pairs))
        [mine] = kernel(
            relay_stack_kernel,
            [me.reshape(1).astype(i32), half, beside, across, got_outer[1]],
            [((count * panels, hidden), bf16)],
            scalars=1,
        )
        other = lax.ppermute(mine, "groups", [(0, 1), (1, 0)])
        last, size = chunks[-1]
        [picked] = kernel(
            functools.partial(relay_pick_kernel, last, tile),
            [arrive, local, up_rows, *got_outer[:-1], *got_middle[:-1]],
            [((2, routes, hidden), bf16)],
        )
        picked, *final = lax.optimization_barrier((picked, got_outer[-1], got_middle[-1]))
        [out] = kernel(
            functools.partial(relay_gate_kernel, last),
            [group.reshape(1).astype(i32), arrive, panel, mine, other, base_rows, picked, *final],
            [((steps * rows, 2, hidden), bf16)],
            scalars=1,
            scratch=[pltpu.VMEM((2 * routes, 4 * size), bf16)],
        )
        return out

    operands = (
        outer_first, middle_first, first, held, info, lows, forward, up_rows,
        arrive, panel, base, half, beside, across,
    )
    out = lax.switch(branch[0], [functools.partial(flow, total) for total in totals], operands)
    return out.reshape(steps, rows, 2, hidden)


def on_device(states, base, route_panels, down, up, magnitude):
    count = lax.axis_size("dp")
    me = lax.axis_index("dp")
    group = lax.axis_index("groups")
    steps, rows, width = states.shape
    hidden = base.shape[-1]
    panels, _, rank, _ = down.shape
    routes = 2 * steps * rows
    cap = max(2, (5 * rows + count - 1) // count)
    slots = -(-steps * cap // ROW_TILE) * ROW_TILE
    bf16, f32, i32 = jnp.bfloat16, jnp.float32, jnp.int32

    def turn(x, shift):
        return lax.ppermute(x, "dp", [(i, (i + shift) % count) for i in range(count)])

    if (count, lax.axis_size("expert"), lax.axis_size("pair")) == (4, 2, 2):
        one = states.reshape(steps * rows, width)
        which = 2 * lax.axis_index("expert") + lax.axis_index("pair")
        far = [(4 * d + e, 4 * ((d + e) % count) + e) for d in range(count) for e in range(4)]
        near = lax.ppermute(route_panels, ("dp", "expert", "pair"), far)
        one, near = lax.optimization_barrier((one, near))
        flat = near.transpose(2, 0, 1).reshape(1, routes)
        near = jnp.concatenate([flat // panels, flat % panels], axis=0).astype(bf16)
        near = jnp.pad(near, ((0, ROW_TILE - 2), (0, 0)))
        beside = lax.ppermute(near, "pair", [(0, 1), (1, 0)])
        both = lax.ppermute(jnp.concatenate([near, beside], axis=0), "expert", [(0, 1), (1, 0)])
        seen = [one] + [turn(one, s) for s in range(1, count)]
        return relayed(seen, [near, beside, both], which, magnitude, base, down, up)

    pairs = route_panels.reshape(steps * rows, 2)
    numbers = jnp.concatenate([pairs // panels, pairs % panels], axis=1).astype(bf16)
    sent = jnp.concatenate(
        [states.reshape(steps * rows, width), jnp.pad(numbers, ((0, 0), (0, LANES - 4)))], axis=1
    )
    seen = [sent] + [turn(sent, s) for s in range(1, count)]

    half = lax.dynamic_index_in_dim(magnitude, group, axis=1, keepdims=False)
    mine = jnp.concatenate([half] + [turn(half, s) for s in range(1, count)], axis=0)
    other = lax.ppermute(mine, "groups", [(0, 1), (1, 0)])

    vmem = pl.BlockSpec(memory_space=pltpu.VMEM)
    smem = pl.BlockSpec(memory_space=pltpu.SMEM)
    params = pltpu.CompilerParams(vmem_limit_bytes=VMEM_LIMIT)
    part, info = pl.pallas_call(
        functools.partial(low_kernel, count, steps, rows, cap, slots),
        out_shape=(
            jax.ShapeDtypeStruct((2 * rank, count * routes), f32),
            jax.ShapeDtypeStruct((8, count * routes), f32),
        ),
        in_specs=[smem] + [vmem] * (1 + count),
        out_specs=(vmem, vmem),
        compiler_params=params,
    )(me.reshape(1).astype(i32), down, *seen)

    low = lax.psum(part, ("expert", "pair"))

    tile = min(1024, hidden)
    col_tiles = hidden // tile
    whole = lambda shape: pl.BlockSpec(shape, lambda p, n: (0,) * len(shape))
    deltas = pl.pallas_call(
        functools.partial(delta_kernel, count, slots),
        out_shape=[jax.ShapeDtypeStruct((slots, 2 * hidden), bf16)] * count,
        grid=(2, col_tiles),
        in_specs=[whole(info.shape)]
        + [whole(low.shape)]
        + [pl.BlockSpec((panels, None, rank, tile), lambda p, n: (0, p, 0, n))],
        out_specs=[pl.BlockSpec((slots, tile), lambda p, n: (0, p * col_tiles + n))] * count,
        scratch_shapes=[pltpu.VMEM((2, count * slots, panels * rank), bf16)],
        compiler_params=params,
    )(info, low, up)
    got = [deltas[0]] + [turn(deltas[s], count - s) for s in range(1, count)]

    ordered = route_panels.transpose(2, 0, 1).reshape(2, steps, rows)
    owner, within = ordered // panels, ordered % panels
    by_step = owner.transpose(1, 0, 2).reshape(steps, 2 * rows)
    earlier = jnp.tril(jnp.ones((2 * rows, 2 * rows), jnp.bool_), -1)
    rank_of = jnp.sum((by_step[:, :, None] == by_step[:, None, :]) & earlier[None], axis=2, dtype=i32)
    slot = rank_of + jnp.arange(steps, dtype=i32)[:, None] * cap
    slot = slot.reshape(steps, 2, rows).transpose(1, 0, 2).reshape(routes)
    owner, within = owner.reshape(routes), within.reshape(routes)
    ahead = (owner - me) % count
    behind = (me - owner) % count
    pick = (jnp.arange(count * slots, dtype=i32)[None, :] == (ahead * slots + slot)[:, None]).astype(bf16)
    panel = (jnp.arange(count * panels, dtype=i32)[None, :] == (behind * panels + within)[:, None]).astype(bf16)
    base_rows = base.transpose(3, 2, 0, 1, 4).reshape(2, routes, hidden)

    tile = min(512, hidden)
    col_tiles = hidden // tile
    whole = lambda shape: pl.BlockSpec(shape, lambda n: (0,) * len(shape))
    col = lambda depth, p: pl.BlockSpec((depth, tile), lambda n, p=p: (0, p * col_tiles + n))
    out = pl.pallas_call(
        functools.partial(gate_kernel, count),
        out_shape=jax.ShapeDtypeStruct((routes, hidden), bf16),
        grid=(col_tiles,),
        in_specs=[smem, whole(pick.shape), whole(panel.shape)]
        + [pl.BlockSpec((2, routes, tile), lambda n: (0, 0, n))]
        + [col(count * panels, 0)] * 2
        + [col(slots, 0)] * count
        + [col(slots, 1)] * count,
        out_specs=col(routes, 0),
        compiler_params=params,
    )(group.reshape(1).astype(i32), pick, panel, base_rows, mine, other, *got, *got)
    return out.reshape(2, steps, rows, hidden).transpose(1, 2, 0, 3)


def solution(mesh):
    return jax.shard_map(
        on_device,
        mesh=mesh,
        in_specs=(
            P(None, ("groups", "dp"), ("expert", "pair")),
            P(None, ("groups", "dp"), None, None, ("expert", "pair")),
            P(None, ("groups", "dp"), None),
            P("dp", None, None, ("expert", "pair")),
            P("dp", None, None, ("expert", "pair")),
            P("dp", None, ("expert", "pair")),
        ),
        out_specs=P(None, ("groups", "dp"), None, ("expert", "pair")),
        check_vma=False,
    )
```
